32 devices in a mesh: dp: 4 (over y, core), seq: 8 (over z, x).
Axes of the slice: x: 2, y: 2, z: 4, core: 2. Of those that a mesh axis runs over, the one named last changes fastest.
Arguments:
- byte_rows: bfloat16 [8, 2048, 768], P('dp', 'seq'), may hold values from -6 to 6
- segments: int32 [8, 2048], P('dp', 'seq'), may hold values from 0 to 2048, as said below
- counts: int32 [8], P('dp'), may hold values from 1024 to 2048
- buckets: int32 [2047], replicated, may hold values from 0 to 31
- cotangent: bfloat16 [8, 1024, 768], P('dp', 'seq'), may hold values from -6 to 6
- vectors: float32 [7, 768], replicated, as said below
- vector_momenta: float32 [7, 768], replicated, may hold values from -160 to 160
- bias_table: float32 [32, 12], replicated, may hold values from -4 to 4
- table_momenta: float32 [32, 12], replicated, may hold values from -56 to 56
- attention_weights: float32 [4, 768, 768], P(None, ('dp', 'seq')), as said below
- attention_left: float32 [4, 768, 768], P(None, ('dp', 'seq')), as said below
- attention_right: float32 [4, 768, 768], P(None, ('dp', 'seq')), as said below
- attention_left_root: float32 [4, 768, 768], P(None, ('dp', 'seq')), as said below
- attention_right_root: float32 [4, 768, 768], P(None, ('dp', 'seq')), as said below
- attention_momenta: float32 [4, 768, 768], P(None, ('dp', 'seq')), may hold values from -160 to 160
- expand_weights: float32 [2, 768, 2048], P(None, ('dp', 'seq')), may hold values from -0.21875 to 0.21875
- expand_left: float32 [2, 768, 768], P(None, ('dp', 'seq')), as said below
- expand_right: float32 [2, 2048, 2048], P(None, ('dp', 'seq')), as said below
- expand_left_root: float32 [2, 768, 768], P(None, ('dp', 'seq')), as said below
- expand_right_root: float32 [2, 2048, 2048], P(None, ('dp', 'seq')), as said below
- expand_momenta: float32 [2, 768, 2048], P(None, ('dp', 'seq')), may hold values from -160 to 160
- shrink_weights: float32 [2048, 768], P(('dp', 'seq')), may hold values from -0.125 to 0.125
- down_left_statistics: float32 [2048, 2048], P(('dp', 'seq')), as said below
- shrink_right: float32 [768, 768], P(('dp', 'seq')), as said below
- shrink_left_root: float32 [2048, 2048], P(('dp', 'seq')), as said below
- shrink_right_root: float32 [768, 768], P(('dp', 'seq')), as said below
- shrink_momenta: float32 [2048, 768], P(('dp', 'seq')), may hold values from -160 to 160
Outputs:
- layer_output: bfloat16 [8, 1024, 768], P('dp', 'seq')
- input_grads: float32 [8, 2048, 768], P('dp', 'seq')
- vectors_new: float32 [7, 768], replicated
- vector_momenta_new: float32 [7, 768], replicated
- table_new: float32 [32, 12], replicated
- table_momenta_new: float32 [32, 12], replicated
- attention_new: float32 [4, 768, 768], P(None, ('dp', 'seq'))
- attention_left_new: float32 [4, 768, 768], P(None, ('dp', 'seq'))
- attention_right_new: float32 [4, 768, 768], P(None, ('dp', 'seq'))
- attention_momenta_new: float32 [4, 768, 768], P(None, ('dp', 'seq'))
- attention_copy: bfloat16 [4, 768, 768], P(None, ('dp', 'seq'))
- expand_new: float32 [2, 768, 2048], P(None, ('dp', 'seq'))
- expand_left_new: float32 [2, 768, 768], P(None, ('dp', 'seq'))
- expand_right_new: float32 [2, 2048, 2048], P(None, ('dp', 'seq'))
- expand_momenta_new: float32 [2, 768, 2048], P(None, ('dp', 'seq'))
- expand_copy: bfloat16 [2, 768, 2048], P(None, ('dp', 'seq'))
- shrink_new: float32 [2048, 768], P(('dp', 'seq'))
- shrink_left_new: float32 [2048, 2048], P(('dp', 'seq'))
- shrink_right_new: float32 [768, 768], P(('dp', 'seq'))
- shrink_momenta_new: float32 [2048, 768], P(('dp', 'seq'))
- shrink_copy: bfloat16 [2048, 768], P(('dp', 'seq'))
The draws below stay inside these ranges and needn't reach their ends.
Inputs may be any that keep to these rules, and one draw needn't show every extreme that they name: `segments`: along a row the item number never falls within its first counts bytes; bytes at or past the row's count carry 2048; in each aligned group of 2 rows one row is a single item 0 with count 2048. `vectors`: rows 0 to 3 are the causal convolution's taps, row 4 the block-score vector, rows 5 and 6 the gains of the two norms. `attention_weights`: slices 0 to 3 are the query, key, value and output projections. `attention_left`: each slice symmetric. `attention_right`: each slice symmetric. `attention_left_root`: each slice symmetric. `attention_right_root`: each slice symmetric. `expand_left`: each slice symmetric. `expand_right`: each slice symmetric. `expand_left_root`: each slice symmetric. `expand_right_root`: each slice symmetric. `down_left_statistics`: symmetric. `shrink_right`: symmetric. `shrink_left_root`: symmetric. `shrink_right_root`: symmetric.
All inputs are finite; a program needn't handle non-finite values.
Results may differ from the reference program's by a relative error of at most 0.019.
Values may be sent and summed in bfloat16 or wider, within the bound.
No kernel may reach another device: no remote copies, remote signals or barrier semaphores. Data moves between devices by JAX's collectives and lax.ppermute only.
A program may use at most 192 MiB of HBM per device.

```python
import math
import jax
import jax.numpy as jnp
from jax import lax

D = 768
H = 12
DH = 64
FF = 2048
NB = 32
MICRO = 2
ITEM = 512
LB = 2048
LT = 1024
ROWS = 8


def packing(key):
    key_one, key_two, key_three, key_four = jax.random.split(key, 4)
    groups = ROWS // MICRO
    full_pick = jax.random.randint(key_one, (groups,), 0, MICRO)
    full_rows = jnp.arange(groups, dtype=jnp.int32) * MICRO + full_pick
    half_row = (full_pick[0] + jax.random.randint(key_four, (), 1, MICRO)) % MICRO
    row_ids = jnp.arange(ROWS, dtype=jnp.int32)
    is_full = jnp.any(row_ids[:, None] == full_rows[None, :], axis=1)
    row_counts = jax.random.randint(key_two, (ROWS,), LB // 2, LB + 1)
    row_counts = jnp.where(is_full, LB, jnp.where(row_ids == half_row, LB // 2, row_counts))
    positions = jnp.arange(LB, dtype=jnp.int32)
    starts = (jax.random.randint(key_three, (ROWS, LB), 0, ITEM) == 0).astype(jnp.int32)
    starts = jnp.where(is_full[:, None] | (positions[None, :] == 0), 0, starts)
    numbers = jnp.cumsum(starts, axis=1)
    numbers = jnp.where(positions[None, :] < row_counts[:, None], numbers, LB)
    return (numbers.astype(jnp.int32), row_counts.astype(jnp.int32))


def stat_base(sum_width):
    return 0.05 * sum_width * 0.1 * ROWS * LT


def attention_stat_base(sum_width):
    return 0.05 * sum_width * 8.0 * ROWS * LT


def positive_block(key, lead_shape, order, base_scale):
    key_one, key_two = jax.random.split(key)
    diagonal = base_scale * jnp.exp(jax.random.uniform(key_one, lead_shape + (order,), jnp.float32, 0.0, math.log(4.0)))
    symmetric_part = jax.random.normal(key_two, lead_shape + (order, order), jnp.float32)
    symmetric_part = (symmetric_part + jnp.swapaxes(symmetric_part, -1, -2)) * (0.3 * base_scale / math.sqrt(2.0 * order))
    return symmetric_part + jnp.eye(order, dtype=jnp.float32) * diagonal[..., None, :]


def draw_segments(key, part):
    return packing(key)[0]


def draw_counts(key, part):
    return packing(key)[1]


def draw_vectors(key, part):
    key = jax.random.fold_in(key, 5)
    key_one, key_two, key_three = jax.random.split(key, 3)
    taps = 0.5 * jax.random.normal(key_one, (4, D), jnp.float32)
    score_row = 2.0 * jax.random.normal(key_two, (1, D), jnp.float32) / math.sqrt(D)
    gain_rows = 1.0 + 0.5 * jax.random.uniform(key_three, (2, D), jnp.float32, -1.0, 1.0)
    return jnp.concatenate([taps, score_row, gain_rows], axis=0)


def draw_attention_weights(key, part):
    key = jax.random.fold_in(key, 7)
    scales = jnp.array([1.0 / math.sqrt(D * DH), 1.0 / math.sqrt(D), 1.0 / math.sqrt(D), 4.0 / math.sqrt(D)], jnp.float32)
    return jax.random.normal(key, (4, D, D), jnp.float32) * scales[:, None, None]


def draw_attention_left(key, part):
    key = jax.random.fold_in(key, 11)
    return positive_block(key, (4,), D, attention_stat_base(D))


def draw_attention_right(key, part):
    key = jax.random.fold_in(key, 12)
    return positive_block(key, (4,), D, attention_stat_base(D))


def draw_attention_left_root(key, part):
    key = jax.random.fold_in(key, 13)
    return positive_block(key, (4,), D, stat_base(D) ** (-0.25))


def draw_attention_right_root(key, part):
    key = jax.random.fold_in(key, 14)
    return positive_block(key, (4,), D, stat_base(D) ** (-0.25))


def draw_expand_left(key, part):
    key = jax.random.fold_in(key, 21)
    return positive_block(key, (2,), D, stat_base(FF))


def draw_expand_right(key, part):
    key = jax.random.fold_in(key, 22)
    return positive_block(key, (2,), FF, stat_base(D))


def draw_expand_left_root(key, part):
    key = jax.random.fold_in(key, 23)
    return positive_block(key, (2,), D, stat_base(FF) ** (-0.25))


def draw_expand_right_root(key, part):
    key = jax.random.fold_in(key, 24)
    return positive_block(key, (2,), FF, stat_base(D) ** (-0.25))


def draw_down_left_statistics(key, part):
    key = jax.random.fold_in(key, 31)
    return positive_block(key, (), FF, stat_base(D))


def draw_shrink_right(key, part):
    key = jax.random.fold_in(key, 32)
    return positive_block(key, (), D, stat_base(FF))


def draw_shrink_left_root(key, part):
    key = jax.random.fold_in(key, 33)
    return positive_block(key, (), FF, stat_base(D) ** (-0.25))


def draw_shrink_right_root(key, part):
    key = jax.random.fold_in(key, 34)
    return positive_block(key, (), D, stat_base(FF) ** (-0.25))


def touch_ends(entries, stream_key, smallest, largest):
    place = [jax.random.randint(jax.random.fold_in(stream_key, axis), (), 0, length) for axis, length in enumerate(entries.shape)]
    main_axis = entries.shape.index(max(entries.shape))
    beside = place[:main_axis] + [(place[main_axis] + 1) % entries.shape[main_axis]] + place[main_axis + 1:]
    return entries.at[tuple(place)].set(smallest).at[tuple(beside)].set(largest)


def shard_levels(rng, extent, pieces, low, top_value):
    factor_of = 1.0
    for dim, blocks in pieces:
        steps = jax.random.uniform(jax.random.fold_in(jax.random.fold_in(rng, 6), dim), (blocks,), jnp.float32, low / len(pieces), top_value / len(pieces))
        factor_of = factor_of * jnp.repeat(jnp.exp(steps), extent[dim] // blocks).reshape((-1,) + (1,) * (len(extent) - 1 - dim))
    return factor_of


def noise(stream_key, extent, width, most, cuts=(), held_as=jnp.bfloat16):
    loudness = shard_levels(stream_key, extent, cuts, -0.22, 0.18) if cuts else 1.0
    entries = jax.random.normal(stream_key, extent, jnp.float32) * width * loudness
    return jnp.minimum(jnp.maximum(entries, -most), most).astype(held_as)


def setup_inputs(seed: int = 0) -> dict:
    streams_of = jax.random.split(jax.random.key(seed), 28)
    byte_rows = noise(streams_of[0], (ROWS, LB, D), 1.0, 6.0, ((0, 4), (1, 8)))
    segments = draw_segments(jax.random.fold_in(streams_of[27], 71), 0)
    counts = draw_counts(jax.random.fold_in(streams_of[27], 71), 0)
    buckets = touch_ends(jax.random.randint(streams_of[3], (2 * LT - 1,), 0, NB), jax.random.fold_in(streams_of[3], 1), 0, NB - 1).astype(jnp.int32)
    cotangent = noise(streams_of[4], (ROWS, LT, D), 1.0, 6.0, ((0, 4), (1, 8)))
    vectors = draw_vectors(jax.random.fold_in(streams_of[27], 71), 0)
    vector_momenta = noise(streams_of[6], (7, D), (0.3 * (ROWS * LT) ** 0.5), 160.0, (), jnp.float32)
    bias_table = noise(streams_of[7], (NB, H), 1.0, 4.0, (), jnp.float32)
    table_momenta = noise(streams_of[8], (NB, H), (0.1 * (ROWS * LT) ** 0.5), 56.0, (), jnp.float32)
    attention_weights = draw_attention_weights(jax.random.fold_in(streams_of[27], 71), 0)
    attention_left = draw_attention_left(jax.random.fold_in(streams_of[27], 71), 0)
    attention_right = draw_attention_right(jax.random.fold_in(streams_of[27], 71), 0)
    attention_left_root = draw_attention_left_root(jax.random.fold_in(streams_of[27], 71), 0)
    attention_right_root = draw_attention_right_root(jax.random.fold_in(streams_of[27], 71), 0)
    attention_momenta = noise(streams_of[14], (4, D, D), ((0.1 * ROWS * LT) ** 0.5), 160.0, ((1, 32),), jnp.float32)
    expand_weights = noise(streams_of[15], (2, D, FF), D ** -0.5, 0.21875, ((1, 32),), jnp.float32)
    expand_left = draw_expand_left(jax.random.fold_in(streams_of[27], 71), 0)
    expand_right = draw_expand_right(jax.random.fold_in(streams_of[27], 71), 0)
    expand_left_root = draw_expand_left_root(jax.random.fold_in(streams_of[27], 71), 0)
    expand_right_root = draw_expand_right_root(jax.random.fold_in(streams_of[27], 71), 0)
    expand_momenta = noise(streams_of[20], (2, D, FF), ((0.1 * ROWS * LT) ** 0.5), 160.0, ((1, 32),), jnp.float32)
    shrink_weights = noise(streams_of[21], (FF, D), FF ** -0.5, 0.125, ((0, 32),), jnp.float32)
    down_left_statistics = draw_down_left_statistics(jax.random.fold_in(streams_of[27], 71), 0)
    shrink_right = draw_shrink_right(jax.random.fold_in(streams_of[27], 71), 0)
    shrink_left_root = draw_shrink_left_root(jax.random.fold_in(streams_of[27], 71), 0)
    shrink_right_root = draw_shrink_right_root(jax.random.fold_in(streams_of[27], 71), 0)
    shrink_momenta = noise(streams_of[26], (FF, D), ((0.1 * ROWS * LT) ** 0.5), 160.0, ((0, 32),), jnp.float32)
    return {"byte_rows": byte_rows, "segments": segments, "counts": counts, "buckets": buckets, "cotangent": cotangent, "vectors": vectors, "vector_momenta": vector_momenta, "bias_table": bias_table, "table_momenta": table_momenta, "attention_weights": attention_weights, "attention_left": attention_left, "attention_right": attention_right, "attention_left_root": attention_left_root, "attention_right_root": attention_right_root, "attention_momenta": attention_momenta, "expand_weights": expand_weights, "expand_left": expand_left, "expand_right": expand_right, "expand_left_root": expand_left_root, "expand_right_root": expand_right_root, "expand_momenta": expand_momenta, "shrink_weights": shrink_weights, "down_left_statistics": down_left_statistics, "shrink_right": shrink_right, "shrink_left_root": shrink_left_root, "shrink_right_root": shrink_right_root, "shrink_momenta": shrink_momenta}


EPSILON = 1e-06
STAT_DECAY = 0.95
MOMENTUM = 0.9
MATRIX_RATE = 0.1
SMALL_RATE = 0.1
MASKED = -1e+30
HIGH_PRECISION = lax.Precision.HIGHEST

@jax.custom_vjp
def low(v):
    return lax.optimization_barrier(v.astype(jnp.bfloat16)).astype(jnp.float32)

@jax.custom_vjp
def low_back(v):
    return v

def low_keep(v):
    return (low(v), None)

def low_pass(kept, grad):
    return (grad,)

def back_keep(v):
    return (v, None)

def back_low(kept, grad):
    return (low(grad),)
low.defvjp(low_keep, low_pass)
low_back.defvjp(back_keep, back_low)

def rms_scale(values, gain_row):
    factor = lax.rsqrt(lax.optimization_barrier(jnp.mean(values * values, axis=-1, keepdims=True)) + EPSILON)
    return values * factor * gain_row

def block_pool(beside_all, positions, block_size, row_total):
    length = positions.shape[0]
    summed = jnp.zeros(beside_all.shape[:-2] + (length, beside_all.shape[-1]), jnp.float32)
    counted = jnp.zeros((length,), jnp.float32)
    for offset in range(1 - block_size, block_size):
        nearby = positions + offset
        inside = (nearby // block_size == positions // block_size) & (nearby >= 0) & (nearby < row_total)
        weight = inside.astype(jnp.float32)
        summed = summed + weight[:, None] * beside_all[..., 3 + offset:3 + offset + length, :]
        counted = counted + weight
    return (summed, counted)

def matmul(left_side, right_side):
    return jnp.dot(left_side, right_side, precision=HIGH_PRECISION, preferred_element_type=jnp.float32)

def forward_row(params, byte_row, segment_row, row_count, buckets):
    attention_weights, expand_weights, shrink_weights, vectors, bias_table = params
    attention_low = low(attention_weights)
    expand_low = low(expand_weights)
    shrink_low = low(shrink_weights)
    positions = jnp.arange(LB, dtype=jnp.int32)
    is_valid = (positions < row_count).astype(jnp.float32)
    embedded = byte_row * is_valid[:, None]
    padded = jnp.pad(embedded, ((3, 0), (0, 0)))
    conv_out = sum((vectors[tap_index] * padded[tap_index:tap_index + LB] for tap_index in range(4)))
    beside_all = jnp.pad(conv_out, ((3, 3), (0, 0)))
    pooled = []
    for block_size in range(1, 5):
        summed, counted = block_pool(beside_all, positions, block_size, LB)
        pooled.append(summed / counted[:, None])
    size_scores = jnp.stack([lax.optimization_barrier(jnp.sum(pooled_item * vectors[4], axis=-1)) for pooled_item in pooled])
    size_weights = jax.nn.softmax(size_scores, axis=0)
    blended = sum((size_weights[size_index][:, None] * pooled[size_index] for size_index in range(4)))
    tokens = blended.reshape(LT, 2, D).mean(axis=1)
    normed = low(rms_scale(tokens, vectors[5]))
    queries = low_back(low(matmul(normed, attention_low[0])))
    keys_all = low_back(low(matmul(normed, attention_low[1])))
    values_all = low_back(low(matmul(normed, attention_low[2])))
    onehot = (buckets[:, None] == jnp.arange(NB, dtype=jnp.int32)[None, :]).astype(jnp.float32)
    bias_rel = matmul(onehot, bias_table)
    token_segs = segment_row[0::2]
    query_heads = queries.reshape(LT, H, DH)
    key_heads = keys_all.reshape(LT, H, DH)
    value_heads = values_all.reshape(LT, H, DH)
    block_span = min(512, LT)

    def query_block(block_start):
        query_part = lax.dynamic_slice_in_dim(query_heads, block_start, block_span, 0)
        raw_scores = jnp.einsum('ihd,jhd->hij', query_part, key_heads, precision=HIGH_PRECISION)
        query_pos = block_start + jnp.arange(block_span, dtype=jnp.int32)
        relative = jnp.arange(LT, dtype=jnp.int32)[None, :] - query_pos[:, None] + LT - 1
        bias_block = jnp.transpose(jnp.take(bias_rel, relative, axis=0), (2, 0, 1))
        query_seg = lax.dynamic_slice_in_dim(token_segs, block_start, block_span, 0)
        same_segment = query_seg[:, None] == token_segs[None, :]
        scores = low_back(jnp.where(same_segment[None], raw_scores + bias_block, MASKED))
        prob_block = low(jax.nn.softmax(scores, axis=-1))
        return jnp.einsum('hij,jhd->ihd', prob_block, value_heads, precision=HIGH_PRECISION)
    starts = jnp.arange(LT // block_span, dtype=jnp.int32) * block_span
    attended_blocks = lax.map(jax.checkpoint(query_block), starts)
    attended = low_back(low(attended_blocks.reshape(LT, D)))
    resid = tokens + low_back(matmul(attended, attention_low[3]))
    normed_two = low(rms_scale(resid, vectors[6]))
    gate_pre = low_back(matmul(normed_two, expand_low[0]))
    upward = low_back(matmul(normed_two, expand_low[1]))
    hidden = low(jax.nn.gelu(gate_pre, approximate=True) * upward)
    return resid + low_back(matmul(hidden, shrink_low))

def shampoo(weight, grad, left, right, left_root, right_inverse_root, momenta):
    new_left = STAT_DECAY * left + (1.0 - STAT_DECAY) * jnp.einsum('gmn,gkn->gmk', grad, grad, precision=HIGH_PRECISION)
    new_right = STAT_DECAY * right + (1.0 - STAT_DECAY) * jnp.einsum('gmn,gmk->gnk', grad, grad, precision=HIGH_PRECISION)
    new_momenta = MOMENTUM * momenta + grad
    product = jnp.einsum('gmn,gnk->gmk', new_momenta, right_inverse_root, precision=HIGH_PRECISION)
    new_weight = weight - MATRIX_RATE * jnp.einsum('gmk,gkn->gmn', left_root, product, precision=HIGH_PRECISION)
    return (new_weight, new_left, new_right, new_momenta, new_weight.astype(jnp.bfloat16))

def reference(byte_rows, segments, counts, buckets, cotangent, vectors, vector_momenta, bias_table, table_momenta, attention_weights, attention_left, attention_right, attention_left_root, attention_right_root, attention_momenta, expand_weights, expand_left, expand_right, expand_left_root, expand_right_root, expand_momenta, shrink_weights, down_left_statistics, shrink_right, shrink_left_root, shrink_right_root, shrink_momenta):
    params = (attention_weights, expand_weights, shrink_weights, vectors, bias_table)
    start_grads = jax.tree.map(jnp.zeros_like, params)

    def row_step(running_grads, row_data):
        byte_row, segment_row, row_count, cot_row = row_data

        def forward(weights, inputs):
            return forward_row(weights, inputs, segment_row, row_count, buckets)
        output, pullback = jax.vjp(forward, params, byte_row.astype(jnp.float32))
        weight_grads, input_grad = pullback(cot_row.astype(jnp.float32))
        running_grads = jax.tree.map(jnp.add, running_grads, weight_grads)
        return (running_grads, (output.astype(jnp.bfloat16), input_grad))
    grads, outputs = lax.scan(row_step, start_grads, (byte_rows, segments, counts, cotangent))
    layer_output, input_grads = outputs
    grad_attention, grad_expand, grad_shrink, grad_vectors, grad_table = grads
    small_rate = SMALL_RATE / math.sqrt(ROWS * LT)
    vector_momenta_new = MOMENTUM * vector_momenta + grad_vectors
    vectors_new = vectors - small_rate * vector_momenta_new
    table_momenta_new = MOMENTUM * table_momenta + grad_table
    table_new = bias_table - small_rate * table_momenta_new
    attention_parts = shampoo(attention_weights, grad_attention, attention_left, attention_right, attention_left_root, attention_right_root, attention_momenta)
    expand_parts = shampoo(expand_weights, grad_expand, expand_left, expand_right, expand_left_root, expand_right_root, expand_momenta)
    shrink_parts = shampoo(shrink_weights[None], grad_shrink[None], down_left_statistics[None], shrink_right[None], shrink_left_root[None], shrink_right_root[None], shrink_momenta[None])
    return (layer_output, input_grads, vectors_new, vector_momenta_new, table_new, table_momenta_new, attention_parts[0], attention_parts[1], attention_parts[2], attention_parts[3], attention_parts[4], expand_parts[0], expand_parts[1], expand_parts[2], expand_parts[3], expand_parts[4], shrink_parts[0][0], shrink_parts[1][0], shrink_parts[2][0], shrink_parts[3][0], shrink_parts[4][0])
```

```python
import functools
import math

import jax
import jax.numpy as jnp
from jax import lax
from jax.experimental import pallas as pl
from jax.experimental.pallas import tpu as pltpu
from jax.sharding import PartitionSpec as P

EPSILON = 1e-06
STAT_DECAY = 0.95
MOMENTUM = 0.9
MATRIX_RATE = 0.1
SMALL_RATE = 0.1
MASKED = -1e30
HIGH_PRECISION = lax.Precision.HIGHEST
BOTH = ("dp", "seq")


def fill_bias(brel_ref, bias_sc, heads, tile):
    span = brel_ref.shape[1]
    rows = lax.broadcasted_iota(jnp.int32, (8, span), 0)
    for h in range(heads):
        wide = jnp.broadcast_to(brel_ref[h:h + 1, :], (8, span))
        first = wide
        for i in range(8):
            first = jnp.where(rows == i, pltpu.roll(wide, span - (tile - 1) + i, 1), first)
        bias_sc[h, 0:8, :] = first
        size = 8
        while size < tile:
            bias_sc[h, size:2 * size, :] = pltpu.roll(bias_sc[h, 0:size, :], size, 1)
            size *= 2

def attn_fwd_kernel(heads, tile, qkv_ref, brel_ref, segc_ref, segr_ref, out_ref, outf_ref, lse_ref, bias_sc):
    step = pl.program_id(0)
    length = qkv_ref.shape[0]
    width = qkv_ref.shape[1] // 3
    dh = width // heads

    @pl.when(step == 0)
    def _():
        fill_bias(brel_ref, bias_sc, heads, tile)

    begin = pl.multiple_of(step * tile, tile)
    offset = pl.multiple_of(length - tile - begin, 128)
    same = segc_ref[...] == segr_ref[...]
    lanes = lax.broadcasted_iota(jnp.int32, (tile, 128), 1)
    lse_all = jnp.zeros((tile, 128), jnp.float32)
    outs = []
    for h in range(heads):
        q = qkv_ref[pl.ds(begin, tile), h * dh:(h + 1) * dh]
        k = qkv_ref[:, width + h * dh:width + (h + 1) * dh]
        v = qkv_ref[:, 2 * width + h * dh:2 * width + (h + 1) * dh]
        scores = lax.dot_general(q, k, (((1,), (1,)), ((), ())), preferred_element_type=jnp.float32)
        scores = jnp.where(same, scores + bias_sc[h, :, pl.ds(offset, length)], MASKED)
        top = jnp.max(scores, axis=1, keepdims=True)
        probs = jnp.exp(scores - top)
        total = jnp.sum(probs, axis=1, keepdims=True)
        out = lax.dot_general(probs.astype(jnp.bfloat16), v, (((1,), (0,)), ((), ())), preferred_element_type=jnp.float32)
        outs.append(out / total)
        lse_all = jnp.where(lanes == h, top + jnp.log(total), lse_all)
    joined = jnp.concatenate(outs, axis=1)
    out_ref[...] = joined.astype(jnp.bfloat16)
    outf_ref[...] = joined
    lse_ref[...] = lse_all

def attn_fwd(qkv, brel, segc, segr, heads, tile=128):
    length = qkv.shape[0]; width = qkv.shape[1] // 3
    full = lambda s: pl.BlockSpec(s, lambda i: (0,) * len(s))
    rowb = lambda w: pl.BlockSpec((tile, w), lambda i: (i, 0))
    return pl.pallas_call(
        functools.partial(attn_fwd_kernel, heads, tile),
        grid=(length // tile,),
        in_specs=[full(qkv.shape), full(brel.shape), rowb(1), full(segr.shape)],
        out_specs=[rowb(width), rowb(width), rowb(128)],
        out_shape=[jax.ShapeDtypeStruct((length, width), jnp.bfloat16), jax.ShapeDtypeStruct((length, width), jnp.float32), jax.ShapeDtypeStruct((length, 128), jnp.float32)],
        scratch_shapes=[pltpu.VMEM((heads, tile, 2 * length), jnp.float32)],
        compiler_params=pltpu.CompilerParams(vmem_limit_bytes=48 * 2**20),
        cost_estimate=pl.CostEstimate(flops=4 * length * length * width, bytes_accessed=6 * length * width * 2, transcendentals=heads * length * length),
    )(qkv, brel, segc, segr)

def attn_bwd_kernel(heads, tile, trans, qkv_ref, grad_ref, outf_ref, lse_ref, brel_ref, segc_ref, segr_ref, dqkv_ref, gb_ref, bias_sc, gb_sc, dk_sc, dv_sc):
    step = pl.program_id(0)
    length = qkv_ref.shape[0]
    width = qkv_ref.shape[1] // 3
    dh = width // heads

    @pl.when(step == 0)
    def _():
        fill_bias(brel_ref, bias_sc, heads, tile)
        gb_sc[...] = jnp.zeros_like(gb_sc)
        dk_sc[...] = jnp.zeros_like(dk_sc)
        dv_sc[...] = jnp.zeros_like(dv_sc)

    begin = pl.multiple_of(step * tile, tile)
    offset = pl.multiple_of(length - tile - begin, 128)
    same = segc_ref[...] == segr_ref[...]
    dqs = []
    for h in range(heads):
        q = qkv_ref[pl.ds(begin, tile), h * dh:(h + 1) * dh]
        k = qkv_ref[:, width + h * dh:width + (h + 1) * dh]
        v = qkv_ref[:, 2 * width + h * dh:2 * width + (h + 1) * dh]
        g = grad_ref[:, h * dh:(h + 1) * dh]
        delta = jnp.sum(g.astype(jnp.float32) * outf_ref[:, h * dh:(h + 1) * dh], axis=1, keepdims=True)
        lse = lse_ref[:, h:h + 1]
        scores = lax.dot_general(q, k, (((1,), (1,)), ((), ())), preferred_element_type=jnp.float32)
        scores = jnp.where(same, scores + bias_sc[h, :, pl.ds(offset, length)], MASKED)
        probs = jnp.exp(scores - lse)
        gp = lax.dot_general(g, v, (((1,), (1,)), ((), ())), preferred_element_type=jnp.float32)
        gs = (probs * (gp - delta))
        gsb = gs.astype(jnp.bfloat16)
        pb = probs.astype(jnp.bfloat16)
        gb_sc[h, :, pl.ds(offset, length)] += gsb.astype(jnp.float32)
        dqs.append(lax.dot_general(gsb, k, (((1,), (0,)), ((), ())), preferred_element_type=jnp.float32))
        if trans:
            dk_sc[h] += lax.dot_general(q, gsb, (((0,), (0,)), ((), ())), preferred_element_type=jnp.float32)
            dv_sc[h] += lax.dot_general(g, pb, (((0,), (0,)), ((), ())), preferred_element_type=jnp.float32)
        else:
            dk_sc[h] += lax.dot_general(gsb, q, (((0,), (0,)), ((), ())), preferred_element_type=jnp.float32)
            dv_sc[h] += lax.dot_general(pb, g, (((0,), (0,)), ((), ())), preferred_element_type=jnp.float32)
    dqkv_ref[pl.ds(begin, tile), 0:width] = jnp.concatenate(dqs, axis=1).astype(jnp.bfloat16)

    @pl.when(step == pl.num_programs(0) - 1)
    def _():
        turn = (lambda x: x.T) if trans else (lambda x: x)
        dqkv_ref[:, width:3 * width] = jnp.concatenate(
            [turn(dk_sc[h]) for h in range(heads)] + [turn(dv_sc[h]) for h in range(heads)], axis=1).astype(jnp.bfloat16)
        span = gb_sc.shape[2]
        rows = lax.broadcasted_iota(jnp.int32, (8, span), 0)
        for h in range(heads):
            size = tile // 2
            part = gb_sc[h]
            while size >= 8:
                part = part[:size] + pltpu.roll(part[size:], span - size, 1)
                size //= 2
            line = jnp.zeros((1, span), jnp.float32)
            for i in range(8):
                line = line + jnp.sum(jnp.where(rows == i, pltpu.roll(part, (tile - 1 - i) % span, 1), 0.0), axis=0, keepdims=True)
            gb_ref[h:h + 1, :] = line

def attn_bwd(qkv, grad, outf, lse, brel, segc, segr, heads, tile=128, trans=True):
    length = qkv.shape[0]; width = qkv.shape[1] // 3; dh = width // heads
    full = lambda s: pl.BlockSpec(s, lambda i: (0,) * len(s))
    rowb = lambda w: pl.BlockSpec((tile, w), lambda i: (i, 0))
    acc = (heads, dh, length) if trans else (heads, length, dh)
    return pl.pallas_call(
        functools.partial(attn_bwd_kernel, heads, tile, trans),
        grid=(length // tile,),
        in_specs=[full(qkv.shape), rowb(width), rowb(width), rowb(128), full(brel.shape), rowb(1), full(segr.shape)],
        out_specs=[full(qkv.shape), full(brel.shape)],
        out_shape=[jax.ShapeDtypeStruct(qkv.shape, jnp.bfloat16), jax.ShapeDtypeStruct(brel.shape, jnp.float32)],
        scratch_shapes=[pltpu.VMEM((heads, tile, 2 * length), jnp.float32), pltpu.VMEM((heads, tile, 2 * length), jnp.float32), pltpu.VMEM(acc, jnp.float32), pltpu.VMEM(acc, jnp.float32)],
        compiler_params=pltpu.CompilerParams(vmem_limit_bytes=56 * 2**20),
        cost_estimate=pl.CostEstimate(flops=10 * length * length * width, bytes_accessed=12 * length * width * 2, transcendentals=heads * length * length),
    )(qkv, grad, outf, lse, brel, segc, segr)


def low(values):
    return values.astype(jnp.bfloat16)


def dot(left_side, right_side, left_dim, right_dim):
    return lax.dot_general(
        left_side,
        right_side,
        (((left_dim,), (right_dim,)), ((), ())),
        preferred_element_type=jnp.float32,
    )


def padded_2(block, sides, width):
    for axis, dim in sides:
        count = lax.axis_size(axis)
        forward = [(i, i + 1) for i in range(count - 1)]
        backward = [(target, source) for source, target in forward]
        low_side = lax.ppermute(
            lax.slice_in_dim(block, block.shape[dim] - width, None, axis=dim), axis, forward
        )
        high_side = lax.ppermute(lax.slice_in_dim(block, 0, width, axis=dim), axis, backward)
        block = jnp.concatenate([low_side, block, high_side], axis=dim)
    return block


def rms_factor(values):
    return lax.rsqrt(jnp.mean(values * values, axis=-1, keepdims=True) + EPSILON)


def norm_back(values, factor, gain_row, grad_out):
    scaled = grad_out * gain_row
    grad_gain = jnp.sum(grad_out * values * factor, axis=0)
    inner_mean = jnp.mean(scaled * values, axis=-1, keepdims=True)
    return (factor * (scaled - values * inner_mean * factor * factor), grad_gain)


def block_pool(around, positions, block_size, row_total):
    length = positions.shape[0]
    summed = jnp.zeros(around.shape[:-2] + (length, around.shape[-1]), jnp.float32)
    counted = jnp.zeros((length,), jnp.float32)
    for offset in range(1 - block_size, block_size):
        nearby = positions + offset
        inside = (
            (nearby // block_size == positions // block_size) & (nearby >= 0) & (nearby < row_total)
        )
        weight = inside.astype(jnp.float32)
        summed = summed + weight[:, None] * around[..., 3 + offset : 3 + offset + length, :]
        counted = counted + weight
    return (summed, counted)


class Layout:
    def __init__(self, head_count, micro_rows):
        self.dp_size = lax.axis_size("dp")
        self.seq_size = lax.axis_size("seq")
        self.count = self.dp_size * self.seq_size
        self.dp = lax.axis_index("dp")
        self.seq = lax.axis_index("seq")
        self.micro = micro_rows
        self.parts = math.gcd(self.dp_size, head_count & -head_count)
        self.groups = self.dp_size // self.parts
        self.part = self.dp % self.parts
        self.head_groups = head_count & -head_count
        self.repeat = self.seq_size // (micro_rows * self.head_groups)
        self.unit = self.seq // self.repeat
        self.matrices = 4
        self.sides = self.seq_size // self.matrices
        self.matrix = self.seq // self.sides
        self.side = self.seq % self.sides
        self.members = [
            [
                (group * self.parts + part) * self.seq_size + matrix * self.sides + side
                for part in range(self.parts)
                for side in range(self.sides)
            ]
            for group in range(self.groups)
            for matrix in range(self.matrices)
        ]
        self.holders = [
            [
                dp * self.seq_size + matrix * self.sides + side
                for dp in range(self.dp_size)
                for side in range(self.sides)
            ]
            for matrix in range(self.matrices)
        ]
        self.owners = [
            [matrix * self.sides + side for matrix in range(self.matrices)]
            for side in range(self.sides)
        ]

    def flip(self, block, axis, bits):
        size = lax.axis_size(axis)
        return lax.ppermute(block, axis, [(i, i ^ bits) for i in range(size)])

    def gather_parts(self, block):
        pieces = {0: block}
        bit = self.parts // 2
        while bit:
            for key in list(pieces):
                pieces[key | bit] = self.flip(pieces[key], "dp", bit)
            bit //= 2
        whole = jnp.zeros((self.parts,) + block.shape, block.dtype)
        for key, piece in pieces.items():
            whole = lax.dynamic_update_index_in_dim(whole, piece, self.part ^ key, 0)
        return whole

    def scatter(self, blocks, axis, index):
        bit = 1
        while blocks.shape[0] > 1:
            pairs = blocks.reshape((blocks.shape[0] // 2, 2) + blocks.shape[1:])
            mine = (index // bit) % 2
            kept = lax.dynamic_index_in_dim(pairs, mine, 1, False)
            sent = lax.dynamic_index_in_dim(pairs, 1 - mine, 1, False)
            blocks = kept.astype(jnp.float32) + self.flip(low(sent), axis, bit).astype(jnp.float32)
            bit *= 2
        return blocks[0]

    def scatter_parts(self, blocks):
        return self.scatter(blocks, "dp", self.part)

    def sum_groups(self, block):
        total = block
        for shift in range(1, self.groups):
            turn = [(i, (i + shift * self.parts) % self.dp_size) for i in range(self.dp_size)]
            total = total + lax.ppermute(low(block), "dp", turn).astype(jnp.float32)
        return total

    def sum_all(self, block):
        for axis in BOTH:
            bit = 1
            while bit < lax.axis_size(axis):
                block = block + self.flip(block, axis, bit)
                bit *= 2
        return block

    def to_units(self, blocks):
        shape = blocks.shape
        blocks = blocks[:, :, None]
        if self.repeat > 1:
            blocks = jnp.broadcast_to(blocks, shape[:2] + (self.repeat,) + shape[2:])
        return self.exchange(blocks.reshape((self.seq_size,) + shape[2:]))

    def exchange(self, blocks):
        return lax.all_to_all(blocks, "seq", 0, 0, tiled=True)

    def gather_members(self, block):
        whole = lax.all_gather(block, BOTH, axis=0, axis_index_groups=self.members)
        return whole.reshape((self.parts, self.sides) + block.shape)

    def gather_holders(self, block):
        whole = lax.all_gather(block, BOTH, axis=0, axis_index_groups=self.holders)
        return whole.reshape((self.dp_size, self.sides) + block.shape)

    def exchange_holders(self, blocks):
        return lax.all_to_all(
            blocks, BOTH, 0, 0, tiled=True, axis_index_groups=self.holders
        )

    def exchange_owners(self, blocks):
        return lax.all_to_all(
            blocks, "seq", 0, 0, tiled=True, axis_index_groups=self.owners
        )

    def block_rows(self, whole):
        span = whole.shape[0] // self.count
        view = whole.reshape((self.dp_size, self.matrices, self.sides, span) + whole.shape[1:])
        view = lax.dynamic_index_in_dim(view, self.dp, 0, False)
        return lax.dynamic_index_in_dim(view, self.side, 1, False)


def gather_all(block):
    return lax.all_gather(block, BOTH, axis=0, tiled=True)


def per_device(
    byte_rows,
    segments,
    counts,
    buckets,
    cotangent,
    vectors,
    vector_momenta,
    bias_table,
    table_momenta,
    attention_weights,
    attention_left,
    attention_right,
    attention_left_root,
    attention_right_root,
    attention_momenta,
    expand_weights,
    expand_left,
    expand_right,
    expand_left_root,
    expand_right_root,
    expand_momenta,
    shrink_weights,
    down_left_statistics,
    shrink_right,
    shrink_left_root,
    shrink_right_root,
    shrink_momenta,
):
    micro_rows, width_bytes, model_width = byte_rows.shape
    head_count = bias_table.shape[1]
    at = Layout(head_count, micro_rows)
    parts, part, seq_size, sequence_position = at.parts, at.part, at.seq_size, at.seq
    row_len = width_bytes * seq_size
    tok_local = width_bytes // 2
    tok_row = row_len // 2
    hidden_width = shrink_weights.shape[1 - 1] * at.count
    heads = head_count // parts
    head_width = model_width // parts
    hidden_part = hidden_width // parts

    row_span = model_width // at.count
    hidden_span = hidden_width // at.count
    dp_size, sides, matrices = at.dp_size, at.sides, at.matrices

    split = low(attention_weights[:3]).reshape(3, row_span, at.head_groups, head_width)
    split = jnp.transpose(split, (2, 1, 0, 3)).reshape(at.head_groups, row_span, 3 * head_width)
    split = at.to_units(jnp.broadcast_to(split[None], (micro_rows,) + split.shape))
    split = split.reshape(seq_size * row_span, 3 * head_width)
    if at.groups == 1:
        weights_qkv = at.gather_parts(split)
    else:
        weights_qkv = lax.all_gather(split, "dp", axis=0)
    weights_qkv = weights_qkv.reshape(model_width, 3 * head_width)

    rest = jnp.concatenate(
        [
            low(attention_weights[3]),
            low(expand_weights[0]),
            low(expand_weights[1]),
            low(shrink_weights).reshape(row_span, hidden_width),
        ],
        axis=1,
    )
    rest = gather_all(rest)

    def columns(whole, begin, width):
        return lax.dynamic_slice_in_dim(whole, begin, width, 1)

    weights_out = rest[:, :model_width]
    weights_expand = jnp.concatenate(
        [
            columns(rest, model_width + i * hidden_width + part * hidden_part, hidden_part)
            for i in range(2)
        ],
        axis=1,
    )
    weights_shrink = lax.dynamic_slice(
        rest,
        (part * (model_width // parts), model_width + 2 * hidden_width),
        (model_width // parts, hidden_width),
    ).reshape(hidden_part, model_width)

    grad_rows_out = cotangent.reshape(-1, model_width)
    grad_rows_all = at.gather_parts(grad_rows_out).reshape(-1, model_width)
    token_segs = segments[:, 0::2]
    seg_row = at.to_units(
        jnp.broadcast_to(token_segs[:, None], (micro_rows, at.head_groups, tok_local))
    ).reshape(tok_row)

    blank = jnp.zeros((row_span, hidden_width + model_width), jnp.bfloat16)
    side_width = (3 * model_width + hidden_width) // sides

    def early_block(i):
        if i == 2:
            feed = [low(shrink_momenta).reshape(row_span, hidden_width), low(shrink_right_root)]
        elif i < 2:
            feed = [low(expand_momenta[i]), low(expand_left_root[i])]
        else:
            feed = [blank]
        joined = jnp.concatenate(
            [low(attention_momenta[i]), low(attention_right_root[i])] + feed, axis=1
        )
        return jnp.transpose(joined.reshape(row_span, sides, side_width), (1, 0, 2))

    early = at.exchange(jnp.concatenate([early_block(i) for i in range(matrices)], axis=0))
    early = at.gather_holders(early.reshape(seq_size * row_span, side_width))
    early = early.reshape(dp_size, sides, seq_size * row_span, side_width)
    early = jnp.transpose(early, (0, 2, 1, 3)).reshape(model_width, sides * side_width)
    attention_old = early[:, :model_width]
    attention_right_whole = early[:, model_width : 2 * model_width]
    feed_old = early[:, 2 * model_width : 2 * model_width + hidden_width]
    feed_left_whole = early[:, 2 * model_width + hidden_width :]
    feed_old = jnp.where(
        at.matrix == 2, feed_old.reshape(hidden_width, model_width).T, feed_old
    )
    roots = jnp.stack(
        [low(expand_right_root[0]), low(expand_right_root[1]), low(shrink_left_root)]
        + [jnp.zeros(shrink_left_root.shape, jnp.bfloat16)]
    )
    feed_right_rows = at.exchange_owners(roots).reshape(-1, hidden_width)
    attention_left_rows = at.exchange_owners(low(attention_left_root)).reshape(-1, model_width)

    positions = sequence_position * width_bytes + jnp.arange(width_bytes, dtype=jnp.int32)
    is_valid = positions[None, :] < counts[:, None]
    embedded = jnp.where(is_valid[:, :, None], byte_rows, jnp.zeros_like(byte_rows))
    widened = padded_2(embedded, (("seq", 1),), 6).astype(jnp.float32)
    conv_out = sum(
        (
            vectors[tap_index] * widened[:, tap_index : tap_index + width_bytes + 9]
            for tap_index in range(4)
        )
    )
    pooled = []
    for block_size in range(1, 5):
        summed, counted = block_pool(conv_out, positions, block_size, row_len)
        pooled.append(summed / counted[:, None])
    size_scores = jnp.stack([jnp.sum(pooled_item * vectors[4], axis=-1) for pooled_item in pooled])
    size_weights = jax.nn.softmax(size_scores, axis=0)
    blended = sum(
        (size_weights[size_index][:, :, None] * pooled[size_index] for size_index in range(4))
    )
    tokens = blended.reshape(micro_rows * tok_local, 2, model_width).mean(axis=1)
    factor_one = rms_factor(tokens)
    normed = low(tokens * factor_one * vectors[5])

    normed_row = at.to_units(
        jnp.broadcast_to(
            normed.reshape(micro_rows, 1, tok_local, model_width),
            (micro_rows, at.head_groups, tok_local, model_width),
        )
    ).reshape(tok_row, model_width)
    qkv_row = low(dot(normed_row, weights_qkv, 1, 0))
    onehot = (buckets[:, None] == jnp.arange(bias_table.shape[0], dtype=jnp.int32)[None, :]).astype(
        jnp.float32
    )
    head_begin = (at.unit % at.head_groups) * heads
    part_table = lax.dynamic_slice_in_dim(bias_table, head_begin, heads, 1)
    bias_rel = jnp.einsum("xb,bh->hx", onehot, part_table, precision=HIGH_PRECISION)
    bias_rel = jnp.pad(bias_rel, ((0, 0), (0, 1)))
    seg_col = seg_row[:, None]
    seg_line = seg_row[None, :]
    tile = min(256, tok_row)
    attended_row, attended_f32, log_totals = attn_fwd(
        qkv_row, bias_rel, seg_col, seg_line, heads, tile
    )

    attended = at.exchange(attended_row.reshape(seq_size, tok_local, head_width))
    attended = attended.reshape(
        micro_rows, at.head_groups, at.repeat, tok_local, head_width
    )[:, :, 0]
    attended = jnp.transpose(attended, (0, 2, 1, 3)).reshape(-1, model_width)
    resid = tokens + dot(attended, weights_out, 1, 0)
    factor_two = rms_factor(resid)
    normed_two = low(resid * factor_two * vectors[6])

    normed_two_all = at.gather_parts(normed_two).reshape(-1, model_width)
    expanded = dot(normed_two_all, weights_expand, 1, 0)
    gate_pre = expanded[:, :hidden_part]
    upward = expanded[:, hidden_part:]
    activated, gelu_back = jax.vjp(functools.partial(jax.nn.gelu, approximate=True), gate_pre)
    hidden = low(activated * upward)
    grad_hidden = dot(grad_rows_all, weights_shrink, 1, 1)
    grad_gate_pre = low(gelu_back(grad_hidden * upward)[0])
    grad_upward = low(grad_hidden * activated)
    grad_expanded = jnp.concatenate([grad_gate_pre, grad_upward], axis=1)
    grad_normed_two = at.scatter_parts(
        dot(grad_expanded, weights_expand, 1, 1).reshape(parts, -1, model_width)
    )
    shrink_out = at.scatter_parts(
        dot(hidden, weights_shrink, 1, 0).reshape(parts, -1, model_width)
    )
    layer_output = low(resid + shrink_out).reshape(micro_rows, tok_local, model_width)
    grad_shrink_t = dot(grad_rows_all, hidden, 0, 0)
    grad_gate_w = dot(normed_two_all, grad_gate_pre, 0, 0)
    grad_up_w = dot(normed_two_all, grad_upward, 0, 0)

    grad_resid_norm, grad_gain_two = norm_back(resid, factor_two, vectors[6], grad_normed_two)
    grad_resid = grad_rows_out.astype(jnp.float32) + grad_resid_norm
    grad_branch = low(grad_resid)
    grad_attended = low(dot(grad_branch, weights_out, 1, 1))
    grad_attended = jnp.transpose(
        grad_attended.reshape(micro_rows, tok_local, at.head_groups, 1, head_width), (0, 2, 3, 1, 4)
    )
    grad_attended = jnp.pad(
        grad_attended, ((0, 0), (0, 0), (0, at.repeat - 1), (0, 0), (0, 0))
    )
    grad_attended_row = at.exchange(
        grad_attended.reshape(seq_size, tok_local, head_width)
    ).reshape(tok_row, head_width)
    grad_output_proj = at.scatter_parts(
        dot(attended, grad_branch, 0, 0).reshape(parts, model_width // parts, model_width)
    )

    def to_sides(block):
        return block.reshape((sides, block.shape[0] // sides) + block.shape[1:])

    feed_blocks = [to_sides(low(item)) for item in (grad_gate_w, grad_up_w, grad_shrink_t)]
    out_block = to_sides(low(grad_output_proj)).reshape(sides, -1, hidden_part)
    out_rows = out_block.shape[1]
    out_block = jnp.pad(
        out_block, ((0, 0), (0, feed_blocks[0].shape[1] - out_rows), (0, 0))
    )
    feed_sum = at.scatter(jnp.concatenate(feed_blocks + [out_block], axis=0), "seq", at.seq)
    feed_sum = at.gather_members(low(at.sum_groups(feed_sum)))
    full_output = feed_sum[:, :, :out_rows].reshape(model_width, model_width)
    full_feed = jnp.transpose(feed_sum, (1, 2, 0, 3)).reshape(model_width, hidden_width)

    def new_momenta(old, full):
        return low(MOMENTUM * old.astype(jnp.float32) + full.astype(jnp.float32))

    def strips(full):
        return at.block_rows(full).reshape(-1, full.shape[1])

    is_shrink = at.matrix == 2
    full_feed_t = full_feed.T
    feed_rows = strips(full_feed)
    feed_cols = strips(full_feed_t)
    feed_left = low(dot(feed_rows, full_feed, 1, 1))
    feed_right = low(dot(feed_cols, full_feed_t, 1, 1))
    feed_product = low(dot(new_momenta(feed_old, full_feed), feed_right_rows, 1, 1))
    feed_step = low(dot(feed_left_whole, feed_product, 1, 0))
    own_cols = feed_step.shape[1]
    moved = feed_step.reshape(dp_size, matrices, sides, row_span, own_cols)
    moved = jnp.transpose(moved, (0, 2, 1, 3, 4)).reshape(
        dp_size * sides, matrices * row_span, own_cols
    )
    moved = at.exchange_holders(moved).reshape(
        dp_size, sides, matrices * row_span, matrices, hidden_span
    )
    moved = jnp.transpose(moved, (2, 0, 3, 1, 4)).reshape(matrices, row_span, hidden_width)
    feed_step = jnp.where(
        is_shrink, feed_step.T.reshape(matrices, row_span, hidden_width), moved
    )
    feed_grad = jnp.where(
        is_shrink,
        feed_cols.reshape(matrices, row_span, hidden_width),
        feed_rows.reshape(matrices, row_span, hidden_width),
    )
    feed_out = at.exchange_owners(
        jnp.concatenate(
            [feed_step, feed_grad, feed_right.reshape(matrices, hidden_span, hidden_width)], axis=1
        )
    ).astype(jnp.float32)
    feed_left_out = at.exchange_owners(feed_left.reshape(matrices, row_span, model_width)).astype(
        jnp.float32
    )

    grad_qkv_row, grad_bias = attn_bwd(
        qkv_row,
        grad_attended_row,
        attended_f32,
        log_totals,
        bias_rel,
        seg_col,
        seg_line,
        heads,
        tile,
    )
    grad_qkv = dot(normed_row, grad_qkv_row, 0, 0)
    sum_qkv = at.scatter_parts(grad_qkv.reshape(parts, model_width // parts, 3 * head_width))
    side_rows = model_width // (parts * sides)
    sum_qkv = low(sum_qkv).reshape(sides, side_rows, 3, head_width)
    sum_qkv = jnp.pad(jnp.transpose(sum_qkv, (2, 0, 1, 3)), ((0, 1), (0, 0), (0, 0), (0, 0)))
    sum_qkv = at.exchange(sum_qkv.reshape(seq_size, side_rows, head_width)).reshape(
        micro_rows, at.head_groups, at.repeat, side_rows, head_width
    )
    sum_qkv = jnp.sum(sum_qkv.astype(jnp.float32), axis=(0, 2))
    sum_qkv = at.sum_groups(jnp.transpose(sum_qkv, (1, 0, 2)).reshape(side_rows, model_width))
    full_qkv = at.gather_members(low(sum_qkv)).reshape(model_width, model_width)
    grad_normed_part = low(dot(grad_qkv_row, weights_qkv, 1, 1))
    grad_normed = at.exchange(grad_normed_part.reshape(seq_size, tok_local, model_width))
    grad_normed = jnp.sum(
        grad_normed.reshape(micro_rows, -1, tok_local, model_width).astype(jnp.float32), axis=1
    ).reshape(micro_rows * tok_local, model_width)
    grad_tokens_norm, grad_gain_one = norm_back(tokens, factor_one, vectors[5], grad_normed)
    grad_tokens = (grad_resid + grad_tokens_norm).reshape(micro_rows, tok_local, model_width)

    grad_blend = jnp.repeat(grad_tokens, 2, axis=1) * 0.5
    grad_weights = jnp.stack([jnp.sum(grad_blend * pooled_item, axis=-1) for pooled_item in pooled])
    grad_sizes = size_weights * (
        grad_weights - jnp.sum(size_weights * grad_weights, axis=0, keepdims=True)
    )
    grad_score = sum(
        (
            jnp.sum(grad_sizes[size_index][:, :, None] * pooled[size_index], axis=(0, 1))
            for size_index in range(4)
        )
    )
    grad_pooled = jnp.stack(
        [
            size_weights[size_index][:, :, None] * grad_blend
            + grad_sizes[size_index][:, :, None] * vectors[4]
            for size_index in range(4)
        ]
    )
    wide_grads = padded_2(low(grad_pooled), (("seq", 2),), 6).astype(jnp.float32)
    ext_positions = sequence_position * width_bytes + jnp.arange(width_bytes + 3, dtype=jnp.int32)
    in_range = (ext_positions < row_len).astype(jnp.float32)[:, None]
    grad_conv = jnp.zeros((micro_rows, width_bytes + 3, model_width), jnp.float32)
    for block_size in range(1, 5):
        summed, counted = block_pool(
            wide_grads[block_size - 1][:, 3:], ext_positions, block_size, row_len
        )
        grad_conv = grad_conv + summed / jnp.maximum(counted, 1.0)[:, None] * in_range
    grad_embedded = sum(
        (
            vectors[tap_index] * grad_conv[:, 3 - tap_index : 3 - tap_index + width_bytes]
            for tap_index in range(4)
        )
    )
    grad_taps = [
        jnp.sum(
            grad_conv[:, :width_bytes] * widened[:, 3 + tap_index : 3 + tap_index + width_bytes],
            axis=(0, 1),
        )
        for tap_index in range(4)
    ]
    input_grads = jnp.where(is_valid[:, :, None], grad_embedded, 0.0)
    grad_vectors = jnp.stack(grad_taps + [grad_score, grad_gain_one, grad_gain_two])
    part_grad = jnp.einsum("xb,hx->bh", onehot, grad_bias[:, :-1], precision=HIGH_PRECISION)
    grad_table = lax.dynamic_update_slice_in_dim(
        jnp.zeros_like(bias_table), part_grad, head_begin, 1
    )
    small = jnp.pad(grad_table.reshape(-1), (0, model_width - grad_table.size))
    small = at.sum_all(jnp.concatenate([grad_vectors, small[None]], axis=0))
    sum_vectors = small[:-1]
    sum_table = small[-1, : grad_table.size].reshape(grad_table.shape)
    total_tokens = micro_rows * at.dp_size * tok_row
    small_rate = SMALL_RATE / math.sqrt(total_tokens)
    vector_momenta_new = MOMENTUM * vector_momenta + sum_vectors
    vectors_new = vectors - small_rate * vector_momenta_new
    table_momenta_new = MOMENTUM * table_momenta + sum_table
    table_new = bias_table - small_rate * table_momenta_new

    full_attention = jnp.where(at.matrix == 3, full_output, full_qkv)
    full_attention_t = full_attention.T
    rows = strips(full_attention)
    attention_product = low(
        dot(attention_left_rows, new_momenta(attention_old, full_attention), 1, 0)
    )
    attention_parts = [
        low(dot(rows, full_attention, 1, 1)),
        low(dot(strips(full_attention_t), full_attention_t, 1, 1)),
        low(dot(attention_product, attention_right_whole, 1, 0)),
        rows,
    ]
    attention_out = at.exchange_owners(
        jnp.concatenate(
            [item.reshape(matrices, row_span, model_width) for item in attention_parts], axis=1
        )
    ).astype(jnp.float32)
    sum_left, sum_right, step, grads = [
        attention_out[:, i * row_span : (i + 1) * row_span] for i in range(4)
    ]

    def statistics(old, increment):
        return STAT_DECAY * old + (1.0 - STAT_DECAY) * increment

    attention_new = attention_weights - MATRIX_RATE * step
    attention_left_new = statistics(attention_left, sum_left)
    attention_right_new = statistics(attention_right, sum_right)
    attention_mom_new = MOMENTUM * attention_momenta + grads

    step, grads, sum_right = (
        feed_out[:, :row_span],
        feed_out[:, row_span : 2 * row_span],
        feed_out[:, 2 * row_span :],
    )
    expand_new = expand_weights - MATRIX_RATE * step[:2]
    expand_left_new = statistics(expand_left, feed_left_out[:2])
    expand_right_new = statistics(expand_right, sum_right[:2])
    expand_mom_new = MOMENTUM * expand_momenta + grads[:2]
    shrink_new = shrink_weights - MATRIX_RATE * step[2].reshape(shrink_weights.shape)
    shrink_left_new = statistics(down_left_statistics, sum_right[2])
    shrink_right_new = statistics(shrink_right, feed_left_out[2])
    shrink_mom_new = MOMENTUM * shrink_momenta + grads[2].reshape(shrink_weights.shape)
    return (
        layer_output,
        input_grads,
        vectors_new,
        vector_momenta_new,
        table_new,
        table_momenta_new,
        attention_new,
        attention_left_new,
        attention_right_new,
        attention_mom_new,
        low(attention_new),
        expand_new,
        expand_left_new,
        expand_right_new,
        expand_mom_new,
        low(expand_new),
        shrink_new,
        shrink_left_new,
        shrink_right_new,
        shrink_mom_new,
        low(shrink_new),
    )


def solution(mesh):
    row = P("dp", "seq", None)
    stack = P(None, BOTH, None)
    flat = P(BOTH, None)
    return jax.shard_map(
        per_device,
        mesh=mesh,
        in_specs=(row, P("dp", "seq"), P("dp"), P(), row)
        + (P(),) * 4
        + (stack,) * 12
        + (flat,) * 6,
        out_specs=(row, row) + (P(),) * 4 + (stack,) * 10 + (flat,) * 5,
        check_vma=False,
    )
```

```python
import functools
import math

import jax
import jax.numpy as jnp
from jax import lax
from jax.experimental import pallas as pl
from jax.experimental.pallas import tpu as pltpu
from jax.sharding import PartitionSpec as P

EPSILON = 1e-06
STAT_DECAY = 0.95
MOMENTUM = 0.9
MATRIX_RATE = 0.1
SMALL_RATE = 0.1
MASKED = -1e30
HIGH_PRECISION = lax.Precision.HIGHEST
BOTH = ("dp", "seq")


def fill_bias(brel_ref, bias_sc, heads, tile):
    span = brel_ref.shape[1]
    rows = lax.broadcasted_iota(jnp.int32, (8, span), 0)
    for h in range(heads):
        wide = jnp.broadcast_to(brel_ref[h:h + 1, :], (8, span))
        first = wide
        for i in range(8):
            first = jnp.where(rows == i, pltpu.roll(wide, span - (tile - 1) + i, 1), first)
        bias_sc[h, 0:8, :] = first
        size = 8
        while size < tile:
            bias_sc[h, size:2 * size, :] = pltpu.roll(bias_sc[h, 0:size, :], size, 1)
            size *= 2

def attn_fwd_kernel(heads, tile, qkv_ref, brel_ref, segc_ref, segr_ref, out_ref, outf_ref, lse_ref, bias_sc):
    step = pl.program_id(0)
    length = qkv_ref.shape[0]
    width = qkv_ref.shape[1] // 3
    dh = outf_ref.shape[1] // heads

    @pl.when(step == 0)
    def _():
        fill_bias(brel_ref, bias_sc, heads, tile)

    begin = pl.multiple_of(step * tile, tile)
    offset = pl.multiple_of(length - tile - begin, 128)
    same = segc_ref[...] == segr_ref[...]
    lanes = lax.broadcasted_iota(jnp.int32, (tile, 128), 1)
    lse_all = jnp.zeros((tile, 128), jnp.float32)
    outs = []
    for h in range(heads):
        q = qkv_ref[pl.ds(begin, tile), h * dh:(h + 1) * dh]
        k = qkv_ref[:, width + h * dh:width + (h + 1) * dh]
        v = qkv_ref[:, 2 * width + h * dh:2 * width + (h + 1) * dh]
        scores = lax.dot_general(q, k, (((1,), (1,)), ((), ())), preferred_element_type=jnp.float32)
        scores = jnp.where(same, scores + bias_sc[h, :, pl.ds(offset, length)], MASKED)
        top = jnp.max(scores, axis=1, keepdims=True)
        probs = jnp.exp(scores - top)
        total = jnp.sum(probs, axis=1, keepdims=True)
        out = lax.dot_general(probs.astype(jnp.bfloat16), v, (((1,), (0,)), ((), ())), preferred_element_type=jnp.float32)
        outs.append(out / total)
        lse_all = jnp.where(lanes == h, top + jnp.log(total), lse_all)
    joined = jnp.concatenate(outs, axis=1)
    outf_ref[...] = joined
    fill = out_ref.shape[1] - joined.shape[1]
    if fill:
        joined = jnp.concatenate([joined, jnp.zeros((tile, fill), jnp.float32)], axis=1)
    out_ref[...] = joined.astype(jnp.bfloat16)
    lse_ref[...] = lse_all

def attn_fwd(qkv, brel, segc, segr, heads, dh, tile=128):
    length = qkv.shape[0]
    width = heads * dh
    full = lambda s: pl.BlockSpec(s, lambda i: (0,) * len(s))
    rowb = lambda w: pl.BlockSpec((tile, w), lambda i: (i, 0))
    return pl.pallas_call(
        functools.partial(attn_fwd_kernel, heads, tile),
        grid=(length // tile,),
        in_specs=[full(qkv.shape), full(brel.shape), rowb(1), full(segr.shape)],
        out_specs=[rowb(qkv.shape[1] // 3), rowb(width), rowb(128)],
        out_shape=[jax.ShapeDtypeStruct((length, qkv.shape[1] // 3), jnp.bfloat16), jax.ShapeDtypeStruct((length, width), jnp.float32), jax.ShapeDtypeStruct((length, 128), jnp.float32)],
        scratch_shapes=[pltpu.VMEM((heads, tile, 2 * length), jnp.float32)],
        compiler_params=pltpu.CompilerParams(vmem_limit_bytes=48 * 2**20),
        cost_estimate=pl.CostEstimate(flops=4 * length * length * width, bytes_accessed=6 * length * width * 2, transcendentals=heads * length * length),
    )(qkv, brel, segc, segr)

def attn_bwd_kernel(heads, tile, trans, qkv_ref, grad_ref, outf_ref, lse_ref, brel_ref, segc_ref, segr_ref, dqkv_ref, gb_ref, bias_sc, gb_sc, dk_sc, dv_sc):
    step = pl.program_id(0)
    length = qkv_ref.shape[0]
    width = qkv_ref.shape[1] // 3
    dh = outf_ref.shape[1] // heads

    @pl.when(step == 0)
    def _():
        fill_bias(brel_ref, bias_sc, heads, tile)
        gb_sc[...] = jnp.zeros_like(gb_sc)
        dk_sc[...] = jnp.zeros_like(dk_sc)
        dv_sc[...] = jnp.zeros_like(dv_sc)

    begin = pl.multiple_of(step * tile, tile)
    offset = pl.multiple_of(length - tile - begin, 128)
    same = segc_ref[...] == segr_ref[...]
    dqs = []
    for h in range(heads):
        q = qkv_ref[pl.ds(begin, tile), h * dh:(h + 1) * dh]
        k = qkv_ref[:, width + h * dh:width + (h + 1) * dh]
        v = qkv_ref[:, 2 * width + h * dh:2 * width + (h + 1) * dh]
        g = grad_ref[:, h * dh:(h + 1) * dh]
        delta = jnp.sum(g.astype(jnp.float32) * outf_ref[:, h * dh:(h + 1) * dh], axis=1, keepdims=True)
        lse = lse_ref[:, h:h + 1]
        scores = lax.dot_general(q, k, (((1,), (1,)), ((), ())), preferred_element_type=jnp.float32)
        scores = jnp.where(same, scores + bias_sc[h, :, pl.ds(offset, length)], MASKED)
        probs = jnp.exp(scores - lse)
        gp = lax.dot_general(g, v, (((1,), (1,)), ((), ())), preferred_element_type=jnp.float32)
        gs = (probs * (gp - delta))
        gsb = gs.astype(jnp.bfloat16)
        pb = probs.astype(jnp.bfloat16)
        gb_sc[h, :, pl.ds(offset, length)] += gsb.astype(jnp.float32)
        dqs.append(lax.dot_general(gsb, k, (((1,), (0,)), ((), ())), preferred_element_type=jnp.float32))
        if trans:
            dk_sc[h] += lax.dot_general(q, gsb, (((0,), (0,)), ((), ())), preferred_element_type=jnp.float32)
            dv_sc[h] += lax.dot_general(g, pb, (((0,), (0,)), ((), ())), preferred_element_type=jnp.float32)
        else:
            dk_sc[h] += lax.dot_general(gsb, q, (((0,), (0,)), ((), ())), preferred_element_type=jnp.float32)
            dv_sc[h] += lax.dot_general(pb, g, (((0,), (0,)), ((), ())), preferred_element_type=jnp.float32)
    fill = width - heads * dh

    def slot(parts):
        rows = parts[0].shape[0]
        filled = parts + ([jnp.zeros((rows, fill), jnp.float32)] if fill else [])
        return jnp.concatenate(filled, axis=1).astype(jnp.bfloat16)

    dqkv_ref[pl.ds(begin, tile), 0:width] = slot(dqs)

    @pl.when(step == pl.num_programs(0) - 1)
    def _():
        turn = (lambda x: x.T) if trans else (lambda x: x)
        dqkv_ref[:, width:2 * width] = slot([turn(dk_sc[h]) for h in range(heads)])
        dqkv_ref[:, 2 * width:3 * width] = slot([turn(dv_sc[h]) for h in range(heads)])
        span = gb_sc.shape[2]
        rows = lax.broadcasted_iota(jnp.int32, (8, span), 0)
        for h in range(heads):
            size = tile // 2
            part = gb_sc[h]
            while size >= 8:
                part = part[:size] + pltpu.roll(part[size:], span - size, 1)
                size //= 2
            line = jnp.zeros((1, span), jnp.float32)
            for i in range(8):
                line = line + jnp.sum(jnp.where(rows == i, pltpu.roll(part, (tile - 1 - i) % span, 1), 0.0), axis=0, keepdims=True)
            gb_ref[h:h + 1, :] = line

def attn_bwd(qkv, grad, outf, lse, brel, segc, segr, heads, tile=128, trans=True):
    length, width = outf.shape
    dh = width // heads
    full = lambda s: pl.BlockSpec(s, lambda i: (0,) * len(s))
    rowb = lambda w: pl.BlockSpec((tile, w), lambda i: (i, 0))
    acc = (heads, dh, length) if trans else (heads, length, dh)
    return pl.pallas_call(
        functools.partial(attn_bwd_kernel, heads, tile, trans),
        grid=(length // tile,),
        in_specs=[full(qkv.shape), rowb(grad.shape[1]), rowb(width), rowb(128), full(brel.shape), rowb(1), full(segr.shape)],
        out_specs=[full(qkv.shape), full(brel.shape)],
        out_shape=[jax.ShapeDtypeStruct(qkv.shape, jnp.bfloat16), jax.ShapeDtypeStruct(brel.shape, jnp.float32)],
        scratch_shapes=[pltpu.VMEM((heads, tile, 2 * length), jnp.float32), pltpu.VMEM((heads, tile, 2 * length), jnp.float32), pltpu.VMEM(acc, jnp.float32), pltpu.VMEM(acc, jnp.float32)],
        compiler_params=pltpu.CompilerParams(vmem_limit_bytes=56 * 2**20),
        cost_estimate=pl.CostEstimate(flops=10 * length * length * width, bytes_accessed=12 * length * width * 2, transcendentals=heads * length * length),
    )(qkv, grad, outf, lse, brel, segc, segr)

def byte_window(bytes_ref, counts_ref, taps, begin, span, place, row_len):
    row = pl.program_id(0)
    positions = place + begin + lax.broadcasted_iota(jnp.int32, (span, 1), 0)
    window = bytes_ref[0, pl.ds(begin, span), :].astype(jnp.float32)
    valid = (positions >= 0) & (positions < counts_ref[row])
    embedded = jnp.where(valid, window, 0.0)
    conv = embedded * taps[3:4]
    for tap in range(3):
        conv = conv + pltpu.roll(embedded, 3 - tap, 0) * taps[tap : tap + 1]
    conv = jnp.where(positions < row_len, conv, 0.0)
    return positions, embedded, conv


def block_sums(values, positions, span):
    ahead = [None] + [pltpu.roll(values, span - i, 0) for i in (1, 2)]
    behind = [None] + [pltpu.roll(values, i, 0) for i in (1, 2)]
    two = values + jnp.where(positions % 2 == 0, ahead[1], behind[1])
    four = two + jnp.where(
        positions % 4 < 2, pltpu.roll(two, span - 2, 0), pltpu.roll(two, 2, 0)
    )
    phase = (positions + 9) % 3
    three = (
        values
        + jnp.where(phase != 2, ahead[1], behind[2])
        + jnp.where(phase == 0, ahead[2], behind[1])
    )
    return two, three, four


def three_sum(values, positions, span):
    phase = (positions + 9) % 3
    return (
        values
        + jnp.where(phase != 2, pltpu.roll(values, span - 1, 0), pltpu.roll(values, 2, 0))
        + jnp.where(phase == 0, pltpu.roll(values, span - 2, 0), pltpu.roll(values, 1, 0))
    )


def three_share(positions, row_len):
    left = row_len - (positions - (positions + 9) % 3)
    return jnp.where(left >= 3, 1.0 / 3.0, jnp.where(left == 2, 0.5, 1.0))


def block_means(conv, positions, span, row_len):
    two, three, four = block_sums(conv, positions, span)
    return [conv, two * 0.5, three * three_share(positions, row_len), four * 0.25]


def size_softmax(pooled, score_row):
    scores = [jnp.sum(item * score_row, axis=1, keepdims=True) for item in pooled]
    top = functools.reduce(jnp.maximum, scores)
    powers = [jnp.exp(item - top) for item in scores]
    total = sum(powers)
    return [item / total for item in powers]


def tokens_kernel(row_len, halo, chunk, counts_ref, place_ref, bytes_ref, vectors_ref, tokens_ref, normed_ref, pair_ref):
    span = chunk + 2 * halo
    taps = vectors_ref[0:4, :]

    def visit(index, carry):
        begin = pl.multiple_of(index * chunk, chunk)
        positions, embedded, conv = byte_window(
            bytes_ref, counts_ref, taps, begin, span, place_ref[0], row_len
        )
        pooled = block_means(conv, positions, span, row_len)
        pooled = [item[halo : halo + chunk] for item in pooled]
        weights = size_softmax(pooled, vectors_ref[4:5, :])
        blended = sum(weight * item for weight, item in zip(weights, pooled))
        half = chunk // 2
        halves = []
        for lane in range(pair_ref.shape[0]):
            pair_ref[lane] = blended[:, lane * 128 : (lane + 1) * 128]
            halves.append(
                pair_ref[lane, pl.Slice(0, half, 2), :] + pair_ref[lane, pl.Slice(1, half, 2), :]
            )
        tokens = 0.5 * jnp.concatenate(halves, axis=1)
        factor = lax.rsqrt(jnp.mean(tokens * tokens, axis=1, keepdims=True) + EPSILON)
        rows = pl.ds(pl.multiple_of(index * half, half), half)
        tokens_ref[rows, :] = tokens
        normed_ref[rows, :] = (tokens * factor * vectors_ref[5:6, :]).astype(jnp.bfloat16)
        return carry

    lax.fori_loop(0, (bytes_ref.shape[1] - 2 * halo) // chunk, visit, 0)


def make_tokens(counts, place, wide_bytes, vectors, row_len, halo=8, chunk=64):
    micro, wide, width = wide_bytes.shape
    count = (wide - 2 * halo) // 2
    return pl.pallas_call(
        functools.partial(tokens_kernel, row_len, halo, chunk),
        grid=(micro,),
        in_specs=[
            pl.BlockSpec(memory_space=pltpu.SMEM),
            pl.BlockSpec(memory_space=pltpu.SMEM),
            pl.BlockSpec((1, wide, width), lambda i: (i, 0, 0)),
            pl.BlockSpec(vectors.shape, lambda i: (0, 0)),
        ],
        out_specs=[pl.BlockSpec((count, width), lambda i: (i, 0))] * 2,
        out_shape=[
            jax.ShapeDtypeStruct((micro * count, width), jnp.float32),
            jax.ShapeDtypeStruct((micro * count, width), jnp.bfloat16),
        ],
        scratch_shapes=[pltpu.VMEM((width // 128, chunk, 128), jnp.float32)],
        compiler_params=pltpu.CompilerParams(vmem_limit_bytes=32 * 2**20),
        cost_estimate=pl.CostEstimate(
            flops=60 * micro * wide * width, bytes_accessed=6 * micro * wide * width, transcendentals=0
        ),
    )(counts, place, wide_bytes, vectors)


def bytes_kernel(row_len, halo, chunk, counts_ref, place_ref, bytes_ref, grads_ref, vectors_ref, out_ref, sums_ref, spread_ref, parts_ref):
    row = pl.program_id(0)
    span = chunk + 2 * halo
    taps = vectors_ref[0:4, :]
    score_row = vectors_ref[4:5, :]
    half = grads_ref.shape[1]
    for lane in range(spread_ref.shape[0]):
        lanes = grads_ref[0, :, lane * 128 : (lane + 1) * 128] * 0.5
        spread_ref[lane, pl.Slice(0, half, 2), :] = lanes
        spread_ref[lane, pl.Slice(1, half, 2), :] = lanes

    @pl.when(row == 0)
    def _():
        parts_ref[...] = jnp.zeros_like(parts_ref)

    def visit(index, carry):
        begin = pl.multiple_of(index * chunk, chunk)
        positions, embedded, conv = byte_window(
            bytes_ref, counts_ref, taps, begin, span, place_ref[0], row_len
        )
        pooled = block_means(conv, positions, span, row_len)
        weights = size_softmax(pooled, score_row)
        grad = jnp.concatenate(
            [spread_ref[lane, pl.ds(begin, span), :] for lane in range(spread_ref.shape[0])], axis=1
        )
        along = [jnp.sum(grad * item, axis=1, keepdims=True) for item in pooled]
        mean = sum(weight * item for weight, item in zip(weights, along))
        sizes = [weight * (item - mean) for weight, item in zip(weights, along)]
        first, second, third, fourth = [
            weight * grad + size * score_row for weight, size in zip(weights, sizes)
        ]
        even = positions % 2 == 0
        pair = 0.5 * second + 0.25 * fourth
        fours = 0.25 * fourth
        pair = pair + jnp.where(even, pltpu.roll(pair, span - 1, 0), pltpu.roll(pair, 1, 0))
        fours = fours + jnp.where(even, pltpu.roll(fours, span - 1, 0), pltpu.roll(fours, 1, 0))
        fours = jnp.where(
            positions % 4 < 2, pltpu.roll(fours, span - 2, 0), pltpu.roll(fours, 2, 0)
        )
        share = three_share(positions, row_len)
        grad_conv = first + pair + fours + three_sum(third, positions, span) * share
        grad_conv = jnp.where((positions < row_len) & (positions >= 0), grad_conv, 0.0)
        back = grad_conv * taps[3:4]
        for tap in range(3):
            back = back + pltpu.roll(grad_conv, span - (3 - tap), 0) * taps[tap : tap + 1]
        own = slice(halo, halo + chunk)
        back = jnp.where(positions < counts_ref[row], back, 0.0)
        out_ref[0, pl.ds(begin, chunk), :] = back[own]

        def fold(values):
            return jnp.sum(values.reshape(chunk // 8, 8, values.shape[1]), axis=0)

        for tap in range(4):
            beside = embedded if tap == 3 else pltpu.roll(embedded, 3 - tap, 0)
            parts_ref[tap] += fold((grad_conv * beside)[own])
        parts_ref[4] += fold(sum(size * item for size, item in zip(sizes, pooled))[own])
        return carry

    lax.fori_loop(0, (bytes_ref.shape[1] - 2 * halo) // chunk, visit, 0)

    @pl.when(row == pl.num_programs(0) - 1)
    def _():
        sums_ref[...] = jnp.zeros_like(sums_ref)
        for item in range(5):
            sums_ref[item : item + 1, :] = jnp.sum(parts_ref[item], axis=0, keepdims=True)


def bytes_back(counts, place, wide_bytes, wide_grads, vectors, row_len, halo=8, chunk=64):
    micro, wide, width = wide_bytes.shape
    count = wide - 2 * halo
    return pl.pallas_call(
        functools.partial(bytes_kernel, row_len, halo, chunk),
        grid=(micro,),
        in_specs=[
            pl.BlockSpec(memory_space=pltpu.SMEM),
            pl.BlockSpec(memory_space=pltpu.SMEM),
            pl.BlockSpec((1, wide, width), lambda i: (i, 0, 0)),
            pl.BlockSpec((1, wide // 2, width), lambda i: (i, 0, 0)),
            pl.BlockSpec(vectors.shape, lambda i: (0, 0)),
        ],
        out_specs=[
            pl.BlockSpec((1, count, width), lambda i: (i, 0, 0)),
            pl.BlockSpec((8, width), lambda i: (0, 0)),
        ],
        out_shape=[
            jax.ShapeDtypeStruct((micro, count, width), jnp.float32),
            jax.ShapeDtypeStruct((8, width), jnp.float32),
        ],
        scratch_shapes=[
            pltpu.VMEM((width // 128, wide, 128), jnp.float32),
            pltpu.VMEM((5, 8, width), jnp.float32),
        ],
        compiler_params=pltpu.CompilerParams(vmem_limit_bytes=32 * 2**20),
        cost_estimate=pl.CostEstimate(
            flops=150 * micro * wide * width, bytes_accessed=8 * micro * wide * width, transcendentals=0
        ),
    )(counts, place, wide_bytes, wide_grads, vectors)

def low(values):
    return values.astype(jnp.bfloat16)


def dot(left_side, right_side, left_dim, right_dim):
    return lax.dot_general(
        left_side,
        right_side,
        (((left_dim,), (right_dim,)), ((), ())),
        preferred_element_type=jnp.float32,
    )


def rms_factor(values):
    return lax.rsqrt(jnp.mean(values * values, axis=-1, keepdims=True) + EPSILON)


def norm_back(values, factor, gain_row, grad_out):
    scaled = grad_out * gain_row
    grad_gain = jnp.sum(grad_out * values * factor, axis=0)
    inner_mean = jnp.mean(scaled * values, axis=-1, keepdims=True)
    return (factor * (scaled - values * inner_mean * factor * factor), grad_gain)


class Layout:
    def __init__(self, head_count, micro_rows):
        self.dp_size = lax.axis_size("dp")
        self.seq_size = lax.axis_size("seq")
        self.count = self.dp_size * self.seq_size
        self.dp = lax.axis_index("dp")
        self.seq = lax.axis_index("seq")
        self.micro = micro_rows
        self.parts = math.gcd(self.dp_size, head_count & -head_count)
        self.groups = self.dp_size // self.parts
        self.part = self.dp % self.parts
        self.head_groups = head_count & -head_count
        self.repeat = self.seq_size // (micro_rows * self.head_groups)
        self.unit = self.seq // self.repeat
        self.matrices = 4
        self.sides = self.seq_size // self.matrices
        self.matrix = self.seq % self.matrices
        self.side = self.seq // self.matrices
        self.member = self.dp * self.sides + self.side
        self.members = [
            [
                (group * self.parts + part) * self.seq_size + side * self.matrices + matrix
                for part in range(self.parts)
                for side in range(self.sides)
            ]
            for group in range(self.groups)
            for matrix in range(self.matrices)
        ]
        self.holders = [
            [
                dp * self.seq_size + side * self.matrices + matrix
                for dp in range(self.dp_size)
                for side in range(self.sides)
            ]
            for matrix in range(self.matrices)
        ]
        self.owners = [
            [side * self.matrices + matrix for matrix in range(self.matrices)]
            for side in range(self.sides)
        ]

    def flip(self, block, axis, bits):
        size = lax.axis_size(axis)
        return lax.ppermute(block, axis, [(i, i ^ bits) for i in range(size)])

    def gather_parts(self, block):
        pieces = {0: block}
        bit = self.parts // 2
        while bit:
            for key in list(pieces):
                pieces[key | bit] = self.flip(pieces[key], "dp", bit)
            bit //= 2
        whole = jnp.zeros((self.parts,) + block.shape, block.dtype)
        for key, piece in pieces.items():
            whole = lax.dynamic_update_index_in_dim(whole, piece, self.part ^ key, 0)
        return whole

    def scatter_step(self, blocks, axis, index, bit):
        pairs = blocks.reshape((blocks.shape[0] // 2, 2) + blocks.shape[1:])
        mine = (index // bit) % 2
        kept = lax.dynamic_index_in_dim(pairs, mine, 1, False)
        sent = lax.dynamic_index_in_dim(pairs, 1 - mine, 1, False)
        return kept.astype(jnp.float32) + self.flip(low(sent), axis, bit).astype(jnp.float32)

    def scatter(self, blocks, axis, index):
        bit = 1
        while blocks.shape[0] > 1:
            blocks = self.scatter_step(blocks, axis, index, bit)
            bit *= 2
        return blocks[0]

    def near_parts(self, block):
        pieces = {0: block}
        bit = self.parts // 2
        while bit:
            for key in list(pieces):
                pieces[key | bit] = self.flip(pieces[key], "dp", bit)
            bit //= 2
        return jnp.concatenate([pieces[key] for key in range(self.parts)], axis=0)

    def scatter_near(self, rows):
        blocks = rows.reshape((self.parts, -1) + rows.shape[1:])
        bit = 1
        while blocks.shape[0] > 1:
            pairs = blocks.reshape((blocks.shape[0] // 2, 2) + blocks.shape[1:])
            got = self.flip(low(pairs[:, 1]), "dp", bit)
            blocks = pairs[:, 0].astype(jnp.float32) + got.astype(jnp.float32)
            bit *= 2
        return blocks[0]

    def scatter_heads(self, blocks):
        index, bit = self.unit % self.head_groups, 1
        while blocks.shape[0] > 1:
            pairs = blocks.reshape((blocks.shape[0] // 2, 2) + blocks.shape[1:])
            mine = (index // bit) % 2
            kept = lax.dynamic_index_in_dim(pairs, mine, 1, False)
            sent = lax.dynamic_index_in_dim(pairs, 1 - mine, 1, False)
            got = self.flip(low(sent), "seq", bit * self.repeat)
            blocks = kept.astype(jnp.float32) + got.astype(jnp.float32)
            bit *= 2
        return blocks[0]

    def sum_groups(self, block):
        total = block
        for shift in range(1, self.groups):
            turn = [(i, (i + shift * self.parts) % self.dp_size) for i in range(self.dp_size)]
            total = total + lax.ppermute(low(block), "dp", turn).astype(jnp.float32)
        return total

    def to_units(self, blocks):
        shape = blocks.shape
        blocks = blocks[:, :, None]
        if self.repeat > 1:
            blocks = jnp.broadcast_to(blocks, shape[:2] + (self.repeat,) + shape[2:])
        return self.exchange(blocks.reshape((self.seq_size,) + shape[2:]))

    def exchange(self, blocks):
        return lax.all_to_all(blocks, "seq", 0, 0, tiled=True)

    def gather_step(self, pieces, bit, axis="seq"):
        grown = []
        for held in pieces:
            keys = sorted(held)
            moved = self.flip(jnp.stack([held[key] for key in keys]), axis, bit)
            held = dict(held)
            for place, key in enumerate(keys):
                held[key | bit] = moved[place]
            grown.append(held)
        return grown

    def gathered(self, held, index):
        whole = jnp.zeros((len(held),) + held[0].shape, held[0].dtype)
        for key, piece in held.items():
            whole = lax.dynamic_update_index_in_dim(whole, piece, index ^ key, 0)
        return whole

    def by_halves(self):
        return self.repeat == 1 and self.micro == 2 and self.head_groups == 4

    def rows_to_units(self, blocks, beside):
        held = [{0: beside}]
        bits = [1 << i for i in reversed(range(self.parts.bit_length() - 1))]
        if not self.by_halves():
            shape = blocks.shape
            blocks = jnp.broadcast_to(blocks[:, None], shape[:1] + (self.head_groups,) + shape[1:])
            whole = self.to_units(blocks)
            for bit in bits:
                held = self.gather_step(held, bit, "dp")
            return whole.reshape((-1,) + shape[2:]), self.gathered(held[0], self.part)
        mine = self.unit // self.head_groups
        near = lax.dynamic_index_in_dim(blocks, mine, 0, False)
        far = self.flip(lax.dynamic_index_in_dim(blocks, 1 - mine, 0, False), "seq", 4)
        near_one = self.flip(near, "seq", 1)
        far, held = lax.optimization_barrier((far, held))
        far_two = self.flip(far, "seq", 2)
        for bit in bits[:1]:
            held = self.gather_step(held, bit, "dp")
        near_one, far_two = lax.optimization_barrier((near_one, far_two))
        near_two = self.flip(jnp.stack([near, near_one]), "seq", 2)
        far_one = self.flip(jnp.stack([far, far_two]), "seq", 1)
        near_two, far_one, held = lax.optimization_barrier((near_two, far_one, held))
        for bit in bits[1:]:
            held = self.gather_step(held, bit, "dp")
        pieces = [near, near_one, near_two[0], near_two[1], far, far_one[0], far_two, far_one[1]]
        whole = self.gathered(dict(enumerate(pieces)), self.seq)
        return whole.reshape((-1,) + blocks.shape[2:]), self.gathered(held[0], self.part)

    def fold_units(self, row):
        blocks = row.reshape((self.seq_size, -1) + row.shape[1:])
        if not self.by_halves():
            return self.exchange(low(blocks))

        def pick(*keys):
            picked = [
                lax.dynamic_index_in_dim(blocks, self.seq ^ key, 0, False).astype(jnp.float32)
                for key in keys
            ]
            return jnp.stack(picked)

        near = pick(0, 1) + self.flip(low(pick(2, 3)), "seq", 2).astype(jnp.float32)
        far = pick(4, 6) + self.flip(low(pick(5, 7)), "seq", 1).astype(jnp.float32)
        return (near, far)

    def fold_halves(self, folded):
        if not self.by_halves():
            return folded
        near, far = folded
        near = near[0] + self.flip(low(near[1]), "seq", 1).astype(jnp.float32)
        far = far[0] + self.flip(low(far[1]), "seq", 2).astype(jnp.float32)
        return (near, far)

    def fold_rows(self, folded):
        if not self.by_halves():
            blocks = folded.astype(jnp.float32)
            return jnp.sum(blocks.reshape((self.micro, -1) + blocks.shape[1:]), axis=1)
        near, far = folded
        far = self.flip(low(far), "seq", 4).astype(jnp.float32)
        first = self.unit // self.head_groups == 0
        return jnp.stack([jnp.where(first, near, far), jnp.where(first, far, near)])

    def gather_members(self, block):
        whole = lax.all_gather(block, BOTH, axis=0, axis_index_groups=self.members)
        return whole.reshape((self.parts, self.sides) + block.shape)

    def spread_members(self, block):
        count = self.parts * self.sides
        blocks = jnp.broadcast_to(block[None], (count,) + block.shape)
        return lax.all_to_all(blocks, BOTH, 0, 0, tiled=True, axis_index_groups=self.members)

    def gather_holders(self, block):
        return lax.all_gather(block, BOTH, axis=0, axis_index_groups=self.holders, tiled=True)

    def exchange_holders(self, blocks):
        return lax.all_to_all(blocks, BOTH, 0, 0, tiled=True, axis_index_groups=self.holders)

    def exchange_owners(self, blocks):
        return lax.all_to_all(blocks, "seq", 0, 0, tiled=True, axis_index_groups=self.owners)


def after(value, token):
    return lax.optimization_barrier((value, token))[0]


def as_width(blocks, width):
    flat = blocks.reshape(blocks.shape[0], -1)
    short = -flat.shape[1] % width
    return jnp.pad(flat, ((0, 0), (0, short))).reshape(blocks.shape[0], -1, width)


def down_to_feed(blocks, width, lanes=256):
    lead, (rows, columns) = blocks.shape[:-2], blocks.shape[-2:]
    groups, parts = width // lanes, columns // lanes
    count = len(lead)
    blocks = blocks.reshape(lead + (groups, rows // groups, parts, lanes))
    order = tuple(range(count)) + (count + 2, count + 1, count, count + 3)
    return jnp.transpose(blocks, order).reshape(lead + (parts * rows // groups, width))


def feed_to_down(blocks, columns, lanes=256):
    lead, (rows, width) = blocks.shape[:-2], blocks.shape[-2:]
    groups, parts = width // lanes, columns // lanes
    count = len(lead)
    blocks = blocks.reshape(lead + (parts, rows // parts, groups, lanes))
    order = tuple(range(count)) + (count + 2, count + 1, count, count + 3)
    return jnp.transpose(blocks, order).reshape(lead + (groups * rows // parts, columns))


def of_width(blocks, rows, columns):
    flat = blocks.reshape(blocks.shape[0], -1)
    return flat[:, : rows * columns].reshape(blocks.shape[0], rows, columns)


def gather_all(block):
    return lax.all_gather(block, BOTH, axis=0, tiled=True)


def per_device(
    byte_rows,
    segments,
    counts,
    buckets,
    cotangent,
    vectors,
    vector_momenta,
    bias_table,
    table_momenta,
    attention_weights,
    attention_left,
    attention_right,
    attention_left_root,
    attention_right_root,
    attention_momenta,
    expand_weights,
    expand_left,
    expand_right,
    expand_left_root,
    expand_right_root,
    expand_momenta,
    shrink_weights,
    down_left_statistics,
    shrink_right,
    shrink_left_root,
    shrink_right_root,
    shrink_momenta,
):
    micro_rows, width_bytes, model_width = byte_rows.shape
    head_count = bias_table.shape[1]
    at = Layout(head_count, micro_rows)
    parts, part, seq_size, sequence_position = at.parts, at.part, at.seq_size, at.seq
    row_len = width_bytes * seq_size
    tok_local = width_bytes // 2
    tok_row = row_len // 2
    hidden_width = shrink_weights.shape[1 - 1] * at.count
    heads = head_count // parts
    head_width = model_width // parts
    hidden_part = hidden_width // parts

    row_span = model_width // at.count
    hidden_span = hidden_width // at.count
    dp_size, sides, matrices = at.dp_size, at.sides, at.matrices

    slot = -(-head_width // 128) * 128
    slot_fill = ((0, 0), (0, 0), (0, 0), (0, slot - head_width))
    split = low(attention_weights[:3]).reshape(3, row_span, at.head_groups, head_width)
    split = jnp.pad(jnp.transpose(split, (2, 1, 0, 3)), slot_fill).reshape(
        at.head_groups, row_span, 3 * slot
    )
    token_segs = segments[:, 0::2]
    digits = jnp.stack([token_segs // 64, token_segs % 64], axis=1).astype(jnp.bfloat16)
    digits = jnp.pad(digits, ((0, 0), (0, row_span - 2), (0, 0)))
    split = jnp.concatenate(
        [
            jnp.broadcast_to(split[None], (micro_rows,) + split.shape),
            jnp.broadcast_to(
                low(attention_weights[3]), (micro_rows, at.head_groups, row_span, model_width)
            ),
            jnp.broadcast_to(
                digits[:, None], (micro_rows, at.head_groups, row_span, tok_local)
            ),
        ],
        axis=3,
    )
    split = at.to_units(split)

    halo = 8
    count = at.seq_size
    forward = [(i, i + 1) for i in range(count - 1)]
    backward = [(i + 1, i) for i in range(count - 1)]
    wide_bytes = jnp.concatenate(
        [
            lax.ppermute(byte_rows[:, width_bytes - halo :], "seq", forward),
            byte_rows,
            lax.ppermute(byte_rows[:, :halo], "seq", backward),
        ],
        axis=1,
    )
    place = (sequence_position * width_bytes - halo).reshape(1)
    tokens, normed = make_tokens(counts, place, wide_bytes, vectors, row_len, halo)
    grad_rows_out = cotangent.reshape(-1, model_width)

    (
        expand_weights_in,
        shrink_weights_in,
        normed,
    ) = lax.optimization_barrier(
        (expand_weights, shrink_weights, normed)
    )
    def columns(whole, begin, width):
        return lax.dynamic_slice_in_dim(whole, begin, width, 1)

    if at.groups == 1:
        rest = low(expand_weights_in).reshape(2, row_span, parts, hidden_part)
        rest = jnp.transpose(rest, (2, 1, 0, 3)).reshape(parts, row_span, 2 * hidden_part)
        rest = lax.all_to_all(after(rest, split), "dp", 0, 0, tiled=True)
        bits = [1 << i for i in reversed(range(seq_size.bit_length() - 1))]
        rest = [{0: item} for item in (rest, low(shrink_weights_in))]
        rest = at.gather_step(rest, bits[0])
    else:
        rest = jnp.concatenate(
            [low(expand_weights_in[0]), low(expand_weights_in[1])]
            + [low(shrink_weights_in).reshape(row_span, hidden_width)],
            axis=1,
        )
        rest = gather_all(rest)
        weights_expand = jnp.concatenate(
            [
                columns(rest, i * hidden_width + part * hidden_part, hidden_part)
                for i in range(2)
            ],
            axis=1,
        )
        weights_shrink = lax.dynamic_slice(
            rest,
            (part * (model_width // parts), 2 * hidden_width),
            (model_width // parts, hidden_width),
        ).reshape(hidden_part, model_width)

    digits = split[:, :2, 3 * slot + model_width :].astype(jnp.int32)
    seg_row = (digits[:, 0] * 64 + digits[:, 1]).reshape(tok_row)
    split = split[:, :, : 3 * slot + model_width].reshape(
        seq_size * row_span, 3 * slot + model_width
    )
    def early_block(i):
        if i == 2:
            feed = [down_to_feed(low(shrink_momenta), hidden_width), low(shrink_right_root)]
        elif i < 2:
            feed = [low(expand_momenta[i]), low(expand_left_root[i])]
        else:
            feed = [jnp.zeros((row_span, hidden_width + model_width), jnp.bfloat16)]
        return jnp.concatenate(
            feed + [low(attention_momenta[i]), low(attention_right_root[i])], axis=1
        )

    early = jnp.stack([early_block(i) for i in range(matrices)])
    early_width = early.shape[2]

    early = at.exchange_owners(after(early, split)).reshape(-1, early_width)
    factor_one = rms_factor(tokens)

    normed_row, weights_qkv = at.rows_to_units(
        normed.reshape(micro_rows, tok_local, model_width), split
    )
    if at.groups > 1:
        weights_qkv = lax.all_gather(split, "dp", axis=0)
    weights_qkv = weights_qkv.reshape(model_width, 3 * slot + model_width)
    weights_qkv, weights_out = weights_qkv[:, : 3 * slot], weights_qkv[:, 3 * slot :]
    weights_out = jnp.pad(
        weights_out.reshape(at.head_groups, head_width, model_width),
        ((0, 0), (0, slot - head_width), (0, 0)),
    ).reshape(-1, model_width)
    grad_rows_all = at.near_parts(after(grad_rows_out, normed))
    qkv_row = low(dot(normed_row, weights_qkv, 1, 0))
    qkv_row, grad_rows_all, early = lax.optimization_barrier((qkv_row, grad_rows_all, early))
    early = at.gather_holders(early)
    if at.groups == 1:
        rest, qkv_row = lax.optimization_barrier((rest, qkv_row))
        for bit in bits[1:-1]:
            rest = at.gather_step(rest, bit)
    onehot = (buckets[:, None] == jnp.arange(bias_table.shape[0], dtype=jnp.int32)[None, :]).astype(
        jnp.float32
    )
    head_begin = (at.unit % at.head_groups) * heads
    part_table = lax.dynamic_slice_in_dim(bias_table, head_begin, heads, 1)
    bias_rel = jnp.einsum("xb,bh->hx", onehot, part_table, precision=HIGH_PRECISION)
    bias_rel = jnp.pad(bias_rel, ((0, 0), (0, 1)))
    seg_col = seg_row[:, None]
    seg_line = seg_row[None, :]
    tile = min(256, tok_row)
    attended_row, attended_f32, log_totals = attn_fwd(
        qkv_row, bias_rel, seg_col, seg_line, heads, head_width // heads, tile
    )
    if at.groups == 1:
        rest, attended_row = lax.optimization_barrier((rest, attended_row))
        rest = at.gather_step(rest, bits[-1])
    roots = jnp.stack(
        [low(expand_right_root[0]), low(expand_right_root[1]), low(shrink_left_root)]
        + [jnp.zeros(shrink_left_root.shape, jnp.bfloat16)]
    )
    lefts = jnp.pad(
        low(attention_left_root), ((0, 0), (0, 0), (0, hidden_width - model_width))
    )
    roots = at.exchange_owners(after(jnp.concatenate([roots, lefts], axis=1), attended_row))
    attended = at.exchange(attended_row.reshape(seq_size, tok_local, slot))
    attended = attended.reshape(
        micro_rows, at.head_groups, at.repeat, tok_local, slot
    )[:, :, 0]
    attended = jnp.transpose(attended, (0, 2, 1, 3)).reshape(micro_rows * tok_local, -1)
    resid = tokens + dot(attended, weights_out, 1, 0)
    factor_two = rms_factor(resid)
    normed_two = low(resid * factor_two * vectors[6])

    if at.groups == 1:
        rest, normed_two = lax.optimization_barrier((rest, normed_two))
        weights_shrink = at.gathered(rest[1], at.seq).reshape(hidden_part, model_width)
        weights_expand = jnp.transpose(at.gathered(rest[0], at.seq), (1, 0, 2, 3)).reshape(model_width, -1)
    normed_two_all = at.near_parts(normed_two)
    normed_two_all, roots = lax.optimization_barrier((normed_two_all, roots))
    expanded = dot(normed_two_all, weights_expand, 1, 0)
    gate_pre = expanded[:, :hidden_part]
    upward = expanded[:, hidden_part:]
    activated, gelu_back = jax.vjp(functools.partial(jax.nn.gelu, approximate=True), gate_pre)
    hidden = low(activated * upward)
    grad_hidden = dot(grad_rows_all, weights_shrink, 1, 1)
    grad_gate_pre = low(gelu_back(grad_hidden * upward)[0])
    grad_upward = low(grad_hidden * activated)
    grad_expanded = jnp.concatenate([grad_gate_pre, grad_upward], axis=1)
    grad_normed_two = at.scatter_near(dot(grad_expanded, weights_expand, 1, 1))
    grad_shrink_t = dot(grad_rows_all, hidden, 0, 0)
    grad_gate_w = dot(normed_two_all, grad_gate_pre, 0, 0)
    grad_up_w = dot(normed_two_all, grad_upward, 0, 0)

    feed_sum = [low(item) for item in (grad_gate_w, grad_up_w, grad_shrink_t)]
    feed_sum = jnp.stack(feed_sum + [jnp.zeros_like(feed_sum[0])])
    grad_normed_two = after(grad_normed_two, feed_sum)

    grad_resid_norm, grad_gain_two = norm_back(resid, factor_two, vectors[6], grad_normed_two)
    grad_resid = grad_rows_out.astype(jnp.float32) + grad_resid_norm
    grad_branch = low(grad_resid)
    grad_attended = low(dot(grad_branch, weights_out, 1, 1)).reshape(
        micro_rows, tok_local, at.head_groups, 1, slot
    )
    grad_attended = jnp.pad(
        jnp.transpose(grad_attended, (0, 2, 3, 1, 4)),
        ((0, 0), (0, 0), (0, at.repeat - 1), (0, 0), (0, 0)),
    )
    grad_attended, early = lax.optimization_barrier((grad_attended, early))
    grad_branch = after(grad_branch, grad_attended)
    grad_out = at.scatter(
        low(
            dot(attended, grad_branch, 0, 0)
            .reshape(at.head_groups, slot, model_width)[:, :head_width]
            .reshape(parts, -1, model_width)
        ),
        "dp",
        at.part,
    )
    grad_attended_row = at.exchange(
        grad_attended.reshape(seq_size, tok_local, slot)
    ).reshape(tok_row, slot)
    feed_sum = at.scatter_step(feed_sum, "seq", at.seq, 1)
    feed_sum = at.scatter_step(feed_sum, "seq", at.seq, 2)

    grad_qkv_row, grad_bias = attn_bwd(
        qkv_row,
        grad_attended_row,
        attended_f32,
        log_totals,
        bias_rel,
        seg_col,
        seg_line,
        heads,
        tile,
    )
    feed_sum, grad_qkv_row = lax.optimization_barrier((feed_sum, grad_qkv_row))
    grad_normed_part = low(dot(grad_qkv_row, weights_qkv, 1, 1))
    grad_normed_part = at.fold_units(grad_normed_part)
    feed_sum = feed_sum.reshape(model_width, hidden_part)
    bit = matrices
    while bit < seq_size:
        feed_sum = feed_sum + at.flip(low(feed_sum), "seq", bit).astype(jnp.float32)
        bit *= 2
    grad_qkv = low(dot(normed_row, grad_qkv_row, 0, 0))
    grad_normed_part, grad_qkv, grad_out = lax.optimization_barrier(
        (grad_normed_part, grad_qkv, grad_out)
    )
    grad_normed_part = at.fold_halves(grad_normed_part)
    feed_sum, grad_normed_part = lax.optimization_barrier((feed_sum, grad_normed_part))
    feed_sum = [{0: low(at.sum_groups(feed_sum))}]
    bit = parts // 2
    while bit > 1:
        feed_sum = at.gather_step(feed_sum, bit, "dp")
        bit //= 2
    shrink_out = after(low(dot(hidden, weights_shrink, 1, 0)), grad_normed_part)
    shrink_out = at.scatter_near(shrink_out)
    layer_output = low(resid + shrink_out).reshape(micro_rows, tok_local, model_width)
    feed_right_rows = roots[:, :hidden_span].reshape(-1, hidden_width)
    attention_left_rows = roots[:, hidden_span:, :model_width].reshape(-1, model_width)


    begins = [0, hidden_width, hidden_width + model_width, hidden_width + 2 * model_width]
    early = after(early, grad_qkv)
    feed_old = early[:, : begins[1]]
    feed_left_whole = early[:, begins[1] : begins[2]]
    attention_old = early[:, begins[2] : begins[3]]
    attention_right_whole = early[:, begins[3] :]
    is_shrink = at.matrix == 2
    feed_start = MOMENTUM * jnp.where(
        is_shrink,
        dot(
            feed_to_down(
                feed_old.reshape(at.count, row_span, hidden_width), model_width
            ).reshape(hidden_width, model_width),
            feed_right_rows,
            0,
            1,
        ),
        dot(feed_old, feed_right_rows, 1, 1),
    )
    attention_start = MOMENTUM * dot(attention_left_rows, attention_old, 1, 0)


    grad_out = jnp.transpose(
        grad_out.reshape(-1, at.head_groups, head_width), (1, 0, 2)
    )
    grad_out = at.scatter_heads(jnp.pad(grad_out, ((0, 0), (0, 0), (0, slot - head_width))))
    side_rows = model_width // (parts * sides)
    sums = at.scatter(grad_qkv.reshape(parts, -1, 3 * slot), "dp", at.part)
    sums = low(jnp.concatenate([sums, grad_out], axis=1))
    sums = jnp.transpose(sums.reshape(sides, side_rows, matrices, slot), (0, 2, 1, 3))
    sums = sums.reshape(seq_size, side_rows, slot)
    grad_normed = at.fold_rows(grad_normed_part).reshape(-1, model_width)
    sums, grad_normed, feed_sum = lax.optimization_barrier(
        (sums, grad_normed, feed_sum)
    )
    if parts > 1:
        feed_sum = at.gather_step(feed_sum, 1, "dp")
    full_feed = at.gathered(feed_sum[0], at.part)
    sums = at.exchange(sums).reshape(
        micro_rows, at.head_groups, at.repeat, side_rows, slot
    )[..., :head_width]
    sums = jnp.sum(sums.astype(jnp.float32), axis=(0, 2))
    sums = at.sum_groups(jnp.transpose(sums, (1, 0, 2)).reshape(side_rows, model_width))
    grad_tokens_norm, grad_gain_one = norm_back(tokens, factor_one, vectors[5], grad_normed)
    grad_tokens = (grad_resid + grad_tokens_norm).reshape(micro_rows, tok_local, model_width)

    edge = halo // 2
    wide_grads = jnp.concatenate(
        [
            lax.ppermute(grad_tokens[:, tok_local - edge :], "seq", forward),
            grad_tokens,
            lax.ppermute(grad_tokens[:, :edge], "seq", backward),
        ],
        axis=1,
    )
    full_attention = at.spread_members(low(sums)).reshape(model_width, model_width)
    wide_grads, feed_start, attention_start = lax.optimization_barrier(
        (wide_grads, feed_start, attention_start)
    )
    input_grads, grad_taps = bytes_back(counts, place, wide_bytes, wide_grads, vectors, row_len, halo)

    grad_vectors = jnp.concatenate(
        [grad_taps[:5], grad_gain_one[None], grad_gain_two[None]], axis=0
    )
    part_grad = jnp.einsum("xb,hx->bh", onehot, grad_bias[:, :-1], precision=HIGH_PRECISION)
    grad_table = lax.dynamic_update_slice_in_dim(
        jnp.zeros_like(bias_table), part_grad, head_begin, 1
    )
    small = jnp.pad(grad_table.reshape(-1), (0, model_width - grad_table.size))
    small = low(jnp.concatenate([grad_vectors, small[None]], axis=0))

    full_feed = after(full_feed, grad_taps)
    member_rows = matrices * row_span
    member_cols = matrices * hidden_span
    feed_rows = lax.dynamic_slice_in_dim(full_feed, at.member * member_rows, member_rows, 1)
    begin = at.member * member_cols
    feed_cols = lax.dynamic_slice(
        full_feed, (begin // hidden_part, 0, begin % hidden_part), (1, model_width, member_cols)
    )[0].T
    def to_owners(strips):
        strips = strips.reshape(strips.shape[0], matrices, row_span, strips.shape[2])
        return jnp.transpose(strips, (1, 2, 0, 3)).reshape(matrices, row_span, hidden_width)

    def down_to_owners(rows):
        return down_to_feed(rows.reshape(matrices, hidden_span, model_width), hidden_width)

    feed_product = low(
        feed_start
        + sum(
            dot(full_feed[i], columns(feed_right_rows, i * hidden_part, hidden_part), 1, 1)
            for i in range(parts)
        )
    )
    feed_step = low(dot(feed_left_whole, feed_product, 1, 0))
    moved = feed_step.reshape(-1, member_rows, member_cols)
    members = moved.shape[0]
    moved = at.exchange_holders(
        jnp.concatenate(
            [
                moved,
                jnp.broadcast_to(
                    small.reshape(1, -1, member_cols),
                    (members, small.size // member_cols, member_cols),
                ),
            ],
            axis=1,
        )
    )
    small = jnp.sum(moved[:, member_rows:].astype(jnp.float32), axis=0).reshape(small.shape)
    moved = moved[:, :member_rows]

    feed_right = jnp.concatenate(
        [low(dot(feed_cols, full_feed[i], 1, 0)) for i in range(parts)], axis=1
    )
    feed_left = low(sum(dot(feed_rows[i], full_feed[i], 1, 1) for i in range(parts)))
    rows = lax.dynamic_slice_in_dim(full_attention, at.member * member_rows, member_rows, 0)
    cols = columns(full_attention, at.member * member_rows, member_rows)
    attention_product = low(attention_start + dot(attention_left_rows, full_attention, 1, 0))
    attention_parts = [
        low(dot(rows, full_attention, 1, 1)),
        low(dot(cols, full_attention, 0, 0)),
        low(dot(attention_product, attention_right_whole, 1, 0)),
        rows,
    ]
    attention_out = jnp.concatenate(
        [item.reshape(matrices, row_span, model_width) for item in attention_parts], axis=1
    )
    feed_sums = at.exchange_owners(
        jnp.concatenate(
            [
                feed_right.reshape(matrices, hidden_span, hidden_width),
                as_width(feed_left.reshape(matrices, row_span, model_width), hidden_width),
                as_width(attention_out, hidden_width),
            ],
            axis=1,
        )
    )
    left_rows = -(-row_span * model_width // hidden_width)
    attention_out = of_width(
        feed_sums[:, hidden_span + left_rows :], 4 * row_span, model_width
    )
    is_down = at.matrix == 2
    feed_pair = jnp.concatenate(
        [
            jnp.where(is_down, down_to_owners(feed_step.T), to_owners(moved)),
            jnp.where(is_down, down_to_owners(feed_cols), to_owners(feed_rows)),
            as_width(jnp.broadcast_to(low(small), (matrices,) + small.shape), hidden_width),
        ],
        axis=1,
    )
    feed_pair = at.exchange_owners(after(feed_pair, feed_sums))
    small = of_width(feed_pair[:, 2 * row_span :], small.shape[0], small.shape[1])
    small = jnp.sum(small.astype(jnp.float32), axis=0)
    sum_vectors = small[:-1]
    sum_table = small[-1, : grad_table.size].reshape(grad_table.shape)
    total_tokens = micro_rows * at.dp_size * tok_row
    small_rate = SMALL_RATE / math.sqrt(total_tokens)
    vector_momenta_new = MOMENTUM * vector_momenta + sum_vectors
    vectors_new = vectors - small_rate * vector_momenta_new
    table_momenta_new = MOMENTUM * table_momenta + sum_table
    table_new = bias_table - small_rate * table_momenta_new

    sum_left, sum_right, step, grads = [
        attention_out[:, i * row_span : (i + 1) * row_span].astype(jnp.float32) for i in range(4)
    ]

    def statistics(old, increment):
        return STAT_DECAY * old + (1.0 - STAT_DECAY) * increment

    attention_new = attention_weights - MATRIX_RATE * step
    attention_left_new = statistics(attention_left, sum_left)
    attention_right_new = statistics(attention_right, sum_right)
    attention_mom_new = MOMENTUM * attention_momenta + grads

    def wide(block):
        return block.astype(jnp.float32)

    step, grads = feed_pair[:, :row_span], feed_pair[:, row_span : 2 * row_span]
    sum_left = of_width(feed_sums[:, hidden_span : hidden_span + left_rows], row_span, model_width)
    expand_new = expand_weights - MATRIX_RATE * wide(step[:2])
    expand_left_new = statistics(expand_left, wide(sum_left[:2]))
    expand_right_new = statistics(expand_right, wide(feed_sums[:2, :hidden_span]))
    expand_mom_new = MOMENTUM * expand_momenta + wide(grads[:2])
    shrink_new = shrink_weights - MATRIX_RATE * wide(feed_to_down(step[2], model_width))
    shrink_left_new = statistics(down_left_statistics, wide(feed_sums[2, :hidden_span]))
    shrink_right_new = statistics(shrink_right, wide(sum_left[2]))
    shrink_mom_new = MOMENTUM * shrink_momenta + wide(feed_to_down(grads[2], model_width))
    return (
        layer_output,
        input_grads,
        vectors_new,
        vector_momenta_new,
        table_new,
        table_momenta_new,
        attention_new,
        attention_left_new,
        attention_right_new,
        attention_mom_new,
        low(attention_new),
        expand_new,
        expand_left_new,
        expand_right_new,
        expand_mom_new,
        low(expand_new),
        shrink_new,
        shrink_left_new,
        shrink_right_new,
        shrink_mom_new,
        low(shrink_new),
    )


def solution(mesh):
    row = P("dp", "seq", None)
    stack = P(None, BOTH, None)
    flat = P(BOTH, None)
    return jax.shard_map(
        per_device,
        mesh=mesh,
        in_specs=(row, P("dp", "seq"), P("dp"), P(), row)
        + (P(),) * 4
        + (stack,) * 12
        + (flat,) * 6,
        out_specs=(row, row) + (P(),) * 4 + (stack,) * 10 + (flat,) * 5,
        check_vma=False,
    )
```

```python
import functools
import math

import jax
import jax.numpy as jnp
from jax import lax
from jax.experimental import pallas as pl
from jax.experimental.pallas import tpu as pltpu
from jax.sharding import PartitionSpec as P

EPSILON = 1e-06
STAT_DECAY = 0.95
MOMENTUM = 0.9
MATRIX_RATE = 0.1
SMALL_RATE = 0.1
MASKED = -1e30
HIGH_PRECISION = lax.Precision.HIGHEST
BOTH = ("dp", "seq")


def fill_bias(brel_ref, bias_sc, heads, tile):
    span = brel_ref.shape[1]
    rows = lax.broadcasted_iota(jnp.int32, (8, span), 0)
    for h in range(heads):
        wide = jnp.broadcast_to(brel_ref[h:h + 1, :], (8, span))
        first = wide
        for i in range(8):
            first = jnp.where(rows == i, pltpu.roll(wide, span - (tile - 1) + i, 1), first)
        bias_sc[h, 0:8, :] = first
        size = 8
        while size < tile:
            bias_sc[h, size:2 * size, :] = pltpu.roll(bias_sc[h, 0:size, :], size, 1)
            size *= 2

def attn_fwd_kernel(heads, tile, qkv_ref, brel_ref, segc_ref, segr_ref, out_ref, outf_ref, lse_ref, bias_sc):
    step = pl.program_id(0)
    length = qkv_ref.shape[0]
    width = qkv_ref.shape[1] // 3
    dh = outf_ref.shape[1] // heads

    @pl.when(step == 0)
    def _():
        fill_bias(brel_ref, bias_sc, heads, tile)

    begin = pl.multiple_of(step * tile, tile)
    offset = pl.multiple_of(length - tile - begin, 128)
    same = segc_ref[...] == segr_ref[...]
    lanes = lax.broadcasted_iota(jnp.int32, (tile, 128), 1)
    lse_all = jnp.zeros((tile, 128), jnp.float32)
    outs = []
    for h in range(heads):
        q = qkv_ref[pl.ds(begin, tile), h * dh:(h + 1) * dh]
        k = qkv_ref[:, width + h * dh:width + (h + 1) * dh]
        v = qkv_ref[:, 2 * width + h * dh:2 * width + (h + 1) * dh]
        scores = lax.dot_general(q, k, (((1,), (1,)), ((), ())), preferred_element_type=jnp.float32)
        scores = jnp.where(same, scores + bias_sc[h, :, pl.ds(offset, length)], MASKED)
        top = jnp.max(scores, axis=1, keepdims=True)
        probs = jnp.exp(scores - top)
        total = jnp.sum(probs, axis=1, keepdims=True)
        out = lax.dot_general(probs.astype(jnp.bfloat16), v, (((1,), (0,)), ((), ())), preferred_element_type=jnp.float32)
        outs.append(out / total)
        lse_all = jnp.where(lanes == h, top + jnp.log(total), lse_all)
    joined = jnp.concatenate(outs, axis=1)
    outf_ref[...] = joined
    fill = out_ref.shape[1] - joined.shape[1]
    if fill:
        joined = jnp.concatenate([joined, jnp.zeros((tile, fill), jnp.float32)], axis=1)
    out_ref[...] = joined.astype(jnp.bfloat16)
    lse_ref[...] = lse_all

def attn_fwd(qkv, brel, segc, segr, heads, dh, tile=128):
    length = qkv.shape[0]
    width = heads * dh
    full = lambda s: pl.BlockSpec(s, lambda i: (0,) * len(s))
    rowb = lambda w: pl.BlockSpec((tile, w), lambda i: (i, 0))
    return pl.pallas_call(
        functools.partial(attn_fwd_kernel, heads, tile),
        grid=(length // tile,),
        in_specs=[full(qkv.shape), full(brel.shape), rowb(1), full(segr.shape)],
        out_specs=[rowb(qkv.shape[1] // 3), rowb(width), rowb(128)],
        out_shape=[jax.ShapeDtypeStruct((length, qkv.shape[1] // 3), jnp.bfloat16), jax.ShapeDtypeStruct((length, width), jnp.float32), jax.ShapeDtypeStruct((length, 128), jnp.float32)],
        scratch_shapes=[pltpu.VMEM((heads, tile, 2 * length), jnp.float32)],
        compiler_params=pltpu.CompilerParams(vmem_limit_bytes=48 * 2**20),
        cost_estimate=pl.CostEstimate(flops=4 * length * length * width, bytes_accessed=6 * length * width * 2, transcendentals=heads * length * length),
    )(qkv, brel, segc, segr)

def attn_bwd_kernel(heads, tile, trans, qkv_ref, grad_ref, outf_ref, lse_ref, brel_ref, segc_ref, segr_ref, dqkv_ref, gb_ref, bias_sc, gb_sc, dk_sc, dv_sc):
    step = pl.program_id(0)
    length = qkv_ref.shape[0]
    width = qkv_ref.shape[1] // 3
    dh = outf_ref.shape[1] // heads

    @pl.when(step == 0)
    def _():
        fill_bias(brel_ref, bias_sc, heads, tile)
        gb_sc[...] = jnp.zeros_like(gb_sc)
        dk_sc[...] = jnp.zeros_like(dk_sc)
        dv_sc[...] = jnp.zeros_like(dv_sc)

    begin = pl.multiple_of(step * tile, tile)
    offset = pl.multiple_of(length - tile - begin, 128)
    same = segc_ref[...] == segr_ref[...]
    dqs = []
    for h in range(heads):
        q = qkv_ref[pl.ds(begin, tile), h * dh:(h + 1) * dh]
        k = qkv_ref[:, width + h * dh:width + (h + 1) * dh]
        v = qkv_ref[:, 2 * width + h * dh:2 * width + (h + 1) * dh]
        g = grad_ref[:, h * dh:(h + 1) * dh]
        delta = jnp.sum(g.astype(jnp.float32) * outf_ref[:, h * dh:(h + 1) * dh], axis=1, keepdims=True)
        lse = lse_ref[:, h:h + 1]
        scores = lax.dot_general(q, k, (((1,), (1,)), ((), ())), preferred_element_type=jnp.float32)
        scores = jnp.where(same, scores + bias_sc[h, :, pl.ds(offset, length)], MASKED)
        probs = jnp.exp(scores - lse)
        gp = lax.dot_general(g, v, (((1,), (1,)), ((), ())), preferred_element_type=jnp.float32)
        gs = (probs * (gp - delta))
        gsb = gs.astype(jnp.bfloat16)
        pb = probs.astype(jnp.bfloat16)
        gb_sc[h, :, pl.ds(offset, length)] += gsb.astype(jnp.float32)
        dqs.append(lax.dot_general(gsb, k, (((1,), (0,)), ((), ())), preferred_element_type=jnp.float32))
        if trans:
            dk_sc[h] += lax.dot_general(q, gsb, (((0,), (0,)), ((), ())), preferred_element_type=jnp.float32)
            dv_sc[h] += lax.dot_general(g, pb, (((0,), (0,)), ((), ())), preferred_element_type=jnp.float32)
        else:
            dk_sc[h] += lax.dot_general(gsb, q, (((0,), (0,)), ((), ())), preferred_element_type=jnp.float32)
            dv_sc[h] += lax.dot_general(pb, g, (((0,), (0,)), ((), ())), preferred_element_type=jnp.float32)
    fill = width - heads * dh

    def slot(parts):
        rows = parts[0].shape[0]
        filled = parts + ([jnp.zeros((rows, fill), jnp.float32)] if fill else [])
        return jnp.concatenate(filled, axis=1).astype(jnp.bfloat16)

    dqkv_ref[pl.ds(begin, tile), 0:width] = slot(dqs)

    @pl.when(step == pl.num_programs(0) - 1)
    def _():
        turn = (lambda x: x.T) if trans else (lambda x: x)
        dqkv_ref[:, width:2 * width] = slot([turn(dk_sc[h]) for h in range(heads)])
        dqkv_ref[:, 2 * width:3 * width] = slot([turn(dv_sc[h]) for h in range(heads)])
        span = gb_sc.shape[2]
        rows = lax.broadcasted_iota(jnp.int32, (8, span), 0)
        for h in range(heads):
            size = tile // 2
            part = gb_sc[h]
            while size >= 8:
                part = part[:size] + pltpu.roll(part[size:], span - size, 1)
                size //= 2
            line = jnp.zeros((1, span), jnp.float32)
            for i in range(8):
                line = line + jnp.sum(jnp.where(rows == i, pltpu.roll(part, (tile - 1 - i) % span, 1), 0.0), axis=0, keepdims=True)
            gb_ref[h:h + 1, :] = line

def attn_bwd(qkv, grad, outf, lse, brel, segc, segr, heads, tile=128, trans=True):
    length, width = outf.shape
    dh = width // heads
    full = lambda s: pl.BlockSpec(s, lambda i: (0,) * len(s))
    rowb = lambda w: pl.BlockSpec((tile, w), lambda i: (i, 0))
    acc = (heads, dh, length) if trans else (heads, length, dh)
    return pl.pallas_call(
        functools.partial(attn_bwd_kernel, heads, tile, trans),
        grid=(length // tile,),
        in_specs=[full(qkv.shape), rowb(grad.shape[1]), rowb(width), rowb(128), full(brel.shape), rowb(1), full(segr.shape)],
        out_specs=[full(qkv.shape), full(brel.shape)],
        out_shape=[jax.ShapeDtypeStruct(qkv.shape, jnp.bfloat16), jax.ShapeDtypeStruct(brel.shape, jnp.float32)],
        scratch_shapes=[pltpu.VMEM((heads, tile, 2 * length), jnp.float32), pltpu.VMEM((heads, tile, 2 * length), jnp.float32), pltpu.VMEM(acc, jnp.float32), pltpu.VMEM(acc, jnp.float32)],
        compiler_params=pltpu.CompilerParams(vmem_limit_bytes=56 * 2**20),
        cost_estimate=pl.CostEstimate(flops=10 * length * length * width, bytes_accessed=12 * length * width * 2, transcendentals=heads * length * length),
    )(qkv, grad, outf, lse, brel, segc, segr)

def byte_window(bytes_ref, counts_ref, taps, begin, span, place, row_len):
    row = pl.program_id(0)
    positions = place + begin + lax.broadcasted_iota(jnp.int32, (span, 1), 0)
    window = bytes_ref[0, pl.ds(begin, span), :].astype(jnp.float32)
    valid = (positions >= 0) & (positions < counts_ref[row])
    embedded = jnp.where(valid, window, 0.0)
    conv = embedded * taps[3:4]
    for tap in range(3):
        conv = conv + pltpu.roll(embedded, 3 - tap, 0) * taps[tap : tap + 1]
    conv = jnp.where(positions < row_len, conv, 0.0)
    return positions, embedded, conv


def block_sums(values, positions, span):
    ahead = [None] + [pltpu.roll(values, span - i, 0) for i in (1, 2)]
    behind = [None] + [pltpu.roll(values, i, 0) for i in (1, 2)]
    two = values + jnp.where(positions % 2 == 0, ahead[1], behind[1])
    four = two + jnp.where(
        positions % 4 < 2, pltpu.roll(two, span - 2, 0), pltpu.roll(two, 2, 0)
    )
    phase = (positions + 9) % 3
    three = (
        values
        + jnp.where(phase != 2, ahead[1], behind[2])
        + jnp.where(phase == 0, ahead[2], behind[1])
    )
    return two, three, four


def three_sum(values, positions, span):
    phase = (positions + 9) % 3
    return (
        values
        + jnp.where(phase != 2, pltpu.roll(values, span - 1, 0), pltpu.roll(values, 2, 0))
        + jnp.where(phase == 0, pltpu.roll(values, span - 2, 0), pltpu.roll(values, 1, 0))
    )


def three_share(positions, row_len):
    left = row_len - (positions - (positions + 9) % 3)
    return jnp.where(left >= 3, 1.0 / 3.0, jnp.where(left == 2, 0.5, 1.0))


def block_means(conv, positions, span, row_len):
    two, three, four = block_sums(conv, positions, span)
    return [conv, two * 0.5, three * three_share(positions, row_len), four * 0.25]


def size_softmax(pooled, score_row):
    scores = [jnp.sum(item * score_row, axis=1, keepdims=True) for item in pooled]
    top = functools.reduce(jnp.maximum, scores)
    powers = [jnp.exp(item - top) for item in scores]
    total = sum(powers)
    return [item / total for item in powers]


def tokens_kernel(row_len, halo, chunk, counts_ref, place_ref, bytes_ref, vectors_ref, tokens_ref, normed_ref, pair_ref):
    span = chunk + 2 * halo
    taps = vectors_ref[0:4, :]

    def visit(index, carry):
        begin = pl.multiple_of(index * chunk, chunk)
        positions, embedded, conv = byte_window(
            bytes_ref, counts_ref, taps, begin, span, place_ref[0], row_len
        )
        pooled = block_means(conv, positions, span, row_len)
        pooled = [item[halo : halo + chunk] for item in pooled]
        weights = size_softmax(pooled, vectors_ref[4:5, :])
        blended = sum(weight * item for weight, item in zip(weights, pooled))
        half = chunk // 2
        halves = []
        for lane in range(pair_ref.shape[0]):
            pair_ref[lane] = blended[:, lane * 128 : (lane + 1) * 128]
            halves.append(
                pair_ref[lane, pl.Slice(0, half, 2), :] + pair_ref[lane, pl.Slice(1, half, 2), :]
            )
        tokens = 0.5 * jnp.concatenate(halves, axis=1)
        factor = lax.rsqrt(jnp.mean(tokens * tokens, axis=1, keepdims=True) + EPSILON)
        rows = pl.ds(pl.multiple_of(index * half, half), half)
        tokens_ref[rows, :] = tokens
        normed_ref[rows, :] = (tokens * factor * vectors_ref[5:6, :]).astype(jnp.bfloat16)
        return carry

    lax.fori_loop(0, (bytes_ref.shape[1] - 2 * halo) // chunk, visit, 0)


def make_tokens(counts, place, wide_bytes, vectors, row_len, halo=8, chunk=64):
    micro, wide, width = wide_bytes.shape
    count = (wide - 2 * halo) // 2
    return pl.pallas_call(
        functools.partial(tokens_kernel, row_len, halo, chunk),
        grid=(micro,),
        in_specs=[
            pl.BlockSpec(memory_space=pltpu.SMEM),
            pl.BlockSpec(memory_space=pltpu.SMEM),
            pl.BlockSpec((1, wide, width), lambda i: (i, 0, 0)),
            pl.BlockSpec(vectors.shape, lambda i: (0, 0)),
        ],
        out_specs=[pl.BlockSpec((count, width), lambda i: (i, 0))] * 2,
        out_shape=[
            jax.ShapeDtypeStruct((micro * count, width), jnp.float32),
            jax.ShapeDtypeStruct((micro * count, width), jnp.bfloat16),
        ],
        scratch_shapes=[pltpu.VMEM((width // 128, chunk, 128), jnp.float32)],
        compiler_params=pltpu.CompilerParams(vmem_limit_bytes=32 * 2**20),
        cost_estimate=pl.CostEstimate(
            flops=60 * micro * wide * width, bytes_accessed=6 * micro * wide * width, transcendentals=0
        ),
    )(counts, place, wide_bytes, vectors)


def bytes_kernel(row_len, halo, chunk, counts_ref, place_ref, bytes_ref, grads_ref, vectors_ref, out_ref, sums_ref, spread_ref, parts_ref):
    row = pl.program_id(0)
    span = chunk + 2 * halo
    taps = vectors_ref[0:4, :]
    score_row = vectors_ref[4:5, :]
    half = grads_ref.shape[1]
    for lane in range(spread_ref.shape[0]):
        lanes = grads_ref[0, :, lane * 128 : (lane + 1) * 128] * 0.5
        spread_ref[lane, pl.Slice(0, half, 2), :] = lanes
        spread_ref[lane, pl.Slice(1, half, 2), :] = lanes

    @pl.when(row == 0)
    def _():
        parts_ref[...] = jnp.zeros_like(parts_ref)

    def visit(index, carry):
        begin = pl.multiple_of(index * chunk, chunk)
        positions, embedded, conv = byte_window(
            bytes_ref, counts_ref, taps, begin, span, place_ref[0], row_len
        )
        pooled = block_means(conv, positions, span, row_len)
        weights = size_softmax(pooled, score_row)
        grad = jnp.concatenate(
            [spread_ref[lane, pl.ds(begin, span), :] for lane in range(spread_ref.shape[0])], axis=1
        )
        along = [jnp.sum(grad * item, axis=1, keepdims=True) for item in pooled]
        mean = sum(weight * item for weight, item in zip(weights, along))
        sizes = [weight * (item - mean) for weight, item in zip(weights, along)]
        first, second, third, fourth = [
            weight * grad + size * score_row for weight, size in zip(weights, sizes)
        ]
        even = positions % 2 == 0
        pair = 0.5 * second + 0.25 * fourth
        fours = 0.25 * fourth
        pair = pair + jnp.where(even, pltpu.roll(pair, span - 1, 0), pltpu.roll(pair, 1, 0))
        fours = fours + jnp.where(even, pltpu.roll(fours, span - 1, 0), pltpu.roll(fours, 1, 0))
        fours = jnp.where(
            positions % 4 < 2, pltpu.roll(fours, span - 2, 0), pltpu.roll(fours, 2, 0)
        )
        share = three_share(positions, row_len)
        grad_conv = first + pair + fours + three_sum(third, positions, span) * share
        grad_conv = jnp.where((positions < row_len) & (positions >= 0), grad_conv, 0.0)
        back = grad_conv * taps[3:4]
        for tap in range(3):
            back = back + pltpu.roll(grad_conv, span - (3 - tap), 0) * taps[tap : tap + 1]
        own = slice(halo, halo + chunk)
        back = jnp.where(positions < counts_ref[row], back, 0.0)
        out_ref[0, pl.ds(begin, chunk), :] = back[own]

        def fold(values):
            return jnp.sum(values.reshape(chunk // 8, 8, values.shape[1]), axis=0)

        for tap in range(4):
            beside = embedded if tap == 3 else pltpu.roll(embedded, 3 - tap, 0)
            parts_ref[tap] += fold((grad_conv * beside)[own])
        parts_ref[4] += fold(sum(size * item for size, item in zip(sizes, pooled))[own])
        return carry

    lax.fori_loop(0, (bytes_ref.shape[1] - 2 * halo) // chunk, visit, 0)

    @pl.when(row == pl.num_programs(0) - 1)
    def _():
        sums_ref[...] = jnp.zeros_like(sums_ref)
        for item in range(5):
            sums_ref[item : item + 1, :] = jnp.sum(parts_ref[item], axis=0, keepdims=True)


def bytes_back(counts, place, wide_bytes, wide_grads, vectors, row_len, halo=8, chunk=64):
    micro, wide, width = wide_bytes.shape
    count = wide - 2 * halo
    return pl.pallas_call(
        functools.partial(bytes_kernel, row_len, halo, chunk),
        grid=(micro,),
        in_specs=[
            pl.BlockSpec(memory_space=pltpu.SMEM),
            pl.BlockSpec(memory_space=pltpu.SMEM),
            pl.BlockSpec((1, wide, width), lambda i: (i, 0, 0)),
            pl.BlockSpec((1, wide // 2, width), lambda i: (i, 0, 0)),
            pl.BlockSpec(vectors.shape, lambda i: (0, 0)),
        ],
        out_specs=[
            pl.BlockSpec((1, count, width), lambda i: (i, 0, 0)),
            pl.BlockSpec((8, width), lambda i: (0, 0)),
        ],
        out_shape=[
            jax.ShapeDtypeStruct((micro, count, width), jnp.float32),
            jax.ShapeDtypeStruct((8, width), jnp.float32),
        ],
        scratch_shapes=[
            pltpu.VMEM((width // 128, wide, 128), jnp.float32),
            pltpu.VMEM((5, 8, width), jnp.float32),
        ],
        compiler_params=pltpu.CompilerParams(vmem_limit_bytes=32 * 2**20),
        cost_estimate=pl.CostEstimate(
            flops=150 * micro * wide * width, bytes_accessed=8 * micro * wide * width, transcendentals=0
        ),
    )(counts, place, wide_bytes, wide_grads, vectors)

def low(values):
    return values.astype(jnp.bfloat16)


def dot(left_side, right_side, left_dim, right_dim):
    return lax.dot_general(
        left_side,
        right_side,
        (((left_dim,), (right_dim,)), ((), ())),
        preferred_element_type=jnp.float32,
    )


def rms_factor(values):
    return lax.rsqrt(jnp.mean(values * values, axis=-1, keepdims=True) + EPSILON)


def norm_back(values, factor, gain_row, grad_out):
    scaled = grad_out * gain_row
    grad_gain = jnp.sum(grad_out * values * factor, axis=0)
    inner_mean = jnp.mean(scaled * values, axis=-1, keepdims=True)
    return (factor * (scaled - values * inner_mean * factor * factor), grad_gain)


def feed_kernel(parts, place_ref, *refs):
    pieces = refs[:parts]
    right_ref, start_ref, left_ref = refs[parts : parts + 3]
    sum_right_ref, sum_left_ref, step_ref, step_t_ref, cols_ref, rows_ref = refs[parts + 3 : -1]
    whole_ref = refs[-1]
    width = pieces[0].shape[1]
    for key, piece in enumerate(pieces):
        begin = pl.multiple_of((place_ref[0] ^ key) * width, width)
        whole_ref[:, pl.ds(begin, width)] = piece[...]
    member = place_ref[1]
    count = cols_ref.shape[0]
    cols = whole_ref[:, pl.ds(pl.multiple_of(member * count, count), count)].T
    cols_ref[...] = cols
    count = rows_ref.shape[0]
    rows = whole_ref[pl.ds(pl.multiple_of(member * count, count), count), :]
    rows_ref[...] = rows
    product = start_ref[...]
    for begin in range(0, whole_ref.shape[1], width):
        block = whole_ref[:, begin : begin + width]
        sum_right_ref[:, begin : begin + width] = lax.dot_general(
            cols, block, (((1,), (0,)), ((), ())), preferred_element_type=jnp.float32
        ).astype(jnp.bfloat16)
        product = product + lax.dot_general(
            block,
            right_ref[:, begin : begin + width],
            (((1,), (1,)), ((), ())),
            preferred_element_type=jnp.float32,
        )
    sum_left_ref[...] = lax.dot_general(
        rows, whole_ref[...], (((1,), (1,)), ((), ())), preferred_element_type=jnp.float32
    ).astype(jnp.bfloat16)
    step = lax.dot_general(
        left_ref[...],
        product.astype(jnp.bfloat16),
        (((1,), (0,)), ((), ())),
        preferred_element_type=jnp.float32,
    )
    step_ref[...] = step.astype(jnp.bfloat16)
    step_t_ref[...] = step.T.astype(jnp.bfloat16)


def feed_update(place, pieces, right_rows, start, left_whole, member_rows):
    rows, width = pieces[0].shape
    cols = right_rows.shape[0]
    total = width * len(pieces)
    vmem = pl.BlockSpec(memory_space=pltpu.VMEM)
    shapes = [(cols, total), (member_rows, rows), (rows, cols), (cols, rows), (cols, rows)]
    shapes.append((member_rows, total))
    return pl.pallas_call(
        functools.partial(feed_kernel, len(pieces)),
        in_specs=[pl.BlockSpec(memory_space=pltpu.SMEM)] + [vmem] * (len(pieces) + 3),
        out_specs=[vmem] * len(shapes),
        out_shape=[jax.ShapeDtypeStruct(shape, jnp.bfloat16) for shape in shapes],
        scratch_shapes=[pltpu.VMEM((rows, total), jnp.bfloat16)],
        compiler_params=pltpu.CompilerParams(vmem_limit_bytes=48 * 2**20),
        cost_estimate=pl.CostEstimate(
            flops=4 * rows * total * cols, bytes_accessed=6 * rows * total, transcendentals=0
        ),
    )(place, *pieces, right_rows, start, left_whole)


def attention_kernel(member_ref, whole_ref, left_ref, start_ref, right_ref, out_ref, square_ref):
    count = left_ref.shape[0]
    mine = pl.ds(pl.multiple_of(member_ref[0] * count, count), count)
    whole = whole_ref[...]
    rows = whole_ref[mine, :]
    out_ref[0] = lax.dot_general(
        rows, whole, (((1,), (1,)), ((), ())), preferred_element_type=jnp.float32
    ).astype(jnp.bfloat16)
    square_ref[...] = lax.dot_general(
        whole, whole, (((0,), (0,)), ((), ())), preferred_element_type=jnp.float32
    )
    out_ref[1] = square_ref[mine, :].astype(jnp.bfloat16)
    product = start_ref[...] + lax.dot_general(
        left_ref[...], whole, (((1,), (0,)), ((), ())), preferred_element_type=jnp.float32
    )
    out_ref[2] = lax.dot_general(
        product.astype(jnp.bfloat16),
        right_ref[...],
        (((1,), (0,)), ((), ())),
        preferred_element_type=jnp.float32,
    ).astype(jnp.bfloat16)
    out_ref[3] = rows


def attention_update(member, whole, left_rows, start, right_whole):
    count, width = left_rows.shape
    vmem = pl.BlockSpec(memory_space=pltpu.VMEM)
    return pl.pallas_call(
        attention_kernel,
        in_specs=[pl.BlockSpec(memory_space=pltpu.SMEM)] + [vmem] * 4,
        out_specs=vmem,
        out_shape=jax.ShapeDtypeStruct((4, count, width), jnp.bfloat16),
        scratch_shapes=[pltpu.VMEM((width, width), jnp.float32)],
        compiler_params=pltpu.CompilerParams(vmem_limit_bytes=32 * 2**20),
        cost_estimate=pl.CostEstimate(
            flops=2 * width**3, bytes_accessed=6 * width * width, transcendentals=0
        ),
    )(member, whole, left_rows, start, right_whole)


class Layout:
    def __init__(self, head_count, micro_rows):
        self.dp_size = lax.axis_size("dp")
        self.seq_size = lax.axis_size("seq")
        self.count = self.dp_size * self.seq_size
        self.dp = lax.axis_index("dp")
        self.seq = lax.axis_index("seq")
        self.micro = micro_rows
        self.parts = math.gcd(self.dp_size, head_count & -head_count)
        self.groups = self.dp_size // self.parts
        self.part = self.dp % self.parts
        self.head_groups = head_count & -head_count
        self.repeat = self.seq_size // (micro_rows * self.head_groups)
        self.unit = self.seq // self.repeat
        self.matrices = 4
        self.sides = self.seq_size // self.matrices
        self.matrix = self.seq % self.matrices
        self.side = self.seq // self.matrices
        self.member = self.dp * self.sides + self.side
        self.members = [
            [
                (group * self.parts + part) * self.seq_size + side * self.matrices + matrix
                for part in range(self.parts)
                for side in range(self.sides)
            ]
            for group in range(self.groups)
            for matrix in range(self.matrices)
        ]
        self.holders = [
            [
                dp * self.seq_size + side * self.matrices + matrix
                for dp in range(self.dp_size)
                for side in range(self.sides)
            ]
            for matrix in range(self.matrices)
        ]
        self.owners = [
            [side * self.matrices + matrix for matrix in range(self.matrices)]
            for side in range(self.sides)
        ]

    def flip(self, block, axis, bits):
        size = lax.axis_size(axis)
        return lax.ppermute(block, axis, [(i, i ^ bits) for i in range(size)])

    def gather_parts(self, block):
        pieces = {0: block}
        bit = self.parts // 2
        while bit:
            for key in list(pieces):
                pieces[key | bit] = self.flip(pieces[key], "dp", bit)
            bit //= 2
        whole = jnp.zeros((self.parts,) + block.shape, block.dtype)
        for key, piece in pieces.items():
            whole = lax.dynamic_update_index_in_dim(whole, piece, self.part ^ key, 0)
        return whole

    def scatter_step(self, blocks, axis, index, bit):
        pairs = blocks.reshape((blocks.shape[0] // 2, 2) + blocks.shape[1:])
        mine = (index // bit) % 2
        kept = lax.dynamic_index_in_dim(pairs, mine, 1, False)
        sent = lax.dynamic_index_in_dim(pairs, 1 - mine, 1, False)
        got = self.flip(low(sent), axis, bit)
        return low(kept.astype(jnp.float32) + got.astype(jnp.float32))

    def scatter(self, blocks, axis, index):
        bit = 1
        while blocks.shape[0] > 1:
            blocks = self.scatter_step(blocks, axis, index, bit)
            bit *= 2
        return blocks[0]

    def near_parts(self, block):
        pieces = {0: block}
        bit = self.parts // 2
        while bit:
            for key in list(pieces):
                pieces[key | bit] = self.flip(pieces[key], "dp", bit)
            bit //= 2
        return jnp.concatenate([pieces[key] for key in range(self.parts)], axis=0)

    def scatter_near(self, rows):
        blocks = rows.reshape((self.parts, -1) + rows.shape[1:])
        bit = 1
        while blocks.shape[0] > 1:
            pairs = blocks.reshape((blocks.shape[0] // 2, 2) + blocks.shape[1:])
            got = self.flip(low(pairs[:, 1]), "dp", bit)
            blocks = pairs[:, 0].astype(jnp.float32) + got.astype(jnp.float32)
            bit *= 2
        return blocks[0]

    def scatter_heads(self, blocks):
        index, bit = self.unit % self.head_groups, 1
        while blocks.shape[0] > 1:
            pairs = blocks.reshape((blocks.shape[0] // 2, 2) + blocks.shape[1:])
            mine = (index // bit) % 2
            kept = lax.dynamic_index_in_dim(pairs, mine, 1, False)
            sent = lax.dynamic_index_in_dim(pairs, 1 - mine, 1, False)
            got = self.flip(low(sent), "seq", bit * self.repeat)
            blocks = kept.astype(jnp.float32) + got.astype(jnp.float32)
            bit *= 2
        return blocks[0]

    def sum_groups(self, block):
        total = block
        for shift in range(1, self.groups):
            turn = [(i, (i + shift * self.parts) % self.dp_size) for i in range(self.dp_size)]
            total = total + lax.ppermute(low(block), "dp", turn).astype(jnp.float32)
        return total

    def to_units(self, blocks):
        shape = blocks.shape
        blocks = blocks[:, :, None]
        if self.repeat > 1:
            blocks = jnp.broadcast_to(blocks, shape[:2] + (self.repeat,) + shape[2:])
        return self.exchange(blocks.reshape((self.seq_size,) + shape[2:]))

    def exchange(self, blocks):
        return lax.all_to_all(blocks, "seq", 0, 0, tiled=True)

    def gather_step(self, pieces, bit, axis="seq"):
        grown = []
        for held in pieces:
            keys = sorted(held)
            moved = self.flip(jnp.stack([held[key] for key in keys]), axis, bit)
            held = dict(held)
            for place, key in enumerate(keys):
                held[key | bit] = moved[place]
            grown.append(held)
        return grown

    def gathered(self, held, index):
        whole = jnp.zeros((len(held),) + held[0].shape, held[0].dtype)
        for key, piece in held.items():
            whole = lax.dynamic_update_index_in_dim(whole, piece, index ^ key, 0)
        return whole

    def by_halves(self):
        return self.repeat == 1 and self.micro == 2 and self.head_groups == 4

    def rows_to_units(self, blocks, beside):
        held = [{0: item} for item in beside]
        bits = [1 << i for i in reversed(range(self.parts.bit_length() - 1))]
        if not self.by_halves():
            shape = blocks.shape
            blocks = jnp.broadcast_to(blocks[:, None], shape[:1] + (self.head_groups,) + shape[1:])
            whole = self.to_units(blocks)
            for bit in bits:
                held = self.gather_step(held, bit, "dp")
            return whole.reshape((-1,) + shape[2:]), held
        mine = self.unit // self.head_groups
        near = lax.dynamic_index_in_dim(blocks, mine, 0, False)
        far = self.flip(lax.dynamic_index_in_dim(blocks, 1 - mine, 0, False), "seq", 4)
        near_one = self.flip(near, "seq", 1)
        far, held = lax.optimization_barrier((far, held))
        far_two = self.flip(far, "seq", 2)
        for bit in bits[:1]:
            held = self.gather_step(held, bit, "dp")
        near_one, far_two = lax.optimization_barrier((near_one, far_two))
        near_two = self.flip(jnp.stack([near, near_one]), "seq", 2)
        far_one = self.flip(jnp.stack([far, far_two]), "seq", 1)
        near_two, far_one, held = lax.optimization_barrier((near_two, far_one, held))
        for bit in bits[1:]:
            held = self.gather_step(held, bit, "dp")
        pieces = [near, near_one, near_two[0], near_two[1], far, far_one[0], far_two, far_one[1]]
        whole = self.gathered(dict(enumerate(pieces)), self.seq)
        return whole.reshape((-1,) + blocks.shape[2:]), held

    def fold_units(self, row):
        blocks = row.reshape((self.seq_size, -1) + row.shape[1:])
        if not self.by_halves():
            return self.exchange(low(blocks))

        def pick(*keys):
            picked = [
                lax.dynamic_index_in_dim(blocks, self.seq ^ key, 0, False).astype(jnp.float32)
                for key in keys
            ]
            return jnp.stack(picked)

        near = pick(0, 1) + self.flip(low(pick(2, 3)), "seq", 2).astype(jnp.float32)
        far = pick(4, 6) + self.flip(low(pick(5, 7)), "seq", 1).astype(jnp.float32)
        return (near, far)

    def fold_halves(self, folded):
        if not self.by_halves():
            return folded
        near, far = folded
        near = near[0] + self.flip(low(near[1]), "seq", 1).astype(jnp.float32)
        far = far[0] + self.flip(low(far[1]), "seq", 2).astype(jnp.float32)
        return (near, far)

    def fold_rows(self, folded):
        if not self.by_halves():
            blocks = folded.astype(jnp.float32)
            return jnp.sum(blocks.reshape((self.micro, -1) + blocks.shape[1:]), axis=1)
        near, far = folded
        far = self.flip(low(far), "seq", 4).astype(jnp.float32)
        first = self.unit // self.head_groups == 0
        return jnp.stack([jnp.where(first, near, far), jnp.where(first, far, near)])

    def gather_members(self, block):
        whole = lax.all_gather(block, BOTH, axis=0, axis_index_groups=self.members)
        return whole.reshape((self.parts, self.sides) + block.shape)

    def spread_members(self, block):
        count = self.parts * self.sides
        blocks = jnp.broadcast_to(block[None], (count,) + block.shape)
        return lax.all_to_all(blocks, BOTH, 0, 0, tiled=True, axis_index_groups=self.members)

    def gather_holders(self, block):
        return lax.all_gather(block, BOTH, axis=0, axis_index_groups=self.holders, tiled=True)

    def exchange_holders(self, blocks):
        return lax.all_to_all(blocks, BOTH, 0, 0, tiled=True, axis_index_groups=self.holders)

    def exchange_owners(self, blocks):
        return lax.all_to_all(blocks, "seq", 0, 0, tiled=True, axis_index_groups=self.owners)


def after(value, token):
    return lax.optimization_barrier((value, token))[0]


def as_width(blocks, width):
    flat = blocks.reshape(blocks.shape[0], -1)
    short = -flat.shape[1] % width
    return jnp.pad(flat, ((0, 0), (0, short))).reshape(blocks.shape[0], -1, width)


def down_to_feed(blocks, width, lanes=256):
    lead, (rows, columns) = blocks.shape[:-2], blocks.shape[-2:]
    groups, parts = width // lanes, columns // lanes
    count = len(lead)
    blocks = blocks.reshape(lead + (groups, rows // groups, parts, lanes))
    order = tuple(range(count)) + (count + 2, count + 1, count, count + 3)
    return jnp.transpose(blocks, order).reshape(lead + (parts * rows // groups, width))


def feed_to_down(blocks, columns, lanes=256):
    lead, (rows, width) = blocks.shape[:-2], blocks.shape[-2:]
    groups, parts = width // lanes, columns // lanes
    count = len(lead)
    blocks = blocks.reshape(lead + (parts, rows // parts, groups, lanes))
    order = tuple(range(count)) + (count + 2, count + 1, count, count + 3)
    return jnp.transpose(blocks, order).reshape(lead + (groups * rows // parts, columns))


def of_width(blocks, rows, columns):
    flat = blocks.reshape(blocks.shape[0], -1)
    return flat[:, : rows * columns].reshape(blocks.shape[0], rows, columns)


def gather_all(block):
    return lax.all_gather(block, BOTH, axis=0, tiled=True)


def per_device(
    byte_rows,
    segments,
    counts,
    buckets,
    cotangent,
    vectors,
    vector_momenta,
    bias_table,
    table_momenta,
    attention_weights,
    attention_left,
    attention_right,
    attention_left_root,
    attention_right_root,
    attention_momenta,
    expand_weights,
    expand_left,
    expand_right,
    expand_left_root,
    expand_right_root,
    expand_momenta,
    shrink_weights,
    down_left_statistics,
    shrink_right,
    shrink_left_root,
    shrink_right_root,
    shrink_momenta,
):
    micro_rows, width_bytes, model_width = byte_rows.shape
    head_count = bias_table.shape[1]
    at = Layout(head_count, micro_rows)
    parts, part, seq_size, sequence_position = at.parts, at.part, at.seq_size, at.seq
    row_len = width_bytes * seq_size
    tok_local = width_bytes // 2
    tok_row = row_len // 2
    hidden_width = shrink_weights.shape[1 - 1] * at.count
    heads = head_count // parts
    head_width = model_width // parts
    hidden_part = hidden_width // parts

    row_span = model_width // at.count
    hidden_span = hidden_width // at.count
    dp_size, sides, matrices = at.dp_size, at.sides, at.matrices

    slot = -(-head_width // 128) * 128
    slot_fill = ((0, 0), (0, 0), (0, 0), (0, slot - head_width))
    split = low(attention_weights[:3]).reshape(3, row_span, at.head_groups, head_width)
    split = jnp.pad(jnp.transpose(split, (2, 1, 0, 3)), slot_fill).reshape(
        at.head_groups, row_span, 3 * slot
    )
    token_segs = segments[:, 0::2]
    digits = jnp.stack([token_segs // 64, token_segs % 64], axis=1).astype(jnp.bfloat16)
    digits = jnp.pad(digits, ((0, 0), (0, row_span - 2), (0, 0)))
    split = jnp.concatenate(
        [
            jnp.broadcast_to(split[None], (micro_rows,) + split.shape),
            jnp.broadcast_to(
                low(attention_weights[3]), (micro_rows, at.head_groups, row_span, model_width)
            ),
            jnp.broadcast_to(
                digits[:, None], (micro_rows, at.head_groups, row_span, tok_local)
            ),
        ],
        axis=3,
    )
    split = at.to_units(split)

    halo = 8
    count = at.seq_size
    forward = [(i, i + 1) for i in range(count - 1)]
    backward = [(i + 1, i) for i in range(count - 1)]
    wide_bytes = jnp.concatenate(
        [
            lax.ppermute(byte_rows[:, width_bytes - halo :], "seq", forward),
            byte_rows,
            lax.ppermute(byte_rows[:, :halo], "seq", backward),
        ],
        axis=1,
    )
    place = (sequence_position * width_bytes - halo).reshape(1)
    tokens, normed = make_tokens(counts, place, wide_bytes, vectors, row_len, halo)
    grad_rows_out = cotangent.reshape(-1, model_width)

    (
        expand_weights_in,
        shrink_weights_in,
        normed,
    ) = lax.optimization_barrier(
        (expand_weights, shrink_weights, normed)
    )
    def columns(whole, begin, width):
        return lax.dynamic_slice_in_dim(whole, begin, width, 1)

    if at.groups == 1:
        rest = low(expand_weights_in).reshape(2, row_span, parts, hidden_part)
        rest = jnp.transpose(rest, (2, 1, 0, 3)).reshape(parts, row_span, 2 * hidden_part)
        rest = lax.all_to_all(after(rest, split), "dp", 0, 0, tiled=True)
        bits = [1 << i for i in reversed(range(seq_size.bit_length() - 1))]
        rest = [{0: item} for item in (rest, low(shrink_weights_in))]
        rest = at.gather_step(rest, bits[0])
    else:
        rest = jnp.concatenate(
            [low(expand_weights_in[0]), low(expand_weights_in[1])]
            + [low(shrink_weights_in).reshape(row_span, hidden_width)],
            axis=1,
        )
        rest = gather_all(rest)
        weights_expand = jnp.concatenate(
            [
                columns(rest, i * hidden_width + part * hidden_part, hidden_part)
                for i in range(2)
            ],
            axis=1,
        )
        weights_shrink = lax.dynamic_slice(
            rest,
            (part * (model_width // parts), 2 * hidden_width),
            (model_width // parts, hidden_width),
        ).reshape(hidden_part, model_width)

    digits = split[:, :2, 3 * slot + model_width :].astype(jnp.int32)
    seg_row = (digits[:, 0] * 64 + digits[:, 1]).reshape(tok_row)
    split = split[:, :, : 3 * slot + model_width].reshape(
        seq_size * row_span, 3 * slot + model_width
    )
    def early_block(i):
        if i == 2:
            feed = [down_to_feed(low(shrink_momenta), hidden_width), low(shrink_right_root)]
        elif i < 2:
            feed = [low(expand_momenta[i]), low(expand_left_root[i])]
        else:
            feed = [jnp.zeros((row_span, hidden_width + model_width), jnp.bfloat16)]
        return jnp.concatenate(
            feed + [low(attention_momenta[i]), low(attention_right_root[i])], axis=1
        )

    early = jnp.stack([early_block(i) for i in range(matrices)])
    early_width = early.shape[2]

    early = at.exchange_owners(after(early, split)).reshape(-1, early_width)
    factor_one = rms_factor(tokens)

    normed_row, held = at.rows_to_units(
        normed.reshape(micro_rows, tok_local, model_width), [split, grad_rows_out]
    )
    grad_rows_all = jnp.concatenate([held[1][key] for key in range(parts)], axis=0)
    if at.groups == 1:
        weights_qkv = at.gathered(held[0], part)
    else:
        weights_qkv = lax.all_gather(split, "dp", axis=0)
    weights_qkv = weights_qkv.reshape(model_width, 3 * slot + model_width)
    weights_qkv, weights_out = weights_qkv[:, : 3 * slot], weights_qkv[:, 3 * slot :]
    weights_out = jnp.pad(
        weights_out.reshape(at.head_groups, head_width, model_width),
        ((0, 0), (0, slot - head_width), (0, 0)),
    ).reshape(-1, model_width)
    qkv_row = low(dot(normed_row, weights_qkv, 1, 0))
    qkv_row, grad_rows_all, early = lax.optimization_barrier((qkv_row, grad_rows_all, early))
    early = at.gather_holders(early)
    if at.groups == 1:
        rest, qkv_row = lax.optimization_barrier((rest, qkv_row))
        for bit in bits[1:-1]:
            rest = at.gather_step(rest, bit)
    onehot = (buckets[:, None] == jnp.arange(bias_table.shape[0], dtype=jnp.int32)[None, :]).astype(
        jnp.float32
    )
    head_begin = (at.unit % at.head_groups) * heads
    part_table = lax.dynamic_slice_in_dim(bias_table, head_begin, heads, 1)
    bias_rel = jnp.einsum("xb,bh->hx", onehot, part_table, precision=HIGH_PRECISION)
    bias_rel = jnp.pad(bias_rel, ((0, 0), (0, 1)))
    seg_col = seg_row[:, None]
    seg_line = seg_row[None, :]
    tile = min(256, tok_row)
    attended_row, attended_f32, log_totals = attn_fwd(
        qkv_row, bias_rel, seg_col, seg_line, heads, head_width // heads, tile
    )
    if at.groups == 1:
        rest, attended_row = lax.optimization_barrier((rest, attended_row))
        rest = at.gather_step(rest, bits[-1])
    roots_in = after((expand_right_root, shrink_left_root, attention_left_root), normed_row)
    roots = jnp.stack(
        [low(roots_in[0][0]), low(roots_in[0][1]), low(roots_in[1])]
        + [jnp.zeros(shrink_left_root.shape, jnp.bfloat16)]
    )
    lefts = jnp.pad(
        low(roots_in[2]), ((0, 0), (0, 0), (0, hidden_width - model_width))
    )
    roots = at.exchange_owners(after(jnp.concatenate([roots, lefts], axis=1), attended_row))
    attended = at.exchange(attended_row.reshape(seq_size, tok_local, slot))
    attended = attended.reshape(
        micro_rows, at.head_groups, at.repeat, tok_local, slot
    )[:, :, 0]
    attended = jnp.transpose(attended, (0, 2, 1, 3)).reshape(micro_rows * tok_local, -1)
    resid = tokens + dot(attended, weights_out, 1, 0)
    factor_two = rms_factor(resid)
    normed_two = low(resid * factor_two * vectors[6])

    normed_two_all = at.near_parts(normed_two)
    if at.groups == 1:
        rest, normed_two_all = lax.optimization_barrier((rest, normed_two_all))
        weights_shrink = at.gathered(rest[1], at.seq).reshape(hidden_part, model_width)
        weights_expand = jnp.transpose(at.gathered(rest[0], at.seq), (1, 0, 2, 3)).reshape(model_width, -1)
    expanded = dot(normed_two_all, weights_expand, 1, 0)
    gate_pre = expanded[:, :hidden_part]
    upward = expanded[:, hidden_part:]
    activated, gelu_back = jax.vjp(functools.partial(jax.nn.gelu, approximate=True), gate_pre)
    hidden = low(activated * upward)
    grad_hidden = dot(grad_rows_all, weights_shrink, 1, 1)
    grad_gate_pre = low(gelu_back(grad_hidden * upward)[0])
    grad_upward = low(grad_hidden * activated)
    grad_normed_two = at.scatter_near(
        dot(grad_gate_pre, weights_expand[:, :hidden_part], 1, 1)
        + dot(grad_upward, weights_expand[:, hidden_part:], 1, 1)
    )
    grad_shrink_t = dot(grad_rows_all, hidden, 0, 0)
    grad_gate_w = dot(normed_two_all, grad_gate_pre, 0, 0)
    grad_up_w = dot(normed_two_all, grad_upward, 0, 0)

    feed_sum = [low(item) for item in (grad_gate_w, grad_up_w, grad_shrink_t)]
    feed_sum = jnp.stack(feed_sum + [jnp.zeros_like(feed_sum[0])])
    grad_normed_two = after(grad_normed_two, feed_sum)

    grad_resid_norm, grad_gain_two = norm_back(resid, factor_two, vectors[6], grad_normed_two)
    grad_resid = grad_rows_out.astype(jnp.float32) + grad_resid_norm
    grad_branch = low(grad_resid)
    grad_attended = low(dot(grad_branch, weights_out, 1, 1)).reshape(
        micro_rows, tok_local, at.head_groups, 1, slot
    )
    grad_attended = jnp.pad(
        jnp.transpose(grad_attended, (0, 2, 3, 1, 4)),
        ((0, 0), (0, 0), (0, at.repeat - 1), (0, 0), (0, 0)),
    )
    grad_attended, early, roots = lax.optimization_barrier((grad_attended, early, roots))
    grad_branch = after(grad_branch, grad_attended)
    grad_out = at.scatter(
        low(
            dot(attended, grad_branch, 0, 0)
            .reshape(at.head_groups, slot, model_width)[:, :head_width]
            .reshape(parts, -1, model_width)
        ),
        "dp",
        at.part,
    )
    grad_attended_row = at.exchange(
        grad_attended.reshape(seq_size, tok_local, slot)
    ).reshape(tok_row, slot)
    feed_sum = at.scatter_step(feed_sum, "seq", at.seq, 1)
    feed_sum, grad_attended_row = lax.optimization_barrier((feed_sum, grad_attended_row))
    feed_sum = at.scatter_step(feed_sum, "seq", at.seq, 2)

    grad_qkv_row, grad_bias = attn_bwd(
        qkv_row,
        grad_attended_row,
        attended_f32,
        log_totals,
        bias_rel,
        seg_col,
        seg_line,
        heads,
        tile,
    )
    grad_normed_part = low(dot(grad_qkv_row, weights_qkv, 1, 1))
    grad_normed_part = at.fold_units(grad_normed_part)
    feed_sum, grad_normed_part = lax.optimization_barrier((feed_sum, grad_normed_part))
    feed_sum = feed_sum.reshape(model_width, hidden_part)
    bit = matrices
    got = low(feed_sum)
    while bit < seq_size:
        got = at.flip(low(feed_sum), "seq", bit)
        bit *= 2
        if bit < seq_size:
            feed_sum = low(feed_sum.astype(jnp.float32) + got.astype(jnp.float32))
    grad_out = after(grad_out, grad_qkv_row)
    grad_out = jnp.transpose(
        grad_out.reshape(-1, at.head_groups, head_width), (1, 0, 2)
    )
    grad_out = at.scatter_heads(jnp.pad(grad_out, ((0, 0), (0, 0), (0, slot - head_width))))
    grad_normed_part, grad_qkv_row = lax.optimization_barrier((grad_normed_part, grad_qkv_row))
    grad_normed_part = at.fold_halves(grad_normed_part)
    grad_qkv = low(dot(normed_row, grad_qkv_row, 0, 0))
    grad_normed_part, grad_qkv, grad_out = lax.optimization_barrier(
        (grad_normed_part, grad_qkv, grad_out)
    )
    grad_normed = at.fold_rows(grad_normed_part).reshape(-1, model_width)

    side_rows = model_width // (parts * sides)
    sums = at.scatter(grad_qkv.reshape(parts, -1, 3 * slot), "dp", at.part)
    sums = low(jnp.concatenate([sums, grad_out], axis=1))
    sums = jnp.transpose(sums.reshape(sides, side_rows, matrices, slot), (0, 2, 1, 3))
    sums = sums.reshape(seq_size, side_rows, slot)

    roots = after(roots, grad_qkv_row)
    feed_right_rows = roots[:, :hidden_span].reshape(-1, hidden_width)
    attention_left_rows = roots[:, hidden_span:, :model_width].reshape(-1, model_width)
    begins = [0, hidden_width, hidden_width + model_width, hidden_width + 2 * model_width]
    early = after(early, grad_qkv)
    feed_old = early[:, : begins[1]]
    feed_left_whole = early[:, begins[1] : begins[2]]
    attention_old = early[:, begins[2] : begins[3]]
    attention_right_whole = early[:, begins[3] :]
    is_shrink = at.matrix == 2
    feed_start = MOMENTUM * jnp.where(
        is_shrink,
        dot(
            feed_to_down(
                feed_old.reshape(at.count, row_span, hidden_width), model_width
            ).reshape(hidden_width, model_width),
            feed_right_rows,
            0,
            1,
        ),
        dot(feed_old, feed_right_rows, 1, 1),
    )
    attention_start = MOMENTUM * dot(attention_left_rows, attention_old, 1, 0)
    grad_normed, feed_start, attention_start, got = lax.optimization_barrier(
        (grad_normed, feed_start, attention_start, got)
    )

    grad_tokens_norm, grad_gain_one = norm_back(tokens, factor_one, vectors[5], grad_normed)
    grad_tokens = (grad_resid + grad_tokens_norm).reshape(micro_rows, tok_local, model_width)
    if seq_size > matrices:
        feed_sum = low(feed_sum.astype(jnp.float32) + got.astype(jnp.float32))
    edge = halo // 2
    wide_grads = jnp.concatenate(
        [
            lax.ppermute(grad_tokens[:, tok_local - edge :], "seq", forward),
            grad_tokens,
            lax.ppermute(grad_tokens[:, :edge], "seq", backward),
        ],
        axis=1,
    )
    sums = at.exchange(after(sums, grad_tokens))
    input_grads, grad_taps = bytes_back(counts, place, wide_bytes, wide_grads, vectors, row_len, halo)
    feed_sum = {0: low(at.sum_groups(feed_sum.astype(jnp.float32)))}
    bit = parts // 2
    if bit:
        feed_sum[bit], grad_taps, sums = lax.optimization_barrier(
            (at.flip(feed_sum[0], "dp", bit), grad_taps, sums)
        )
        bit //= 2
    while bit:
        for key in list(feed_sum):
            feed_sum[key | bit] = at.flip(feed_sum[key], "dp", bit)
        bit //= 2
    sums = sums.reshape(
        micro_rows, at.head_groups, at.repeat, side_rows, slot
    )[..., :head_width]
    sums = jnp.sum(sums.astype(jnp.float32), axis=(0, 2))
    sums = at.sum_groups(jnp.transpose(sums, (1, 0, 2)).reshape(side_rows, model_width))
    full_attention = at.gather_members(low(sums)).reshape(model_width, model_width)
    grad_vectors = jnp.concatenate(
        [grad_taps[:5], grad_gain_one[None], grad_gain_two[None]], axis=0
    )
    part_grad = jnp.einsum("xb,hx->bh", onehot, grad_bias[:, :-1], precision=HIGH_PRECISION)
    grad_table = lax.dynamic_update_slice_in_dim(
        jnp.zeros_like(bias_table), part_grad, head_begin, 1
    )
    small = jnp.pad(grad_table.reshape(-1), (0, model_width - grad_table.size))
    small = low(jnp.concatenate([grad_vectors, small[None]], axis=0))

    member_rows = matrices * row_span
    member_cols = matrices * hidden_span
    def to_owners(strips):
        strips = strips.reshape(strips.shape[0], matrices, row_span, strips.shape[2])
        return jnp.transpose(strips, (1, 2, 0, 3)).reshape(matrices, row_span, hidden_width)

    def down_to_owners(rows):
        return down_to_feed(rows.reshape(matrices, hidden_span, model_width), hidden_width)

    whole_tiles = member_rows % 16 == 0 and member_cols % 128 == 0
    if whole_tiles:
        feed_right, feed_left, feed_step, feed_step_t, feed_cols, feed_rows = feed_update(
            jnp.stack([at.part, at.member]),
            [feed_sum[key] for key in range(parts)],
            feed_right_rows,
            feed_start,
            feed_left_whole,
            member_rows,
        )
    else:
        full_feed = at.gathered(feed_sum, at.part)
        feed_rows = lax.dynamic_slice_in_dim(full_feed, at.member * member_rows, member_rows, 1)
        begin = at.member * member_cols
        feed_cols = lax.dynamic_slice(
            full_feed, (begin // hidden_part, 0, begin % hidden_part), (1, model_width, member_cols)
        )[0].T
        feed_product = low(
            feed_start
            + sum(
                dot(full_feed[i], columns(feed_right_rows, i * hidden_part, hidden_part), 1, 1)
                for i in range(parts)
            )
        )
        feed_step = low(dot(feed_left_whole, feed_product, 1, 0))
        feed_right = jnp.concatenate(
            [low(dot(feed_cols, full_feed[i], 1, 0)) for i in range(parts)], axis=1
        )
        feed_left = low(sum(dot(feed_rows[i], full_feed[i], 1, 1) for i in range(parts)))
        feed_step_t = feed_step.T
        feed_rows = jnp.transpose(feed_rows, (1, 0, 2)).reshape(member_rows, hidden_width)
    shrink_out = low(dot(after(hidden, grad_qkv_row), weights_shrink, 1, 0))
    shrink_out = at.scatter_near(after(shrink_out, feed_step))
    layer_output = low(resid + shrink_out).reshape(micro_rows, tok_local, model_width)

    moved = feed_step.reshape(-1, member_rows, member_cols)
    members = moved.shape[0]
    moved = at.exchange_holders(
        jnp.concatenate(
            [
                moved,
                jnp.broadcast_to(
                    small.reshape(1, -1, member_cols),
                    (members, small.size // member_cols, member_cols),
                ),
            ],
            axis=1,
        )
    )
    small = jnp.sum(moved[:, member_rows:].astype(jnp.float32), axis=0).reshape(small.shape)
    moved = moved[:, :member_rows]

    feed_sums = at.exchange_owners(
        jnp.concatenate(
            [
                feed_right.reshape(matrices, hidden_span, hidden_width),
                as_width(feed_left.reshape(matrices, row_span, model_width), hidden_width),
            ],
            axis=1,
        )
    )
    if whole_tiles:
        attention_parts = attention_update(
            at.member.reshape(1),
            after(full_attention, moved),
            attention_left_rows,
            attention_start,
            attention_right_whole,
        )
    else:
        rows = lax.dynamic_slice_in_dim(full_attention, at.member * member_rows, member_rows, 0)
        cols = columns(full_attention, at.member * member_rows, member_rows)
        attention_product = low(attention_start + dot(attention_left_rows, full_attention, 1, 0))
        attention_parts = [
            low(dot(rows, full_attention, 1, 1)),
            low(dot(cols, full_attention, 0, 0)),
            low(dot(attention_product, attention_right_whole, 1, 0)),
            rows,
        ]
    attention_out = jnp.concatenate(
        [item.reshape(matrices, row_span, model_width) for item in attention_parts], axis=1
    )
    left_rows = -(-row_span * model_width // hidden_width)
    is_down = at.matrix == 2
    feed_pair = jnp.concatenate(
        [
            jnp.where(is_down, down_to_owners(feed_step_t), to_owners(moved)),
            jnp.where(
                is_down,
                down_to_owners(feed_cols),
                feed_rows.reshape(matrices, row_span, hidden_width),
            ),
            as_width(jnp.broadcast_to(low(small), (matrices,) + small.shape), hidden_width),
            as_width(attention_out, hidden_width),
        ],
        axis=1,
    )
    feed_pair = at.exchange_owners(after(feed_pair, feed_sums))
    small_rows = -(-small.size // hidden_width)
    attention_out = of_width(
        feed_pair[:, 2 * row_span + small_rows :], 4 * row_span, model_width
    )
    small = of_width(
        feed_pair[:, 2 * row_span : 2 * row_span + small_rows], small.shape[0], small.shape[1]
    )
    small = jnp.sum(small.astype(jnp.float32), axis=0)
    sum_vectors = small[:-1]
    sum_table = small[-1, : grad_table.size].reshape(grad_table.shape)
    total_tokens = micro_rows * at.dp_size * tok_row
    small_rate = SMALL_RATE / math.sqrt(total_tokens)
    vector_momenta_new = MOMENTUM * vector_momenta + sum_vectors
    vectors_new = vectors - small_rate * vector_momenta_new
    table_momenta_new = MOMENTUM * table_momenta + sum_table
    table_new = bias_table - small_rate * table_momenta_new

    sum_left, sum_right, step, grads = [
        attention_out[:, i * row_span : (i + 1) * row_span].astype(jnp.float32) for i in range(4)
    ]

    def statistics(old, increment):
        return STAT_DECAY * old + (1.0 - STAT_DECAY) * increment

    attention_new = attention_weights - MATRIX_RATE * step
    attention_left_new = statistics(attention_left, sum_left)
    attention_right_new = statistics(attention_right, sum_right)
    attention_mom_new = MOMENTUM * attention_momenta + grads

    def wide(block):
        return block.astype(jnp.float32)

    step, grads = feed_pair[:, :row_span], feed_pair[:, row_span : 2 * row_span]
    sum_left = of_width(feed_sums[:, hidden_span : hidden_span + left_rows], row_span, model_width)
    expand_new = expand_weights - MATRIX_RATE * wide(step[:2])
    expand_left_new = statistics(expand_left, wide(sum_left[:2]))
    expand_right_new = statistics(expand_right, wide(feed_sums[:2, :hidden_span]))
    expand_mom_new = MOMENTUM * expand_momenta + wide(grads[:2])
    shrink_new = shrink_weights - MATRIX_RATE * wide(feed_to_down(step[2], model_width))
    shrink_left_new = statistics(down_left_statistics, wide(feed_sums[2, :hidden_span]))
    shrink_right_new = statistics(shrink_right, wide(sum_left[2]))
    shrink_mom_new = MOMENTUM * shrink_momenta + wide(feed_to_down(grads[2], model_width))
    return (
        layer_output,
        input_grads,
        vectors_new,
        vector_momenta_new,
        table_new,
        table_momenta_new,
        attention_new,
        attention_left_new,
        attention_right_new,
        attention_mom_new,
        low(attention_new),
        expand_new,
        expand_left_new,
        expand_right_new,
        expand_mom_new,
        low(expand_new),
        shrink_new,
        shrink_left_new,
        shrink_right_new,
        shrink_mom_new,
        low(shrink_new),
    )


def solution(mesh):
    row = P("dp", "seq", None)
    stack = P(None, BOTH, None)
    flat = P(BOTH, None)
    return jax.shard_map(
        per_device,
        mesh=mesh,
        in_specs=(row, P("dp", "seq"), P("dp"), P(), row)
        + (P(),) * 4
        + (stack,) * 12
        + (flat,) * 6,
        out_specs=(row, row) + (P(),) * 4 + (stack,) * 10 + (flat,) * 5,
        check_vma=False,
    )
```

```python
import functools
import math

import jax
import jax.numpy as jnp
from jax import lax
from jax.experimental import pallas as pl
from jax.experimental.pallas import tpu as pltpu
from jax.sharding import PartitionSpec as P

EPSILON = 1e-06
STAT_DECAY = 0.95
MOMENTUM = 0.9
MATRIX_RATE = 0.1
SMALL_RATE = 0.1
MASKED = -1e30
HIGH_PRECISION = lax.Precision.HIGHEST
BOTH = ("dp", "seq")


def fill_bias(brel_ref, bias_sc, heads, tile):
    span = brel_ref.shape[1]
    rows = lax.broadcasted_iota(jnp.int32, (8, span), 0)
    for h in range(heads):
        wide = jnp.broadcast_to(brel_ref[h:h + 1, :], (8, span))
        first = wide
        for i in range(8):
            first = jnp.where(rows == i, pltpu.roll(wide, span - (tile - 1) + i, 1), first)
        bias_sc[h, 0:8, :] = first
        size = 8
        while size < tile:
            bias_sc[h, size:2 * size, :] = pltpu.roll(bias_sc[h, 0:size, :], size, 1)
            size *= 2

def attn_fwd_kernel(heads, tile, qkv_ref, brel_ref, segc_ref, segr_ref, out_ref, outf_ref, lse_ref, bias_sc):
    step = pl.program_id(0)
    length = qkv_ref.shape[0]
    width = qkv_ref.shape[1] // 3
    dh = outf_ref.shape[1] // heads

    @pl.when(step == 0)
    def _():
        fill_bias(brel_ref, bias_sc, heads, tile)

    begin = pl.multiple_of(step * tile, tile)
    offset = pl.multiple_of(length - tile - begin, 128)
    same = segc_ref[...] == segr_ref[...]
    lanes = lax.broadcasted_iota(jnp.int32, (tile, 128), 1)
    lse_all = jnp.zeros((tile, 128), jnp.float32)
    outs = []
    for h in range(heads):
        q = qkv_ref[pl.ds(begin, tile), h * dh:(h + 1) * dh]
        k = qkv_ref[:, width + h * dh:width + (h + 1) * dh]
        v = qkv_ref[:, 2 * width + h * dh:2 * width + (h + 1) * dh]
        scores = lax.dot_general(q, k, (((1,), (1,)), ((), ())), preferred_element_type=jnp.float32)
        scores = jnp.where(same, scores + bias_sc[h, :, pl.ds(offset, length)], MASKED)
        top = jnp.max(scores, axis=1, keepdims=True)
        probs = jnp.exp(scores - top)
        total = jnp.sum(probs, axis=1, keepdims=True)
        out = lax.dot_general(probs.astype(jnp.bfloat16), v, (((1,), (0,)), ((), ())), preferred_element_type=jnp.float32)
        outs.append(out / total)
        lse_all = jnp.where(lanes == h, top + jnp.log(total), lse_all)
    joined = jnp.concatenate(outs, axis=1)
    outf_ref[...] = joined
    fill = out_ref.shape[1] - joined.shape[1]
    if fill:
        joined = jnp.concatenate([joined, jnp.zeros((tile, fill), jnp.float32)], axis=1)
    out_ref[...] = joined.astype(jnp.bfloat16)
    lse_ref[...] = lse_all

def attn_fwd(qkv, brel, segc, segr, heads, dh, tile=128):
    length = qkv.shape[0]
    width = heads * dh
    full = lambda s: pl.BlockSpec(s, lambda i: (0,) * len(s))
    rowb = lambda w: pl.BlockSpec((tile, w), lambda i: (i, 0))
    return pl.pallas_call(
        functools.partial(attn_fwd_kernel, heads, tile),
        grid=(length // tile,),
        in_specs=[full(qkv.shape), full(brel.shape), rowb(1), full(segr.shape)],
        out_specs=[rowb(qkv.shape[1] // 3), rowb(width), rowb(128)],
        out_shape=[jax.ShapeDtypeStruct((length, qkv.shape[1] // 3), jnp.bfloat16), jax.ShapeDtypeStruct((length, width), jnp.float32), jax.ShapeDtypeStruct((length, 128), jnp.float32)],
        scratch_shapes=[pltpu.VMEM((heads, tile, 2 * length), jnp.float32)],
        compiler_params=pltpu.CompilerParams(vmem_limit_bytes=48 * 2**20),
        cost_estimate=pl.CostEstimate(flops=4 * length * length * width, bytes_accessed=6 * length * width * 2, transcendentals=heads * length * length),
    )(qkv, brel, segc, segr)

def attn_bwd_kernel(heads, tile, trans, qkv_ref, grad_ref, outf_ref, lse_ref, brel_ref, segc_ref, segr_ref, dqkv_ref, gb_ref, bias_sc, gb_sc, dk_sc, dv_sc):
    step = pl.program_id(0)
    length = qkv_ref.shape[0]
    width = qkv_ref.shape[1] // 3
    dh = outf_ref.shape[1] // heads

    @pl.when(step == 0)
    def _():
        fill_bias(brel_ref, bias_sc, heads, tile)
        gb_sc[...] = jnp.zeros_like(gb_sc)
        dk_sc[...] = jnp.zeros_like(dk_sc)
        dv_sc[...] = jnp.zeros_like(dv_sc)

    begin = pl.multiple_of(step * tile, tile)
    offset = pl.multiple_of(length - tile - begin, 128)
    same = segc_ref[...] == segr_ref[...]
    dqs = []
    for h in range(heads):
        q = qkv_ref[pl.ds(begin, tile), h * dh:(h + 1) * dh]
        k = qkv_ref[:, width + h * dh:width + (h + 1) * dh]
        v = qkv_ref[:, 2 * width + h * dh:2 * width + (h + 1) * dh]
        g = grad_ref[:, h * dh:(h + 1) * dh]
        delta = jnp.sum(g.astype(jnp.float32) * outf_ref[:, h * dh:(h + 1) * dh], axis=1, keepdims=True)
        lse = lse_ref[:, h:h + 1]
        scores = lax.dot_general(q, k, (((1,), (1,)), ((), ())), preferred_element_type=jnp.float32)
        scores = jnp.where(same, scores + bias_sc[h, :, pl.ds(offset, length)], MASKED)
        probs = jnp.exp(scores - lse)
        gp = lax.dot_general(g, v, (((1,), (1,)), ((), ())), preferred_element_type=jnp.float32)
        gs = (probs * (gp - delta))
        gsb = gs.astype(jnp.bfloat16)
        pb = probs.astype(jnp.bfloat16)
        gb_sc[h, :, pl.ds(offset, length)] += gsb.astype(jnp.float32)
        dqs.append(lax.dot_general(gsb, k, (((1,), (0,)), ((), ())), preferred_element_type=jnp.float32))
        if trans:
            dk_sc[h] += lax.dot_general(q, gsb, (((0,), (0,)), ((), ())), preferred_element_type=jnp.float32)
            dv_sc[h] += lax.dot_general(g, pb, (((0,), (0,)), ((), ())), preferred_element_type=jnp.float32)
        else:
            dk_sc[h] += lax.dot_general(gsb, q, (((0,), (0,)), ((), ())), preferred_element_type=jnp.float32)
            dv_sc[h] += lax.dot_general(pb, g, (((0,), (0,)), ((), ())), preferred_element_type=jnp.float32)
    fill = width - heads * dh

    def slot(parts):
        rows = parts[0].shape[0]
        filled = parts + ([jnp.zeros((rows, fill), jnp.float32)] if fill else [])
        return jnp.concatenate(filled, axis=1).astype(jnp.bfloat16)

    dqkv_ref[pl.ds(begin, tile), 0:width] = slot(dqs)

    @pl.when(step == pl.num_programs(0) - 1)
    def _():
        turn = (lambda x: x.T) if trans else (lambda x: x)
        dqkv_ref[:, width:2 * width] = slot([turn(dk_sc[h]) for h in range(heads)])
        dqkv_ref[:, 2 * width:3 * width] = slot([turn(dv_sc[h]) for h in range(heads)])
        span = gb_sc.shape[2]
        rows = lax.broadcasted_iota(jnp.int32, (8, span), 0)
        for h in range(heads):
            size = tile // 2
            part = gb_sc[h]
            while size >= 8:
                part = part[:size] + pltpu.roll(part[size:], span - size, 1)
                size //= 2
            line = jnp.zeros((1, span), jnp.float32)
            for i in range(8):
                line = line + jnp.sum(jnp.where(rows == i, pltpu.roll(part, (tile - 1 - i) % span, 1), 0.0), axis=0, keepdims=True)
            gb_ref[h:h + 1, :] = line

def attn_bwd(qkv, grad, outf, lse, brel, segc, segr, heads, tile=128, trans=True):
    length, width = outf.shape
    dh = width // heads
    full = lambda s: pl.BlockSpec(s, lambda i: (0,) * len(s))
    rowb = lambda w: pl.BlockSpec((tile, w), lambda i: (i, 0))
    acc = (heads, dh, length) if trans else (heads, length, dh)
    return pl.pallas_call(
        functools.partial(attn_bwd_kernel, heads, tile, trans),
        grid=(length // tile,),
        in_specs=[full(qkv.shape), rowb(grad.shape[1]), rowb(width), rowb(128), full(brel.shape), rowb(1), full(segr.shape)],
        out_specs=[full(qkv.shape), full(brel.shape)],
        out_shape=[jax.ShapeDtypeStruct(qkv.shape, jnp.bfloat16), jax.ShapeDtypeStruct(brel.shape, jnp.float32)],
        scratch_shapes=[pltpu.VMEM((heads, tile, 2 * length), jnp.float32), pltpu.VMEM((heads, tile, 2 * length), jnp.float32), pltpu.VMEM(acc, jnp.float32), pltpu.VMEM(acc, jnp.float32)],
        compiler_params=pltpu.CompilerParams(vmem_limit_bytes=56 * 2**20),
        cost_estimate=pl.CostEstimate(flops=10 * length * length * width, bytes_accessed=12 * length * width * 2, transcendentals=heads * length * length),
    )(qkv, grad, outf, lse, brel, segc, segr)

def byte_window(bytes_ref, counts_ref, taps, begin, span, place, row_len):
    row = pl.program_id(0)
    positions = place + begin + lax.broadcasted_iota(jnp.int32, (span, 1), 0)
    window = bytes_ref[0, pl.ds(begin, span), :].astype(jnp.float32)
    valid = (positions >= 0) & (positions < counts_ref[row])
    embedded = jnp.where(valid, window, 0.0)
    conv = embedded * taps[3:4]
    for tap in range(3):
        conv = conv + pltpu.roll(embedded, 3 - tap, 0) * taps[tap : tap + 1]
    conv = jnp.where(positions < row_len, conv, 0.0)
    return positions, embedded, conv


def block_sums(values, positions, span):
    ahead = [None] + [pltpu.roll(values, span - i, 0) for i in (1, 2)]
    behind = [None] + [pltpu.roll(values, i, 0) for i in (1, 2)]
    two = values + jnp.where(positions % 2 == 0, ahead[1], behind[1])
    four = two + jnp.where(
        positions % 4 < 2, pltpu.roll(two, span - 2, 0), pltpu.roll(two, 2, 0)
    )
    phase = (positions + 9) % 3
    three = (
        values
        + jnp.where(phase != 2, ahead[1], behind[2])
        + jnp.where(phase == 0, ahead[2], behind[1])
    )
    return two, three, four


def three_sum(values, positions, span):
    phase = (positions + 9) % 3
    return (
        values
        + jnp.where(phase != 2, pltpu.roll(values, span - 1, 0), pltpu.roll(values, 2, 0))
        + jnp.where(phase == 0, pltpu.roll(values, span - 2, 0), pltpu.roll(values, 1, 0))
    )


def three_share(positions, row_len):
    left = row_len - (positions - (positions + 9) % 3)
    return jnp.where(left >= 3, 1.0 / 3.0, jnp.where(left == 2, 0.5, 1.0))


def block_means(conv, positions, span, row_len):
    two, three, four = block_sums(conv, positions, span)
    return [conv, two * 0.5, three * three_share(positions, row_len), four * 0.25]


def size_softmax(pooled, score_row):
    scores = [jnp.sum(item * score_row, axis=1, keepdims=True) for item in pooled]
    top = functools.reduce(jnp.maximum, scores)
    powers = [jnp.exp(item - top) for item in scores]
    total = sum(powers)
    return [item / total for item in powers]


def tokens_kernel(row_len, halo, chunk, counts_ref, place_ref, bytes_ref, vectors_ref, tokens_ref, normed_ref, pair_ref):
    span = chunk + 2 * halo
    taps = vectors_ref[0:4, :]

    def visit(index, carry):
        begin = pl.multiple_of(index * chunk, chunk)
        positions, embedded, conv = byte_window(
            bytes_ref, counts_ref, taps, begin, span, place_ref[0], row_len
        )
        pooled = block_means(conv, positions, span, row_len)
        pooled = [item[halo : halo + chunk] for item in pooled]
        weights = size_softmax(pooled, vectors_ref[4:5, :])
        blended = sum(weight * item for weight, item in zip(weights, pooled))
        half = chunk // 2
        halves = []
        for lane in range(pair_ref.shape[0]):
            pair_ref[lane] = blended[:, lane * 128 : (lane + 1) * 128]
            halves.append(
                pair_ref[lane, pl.Slice(0, half, 2), :] + pair_ref[lane, pl.Slice(1, half, 2), :]
            )
        tokens = 0.5 * jnp.concatenate(halves, axis=1)
        factor = lax.rsqrt(jnp.mean(tokens * tokens, axis=1, keepdims=True) + EPSILON)
        rows = pl.ds(pl.multiple_of(index * half, half), half)
        tokens_ref[rows, :] = tokens
        normed_ref[rows, :] = (tokens * factor * vectors_ref[5:6, :]).astype(jnp.bfloat16)
        return carry

    lax.fori_loop(0, (bytes_ref.shape[1] - 2 * halo) // chunk, visit, 0)


def make_tokens(counts, place, wide_bytes, vectors, row_len, halo=8, chunk=64):
    micro, wide, width = wide_bytes.shape
    count = (wide - 2 * halo) // 2
    return pl.pallas_call(
        functools.partial(tokens_kernel, row_len, halo, chunk),
        grid=(micro,),
        in_specs=[
            pl.BlockSpec(memory_space=pltpu.SMEM),
            pl.BlockSpec(memory_space=pltpu.SMEM),
            pl.BlockSpec((1, wide, width), lambda i: (i, 0, 0)),
            pl.BlockSpec(vectors.shape, lambda i: (0, 0)),
        ],
        out_specs=[pl.BlockSpec((count, width), lambda i: (i, 0))] * 2,
        out_shape=[
            jax.ShapeDtypeStruct((micro * count, width), jnp.float32),
            jax.ShapeDtypeStruct((micro * count, width), jnp.bfloat16),
        ],
        scratch_shapes=[pltpu.VMEM((width // 128, chunk, 128), jnp.float32)],
        compiler_params=pltpu.CompilerParams(vmem_limit_bytes=32 * 2**20),
        cost_estimate=pl.CostEstimate(
            flops=60 * micro * wide * width, bytes_accessed=6 * micro * wide * width, transcendentals=0
        ),
    )(counts, place, wide_bytes, vectors)


def bytes_kernel(row_len, halo, chunk, counts_ref, place_ref, bytes_ref, grads_ref, vectors_ref, out_ref, sums_ref, spread_ref, parts_ref):
    row = pl.program_id(0)
    span = chunk + 2 * halo
    taps = vectors_ref[0:4, :]
    score_row = vectors_ref[4:5, :]
    half = grads_ref.shape[1]
    for lane in range(spread_ref.shape[0]):
        lanes = grads_ref[0, :, lane * 128 : (lane + 1) * 128] * 0.5
        spread_ref[lane, pl.Slice(0, half, 2), :] = lanes
        spread_ref[lane, pl.Slice(1, half, 2), :] = lanes

    @pl.when(row == 0)
    def _():
        parts_ref[...] = jnp.zeros_like(parts_ref)

    def visit(index, carry):
        begin = pl.multiple_of(index * chunk, chunk)
        positions, embedded, conv = byte_window(
            bytes_ref, counts_ref, taps, begin, span, place_ref[0], row_len
        )
        pooled = block_means(conv, positions, span, row_len)
        weights = size_softmax(pooled, score_row)
        grad = jnp.concatenate(
            [spread_ref[lane, pl.ds(begin, span), :] for lane in range(spread_ref.shape[0])], axis=1
        )
        along = [jnp.sum(grad * item, axis=1, keepdims=True) for item in pooled]
        mean = sum(weight * item for weight, item in zip(weights, along))
        sizes = [weight * (item - mean) for weight, item in zip(weights, along)]
        first, second, third, fourth = [
            weight * grad + size * score_row for weight, size in zip(weights, sizes)
        ]
        even = positions % 2 == 0
        pair = 0.5 * second + 0.25 * fourth
        fours = 0.25 * fourth
        pair = pair + jnp.where(even, pltpu.roll(pair, span - 1, 0), pltpu.roll(pair, 1, 0))
        fours = fours + jnp.where(even, pltpu.roll(fours, span - 1, 0), pltpu.roll(fours, 1, 0))
        fours = jnp.where(
            positions % 4 < 2, pltpu.roll(fours, span - 2, 0), pltpu.roll(fours, 2, 0)
        )
        share = three_share(positions, row_len)
        grad_conv = first + pair + fours + three_sum(third, positions, span) * share
        grad_conv = jnp.where((positions < row_len) & (positions >= 0), grad_conv, 0.0)
        back = grad_conv * taps[3:4]
        for tap in range(3):
            back = back + pltpu.roll(grad_conv, span - (3 - tap), 0) * taps[tap : tap + 1]
        own = slice(halo, halo + chunk)
        back = jnp.where(positions < counts_ref[row], back, 0.0)
        out_ref[0, pl.ds(begin, chunk), :] = back[own]

        def fold(values):
            return jnp.sum(values.reshape(chunk // 8, 8, values.shape[1]), axis=0)

        for tap in range(4):
            beside = embedded if tap == 3 else pltpu.roll(embedded, 3 - tap, 0)
            parts_ref[tap] += fold((grad_conv * beside)[own])
        parts_ref[4] += fold(sum(size * item for size, item in zip(sizes, pooled))[own])
        return carry

    lax.fori_loop(0, (bytes_ref.shape[1] - 2 * halo) // chunk, visit, 0)

    @pl.when(row == pl.num_programs(0) - 1)
    def _():
        sums_ref[...] = jnp.zeros_like(sums_ref)
        for item in range(5):
            sums_ref[item : item + 1, :] = jnp.sum(parts_ref[item], axis=0, keepdims=True)


def bytes_back(counts, place, wide_bytes, wide_grads, vectors, row_len, halo=8, chunk=64):
    micro, wide, width = wide_bytes.shape
    count = wide - 2 * halo
    return pl.pallas_call(
        functools.partial(bytes_kernel, row_len, halo, chunk),
        grid=(micro,),
        in_specs=[
            pl.BlockSpec(memory_space=pltpu.SMEM),
            pl.BlockSpec(memory_space=pltpu.SMEM),
            pl.BlockSpec((1, wide, width), lambda i: (i, 0, 0)),
            pl.BlockSpec((1, wide // 2, width), lambda i: (i, 0, 0)),
            pl.BlockSpec(vectors.shape, lambda i: (0, 0)),
        ],
        out_specs=[
            pl.BlockSpec((1, count, width), lambda i: (i, 0, 0)),
            pl.BlockSpec((8, width), lambda i: (0, 0)),
        ],
        out_shape=[
            jax.ShapeDtypeStruct((micro, count, width), jnp.float32),
            jax.ShapeDtypeStruct((8, width), jnp.float32),
        ],
        scratch_shapes=[
            pltpu.VMEM((width // 128, wide, 128), jnp.float32),
            pltpu.VMEM((5, 8, width), jnp.float32),
        ],
        compiler_params=pltpu.CompilerParams(vmem_limit_bytes=32 * 2**20),
        cost_estimate=pl.CostEstimate(
            flops=150 * micro * wide * width, bytes_accessed=8 * micro * wide * width, transcendentals=0
        ),
    )(counts, place, wide_bytes, wide_grads, vectors)

def low(values):
    return values.astype(jnp.bfloat16)


def dot(left_side, right_side, left_dim, right_dim):
    return lax.dot_general(
        left_side,
        right_side,
        (((left_dim,), (right_dim,)), ((), ())),
        preferred_element_type=jnp.float32,
    )


def rms_factor(values):
    return lax.rsqrt(jnp.mean(values * values, axis=-1, keepdims=True) + EPSILON)


def norm_back(values, factor, gain_row, grad_out):
    scaled = grad_out * gain_row
    grad_gain = jnp.sum(grad_out * values * factor, axis=0)
    inner_mean = jnp.mean(scaled * values, axis=-1, keepdims=True)
    return (factor * (scaled - values * inner_mean * factor * factor), grad_gain)


def feed_kernel(parts, place_ref, *refs):
    pieces = refs[:parts]
    right_ref, start_ref, left_ref = refs[parts : parts + 3]
    sum_right_ref, sum_left_ref, step_ref, step_t_ref, cols_ref, rows_ref = refs[parts + 3 : -1]
    whole_ref = refs[-1]
    width = pieces[0].shape[1]
    for key, piece in enumerate(pieces):
        begin = pl.multiple_of((place_ref[0] ^ key) * width, width)
        whole_ref[:, pl.ds(begin, width)] = piece[...]
    member = place_ref[1]
    count = cols_ref.shape[0]
    cols = whole_ref[:, pl.ds(pl.multiple_of(member * count, count), count)].T
    cols_ref[...] = cols
    count = rows_ref.shape[0]
    rows = whole_ref[pl.ds(pl.multiple_of(member * count, count), count), :]
    rows_ref[...] = rows
    product = start_ref[...]
    for begin in range(0, whole_ref.shape[1], width):
        block = whole_ref[:, begin : begin + width]
        sum_right_ref[:, begin : begin + width] = lax.dot_general(
            cols, block, (((1,), (0,)), ((), ())), preferred_element_type=jnp.float32
        ).astype(jnp.bfloat16)
        product = product + lax.dot_general(
            block,
            right_ref[:, begin : begin + width],
            (((1,), (1,)), ((), ())),
            preferred_element_type=jnp.float32,
        )
    sum_left_ref[...] = lax.dot_general(
        rows, whole_ref[...], (((1,), (1,)), ((), ())), preferred_element_type=jnp.float32
    ).astype(jnp.bfloat16)
    step = lax.dot_general(
        left_ref[...],
        product.astype(jnp.bfloat16),
        (((1,), (0,)), ((), ())),
        preferred_element_type=jnp.float32,
    )
    step_ref[...] = step.astype(jnp.bfloat16)
    step_t_ref[...] = step.T.astype(jnp.bfloat16)


def feed_update(place, pieces, right_rows, start, left_whole, member_rows):
    rows, width = pieces[0].shape
    cols = right_rows.shape[0]
    total = width * len(pieces)
    vmem = pl.BlockSpec(memory_space=pltpu.VMEM)
    shapes = [(cols, total), (member_rows, rows), (rows, cols), (cols, rows), (cols, rows)]
    shapes.append((member_rows, total))
    return pl.pallas_call(
        functools.partial(feed_kernel, len(pieces)),
        grid=(1,),
        in_specs=[pl.BlockSpec(memory_space=pltpu.SMEM)]
        + [vmem] * (len(pieces) + 2)
        + [pl.BlockSpec((rows, rows), lambda i: (0, 0))],
        out_specs=[vmem] * len(shapes),
        out_shape=[jax.ShapeDtypeStruct(shape, jnp.bfloat16) for shape in shapes],
        scratch_shapes=[pltpu.VMEM((rows, total), jnp.bfloat16)],
        compiler_params=pltpu.CompilerParams(vmem_limit_bytes=48 * 2**20),
        cost_estimate=pl.CostEstimate(
            flops=4 * rows * total * cols, bytes_accessed=6 * rows * total, transcendentals=0
        ),
    )(place, *pieces, right_rows, start, left_whole)


def attention_kernel(member_ref, whole_ref, left_ref, start_ref, right_ref, out_ref, square_ref):
    count = left_ref.shape[0]
    mine = pl.ds(pl.multiple_of(member_ref[0] * count, count), count)
    whole = whole_ref[...]
    rows = whole_ref[mine, :]
    out_ref[0] = lax.dot_general(
        rows, whole, (((1,), (1,)), ((), ())), preferred_element_type=jnp.float32
    ).astype(jnp.bfloat16)
    square_ref[...] = lax.dot_general(
        whole, whole, (((0,), (0,)), ((), ())), preferred_element_type=jnp.float32
    )
    out_ref[1] = square_ref[mine, :].astype(jnp.bfloat16)
    product = start_ref[...] + lax.dot_general(
        left_ref[...], whole, (((1,), (0,)), ((), ())), preferred_element_type=jnp.float32
    )
    out_ref[2] = lax.dot_general(
        product.astype(jnp.bfloat16),
        right_ref[...],
        (((1,), (0,)), ((), ())),
        preferred_element_type=jnp.float32,
    ).astype(jnp.bfloat16)
    out_ref[3] = rows


def attention_update(member, whole, left_rows, start, right_whole):
    count, width = left_rows.shape
    vmem = pl.BlockSpec(memory_space=pltpu.VMEM)
    return pl.pallas_call(
        attention_kernel,
        grid=(1,),
        in_specs=[pl.BlockSpec(memory_space=pltpu.SMEM)]
        + [vmem] * 3
        + [pl.BlockSpec((width, width), lambda i: (0, 2))],
        out_specs=vmem,
        out_shape=jax.ShapeDtypeStruct((4, count, width), jnp.bfloat16),
        scratch_shapes=[pltpu.VMEM((width, width), jnp.float32)],
        compiler_params=pltpu.CompilerParams(vmem_limit_bytes=32 * 2**20),
        cost_estimate=pl.CostEstimate(
            flops=2 * width**3, bytes_accessed=6 * width * width, transcendentals=0
        ),
    )(member, whole, left_rows, start, right_whole)


class Layout:
    def __init__(self, head_count, micro_rows):
        self.dp_size = lax.axis_size("dp")
        self.seq_size = lax.axis_size("seq")
        self.count = self.dp_size * self.seq_size
        self.dp = lax.axis_index("dp")
        self.seq = lax.axis_index("seq")
        self.micro = micro_rows
        self.parts = math.gcd(self.dp_size, head_count & -head_count)
        self.groups = self.dp_size // self.parts
        self.part = self.dp % self.parts
        self.head_groups = head_count & -head_count
        self.repeat = self.seq_size // (micro_rows * self.head_groups)
        self.unit = self.seq // self.repeat
        self.matrices = 4
        self.sides = self.seq_size // self.matrices
        self.matrix = self.seq % self.matrices
        self.side = self.seq // self.matrices
        self.member = self.dp * self.sides + self.side
        self.members = [
            [
                (group * self.parts + part) * self.seq_size + side * self.matrices + matrix
                for part in range(self.parts)
                for side in range(self.sides)
            ]
            for group in range(self.groups)
            for matrix in range(self.matrices)
        ]
        self.holders = [
            [
                dp * self.seq_size + side * self.matrices + matrix
                for dp in range(self.dp_size)
                for side in range(self.sides)
            ]
            for matrix in range(self.matrices)
        ]
        self.owners = [
            [side * self.matrices + matrix for matrix in range(self.matrices)]
            for side in range(self.sides)
        ]

    def flip(self, block, axis, bits):
        size = lax.axis_size(axis)
        return lax.ppermute(block, axis, [(i, i ^ bits) for i in range(size)])

    def gather_parts(self, block):
        pieces = {0: block}
        bit = self.parts // 2
        while bit:
            for key in list(pieces):
                pieces[key | bit] = self.flip(pieces[key], "dp", bit)
            bit //= 2
        whole = jnp.zeros((self.parts,) + block.shape, block.dtype)
        for key, piece in pieces.items():
            whole = lax.dynamic_update_index_in_dim(whole, piece, self.part ^ key, 0)
        return whole

    def scatter_step(self, blocks, axis, index, bit):
        pairs = blocks.reshape((blocks.shape[0] // 2, 2) + blocks.shape[1:])
        mine = (index // bit) % 2
        kept = lax.dynamic_index_in_dim(pairs, mine, 1, False)
        sent = lax.dynamic_index_in_dim(pairs, 1 - mine, 1, False)
        got = self.flip(low(sent), axis, bit)
        return low(kept.astype(jnp.float32) + got.astype(jnp.float32))

    def scatter(self, blocks, axis, index):
        bit = 1
        while blocks.shape[0] > 1:
            blocks = self.scatter_step(blocks, axis, index, bit)
            bit *= 2
        return blocks[0]

    def near_parts(self, block):
        pieces = {0: block}
        bit = self.parts // 2
        while bit:
            for key in list(pieces):
                pieces[key | bit] = self.flip(pieces[key], "dp", bit)
            bit //= 2
        return jnp.concatenate([pieces[key] for key in range(self.parts)], axis=0)

    def scatter_near(self, rows):
        blocks = rows.reshape((self.parts, -1) + rows.shape[1:])
        bit = 1
        while blocks.shape[0] > 1:
            pairs = blocks.reshape((blocks.shape[0] // 2, 2) + blocks.shape[1:])
            got = self.flip(low(pairs[:, 1]), "dp", bit)
            blocks = pairs[:, 0].astype(jnp.float32) + got.astype(jnp.float32)
            bit *= 2
        return blocks[0]

    def scatter_heads(self, blocks):
        index, bit = self.unit % self.head_groups, 1
        while blocks.shape[0] > 1:
            pairs = blocks.reshape((blocks.shape[0] // 2, 2) + blocks.shape[1:])
            mine = (index // bit) % 2
            kept = lax.dynamic_index_in_dim(pairs, mine, 1, False)
            sent = lax.dynamic_index_in_dim(pairs, 1 - mine, 1, False)
            got = self.flip(low(sent), "seq", bit * self.repeat)
            blocks = kept.astype(jnp.float32) + got.astype(jnp.float32)
            bit *= 2
        return blocks[0]

    def sum_groups(self, block):
        total = block
        for shift in range(1, self.groups):
            turn = [(i, (i + shift * self.parts) % self.dp_size) for i in range(self.dp_size)]
            total = total + lax.ppermute(low(block), "dp", turn).astype(jnp.float32)
        return total

    def to_units(self, blocks):
        shape = blocks.shape
        blocks = blocks[:, :, None]
        if self.repeat > 1:
            blocks = jnp.broadcast_to(blocks, shape[:2] + (self.repeat,) + shape[2:])
        return self.exchange(blocks.reshape((self.seq_size,) + shape[2:]))

    def exchange(self, blocks):
        return lax.all_to_all(blocks, "seq", 0, 0, tiled=True)

    def gather_step(self, pieces, bit, axis="seq"):
        grown = []
        for held in pieces:
            keys = sorted(held)
            moved = self.flip(jnp.stack([held[key] for key in keys]), axis, bit)
            held = dict(held)
            for place, key in enumerate(keys):
                held[key | bit] = moved[place]
            grown.append(held)
        return grown

    def gathered(self, held, index):
        whole = jnp.zeros((len(held),) + held[0].shape, held[0].dtype)
        for key, piece in held.items():
            whole = lax.dynamic_update_index_in_dim(whole, piece, index ^ key, 0)
        return whole

    def by_halves(self):
        return self.repeat == 1 and self.micro == 2 and self.head_groups == 4

    def rows_to_units(self, blocks, beside):
        held = [{0: item} for item in beside]
        bits = [1 << i for i in reversed(range(self.parts.bit_length() - 1))]
        if not self.by_halves():
            shape = blocks.shape
            blocks = jnp.broadcast_to(blocks[:, None], shape[:1] + (self.head_groups,) + shape[1:])
            whole = self.to_units(blocks)
            for bit in bits:
                held = self.gather_step(held, bit, "dp")
            return whole.reshape((-1,) + shape[2:]), held
        mine = self.unit // self.head_groups
        near = lax.dynamic_index_in_dim(blocks, mine, 0, False)
        far = self.flip(lax.dynamic_index_in_dim(blocks, 1 - mine, 0, False), "seq", 4)
        near_one = self.flip(near, "seq", 1)
        far, held = lax.optimization_barrier((far, held))
        far_two = self.flip(far, "seq", 2)
        for bit in bits[:1]:
            held = self.gather_step(held, bit, "dp")
        near_one, far_two = lax.optimization_barrier((near_one, far_two))
        near_two = self.flip(jnp.stack([near, near_one]), "seq", 2)
        far_one = self.flip(jnp.stack([far, far_two]), "seq", 1)
        near_two, far_one, held = lax.optimization_barrier((near_two, far_one, held))
        for bit in bits[1:]:
            held = self.gather_step(held, bit, "dp")
        pieces = [near, near_one, near_two[0], near_two[1], far, far_one[0], far_two, far_one[1]]
        whole = self.gathered(dict(enumerate(pieces)), self.seq)
        return whole.reshape((-1,) + blocks.shape[2:]), held

    def fold_units(self, row):
        blocks = row.reshape((self.seq_size, -1) + row.shape[1:])
        if not self.by_halves():
            return self.exchange(low(blocks))

        def pick(*keys):
            picked = [
                lax.dynamic_index_in_dim(blocks, self.seq ^ key, 0, False).astype(jnp.float32)
                for key in keys
            ]
            return jnp.stack(picked)

        near = pick(0, 1) + self.flip(low(pick(2, 3)), "seq", 2).astype(jnp.float32)
        far = pick(4, 6) + self.flip(low(pick(5, 7)), "seq", 1).astype(jnp.float32)
        return (near, far)

    def fold_halves(self, folded):
        if not self.by_halves():
            return folded
        near, far = folded
        near = near[0] + self.flip(low(near[1]), "seq", 1).astype(jnp.float32)
        far = far[0] + self.flip(low(far[1]), "seq", 2).astype(jnp.float32)
        return (near, far)

    def fold_rows(self, folded):
        if not self.by_halves():
            blocks = folded.astype(jnp.float32)
            return jnp.sum(blocks.reshape((self.micro, -1) + blocks.shape[1:]), axis=1)
        near, far = folded
        far = self.flip(low(far), "seq", 4).astype(jnp.float32)
        first = self.unit // self.head_groups == 0
        return jnp.stack([jnp.where(first, near, far), jnp.where(first, far, near)])

    def gather_members(self, block):
        whole = lax.all_gather(block, BOTH, axis=0, axis_index_groups=self.members)
        return whole.reshape((self.parts, self.sides) + block.shape)

    def spread_members(self, block):
        count = self.parts * self.sides
        blocks = jnp.broadcast_to(block[None], (count,) + block.shape)
        return lax.all_to_all(blocks, BOTH, 0, 0, tiled=True, axis_index_groups=self.members)

    def gather_holders(self, block):
        return lax.all_gather(block, BOTH, axis=0, axis_index_groups=self.holders, tiled=True)

    def exchange_holders(self, blocks):
        return lax.all_to_all(blocks, BOTH, 0, 0, tiled=True, axis_index_groups=self.holders)

    def exchange_owners(self, blocks):
        return lax.all_to_all(blocks, "seq", 0, 0, tiled=True, axis_index_groups=self.owners)


def after(value, token):
    return lax.optimization_barrier((value, token))[0]


def as_width(blocks, width):
    flat = blocks.reshape(blocks.shape[0], -1)
    short = -flat.shape[1] % width
    return jnp.pad(flat, ((0, 0), (0, short))).reshape(blocks.shape[0], -1, width)


def down_to_feed(blocks, width, lanes=256):
    lead, (rows, columns) = blocks.shape[:-2], blocks.shape[-2:]
    groups, parts = width // lanes, columns // lanes
    count = len(lead)
    blocks = blocks.reshape(lead + (groups, rows // groups, parts, lanes))
    order = tuple(range(count)) + (count + 2, count + 1, count, count + 3)
    return jnp.transpose(blocks, order).reshape(lead + (parts * rows // groups, width))


def feed_to_down(blocks, columns, lanes=256):
    lead, (rows, width) = blocks.shape[:-2], blocks.shape[-2:]
    groups, parts = width // lanes, columns // lanes
    count = len(lead)
    blocks = blocks.reshape(lead + (parts, rows // parts, groups, lanes))
    order = tuple(range(count)) + (count + 2, count + 1, count, count + 3)
    return jnp.transpose(blocks, order).reshape(lead + (groups * rows // parts, columns))


def of_width(blocks, rows, columns):
    flat = blocks.reshape(blocks.shape[0], -1)
    return flat[:, : rows * columns].reshape(blocks.shape[0], rows, columns)


def gather_all(block):
    return lax.all_gather(block, BOTH, axis=0, tiled=True)


def per_device(
    byte_rows,
    segments,
    counts,
    buckets,
    cotangent,
    vectors,
    vector_momenta,
    bias_table,
    table_momenta,
    attention_weights,
    attention_left,
    attention_right,
    attention_left_root,
    attention_right_root,
    attention_momenta,
    expand_weights,
    expand_left,
    expand_right,
    expand_left_root,
    expand_right_root,
    expand_momenta,
    shrink_weights,
    down_left_statistics,
    shrink_right,
    shrink_left_root,
    shrink_right_root,
    shrink_momenta,
):
    micro_rows, width_bytes, model_width = byte_rows.shape
    head_count = bias_table.shape[1]
    at = Layout(head_count, micro_rows)
    parts, part, seq_size, sequence_position = at.parts, at.part, at.seq_size, at.seq
    row_len = width_bytes * seq_size
    tok_local = width_bytes // 2
    tok_row = row_len // 2
    hidden_width = shrink_weights.shape[1 - 1] * at.count
    heads = head_count // parts
    head_width = model_width // parts
    hidden_part = hidden_width // parts

    row_span = model_width // at.count
    hidden_span = hidden_width // at.count
    dp_size, sides, matrices = at.dp_size, at.sides, at.matrices

    slot = -(-head_width // 128) * 128
    slot_fill = ((0, 0), (0, 0), (0, 0), (0, slot - head_width))
    split = low(attention_weights[:3]).reshape(3, row_span, at.head_groups, head_width)
    split = jnp.pad(jnp.transpose(split, (2, 1, 0, 3)), slot_fill).reshape(
        at.head_groups, row_span, 3 * slot
    )
    token_segs = segments[:, 0::2]
    digits = jnp.stack([token_segs // 64, token_segs % 64], axis=1).astype(jnp.bfloat16)
    digits = jnp.pad(digits, ((0, 0), (0, row_span - 2), (0, 0)))
    split = jnp.concatenate(
        [
            jnp.broadcast_to(split[None], (micro_rows,) + split.shape),
            jnp.broadcast_to(
                low(attention_weights[3]), (micro_rows, at.head_groups, row_span, model_width)
            ),
            jnp.broadcast_to(
                digits[:, None], (micro_rows, at.head_groups, row_span, tok_local)
            ),
        ],
        axis=3,
    )
    split = at.to_units(split)

    halo = 8
    count = at.seq_size
    forward = [(i, i + 1) for i in range(count - 1)]
    backward = [(i + 1, i) for i in range(count - 1)]
    wide_bytes = jnp.concatenate(
        [
            lax.ppermute(byte_rows[:, width_bytes - halo :], "seq", forward),
            byte_rows,
            lax.ppermute(byte_rows[:, :halo], "seq", backward),
        ],
        axis=1,
    )
    place = (sequence_position * width_bytes - halo).reshape(1)
    tokens, normed = make_tokens(counts, place, wide_bytes, vectors, row_len, halo)
    grad_rows_out = cotangent.reshape(-1, model_width)

    (
        expand_weights_in,
        shrink_weights_in,
        normed,
    ) = lax.optimization_barrier(
        (expand_weights, shrink_weights, normed)
    )
    def columns(whole, begin, width):
        return lax.dynamic_slice_in_dim(whole, begin, width, 1)

    if at.groups == 1:
        rest = low(expand_weights_in).reshape(2, row_span, parts, hidden_part)
        rest = jnp.transpose(rest, (2, 1, 0, 3)).reshape(parts, row_span, 2 * hidden_part)
        rest = lax.all_to_all(after(rest, split), "dp", 0, 0, tiled=True)
        bits = [1 << i for i in reversed(range(seq_size.bit_length() - 1))]
        rest = [{0: item} for item in (rest, low(shrink_weights_in))]
        rest = at.gather_step(rest, bits[0])
    else:
        rest = jnp.concatenate(
            [low(expand_weights_in[0]), low(expand_weights_in[1])]
            + [low(shrink_weights_in).reshape(row_span, hidden_width)],
            axis=1,
        )
        rest = gather_all(rest)
        weights_expand = jnp.concatenate(
            [
                columns(rest, i * hidden_width + part * hidden_part, hidden_part)
                for i in range(2)
            ],
            axis=1,
        )
        weights_shrink = lax.dynamic_slice(
            rest,
            (part * (model_width // parts), 2 * hidden_width),
            (model_width // parts, hidden_width),
        ).reshape(hidden_part, model_width)

    digits = split[:, :2, 3 * slot + model_width :].astype(jnp.int32)
    seg_row = (digits[:, 0] * 64 + digits[:, 1]).reshape(tok_row)
    split = split[:, :, : 3 * slot + model_width].reshape(
        seq_size * row_span, 3 * slot + model_width
    )
    def early_block(i):
        if i == 2:
            feed = [low(shrink_right_root), down_to_feed(low(shrink_momenta), hidden_width)]
        elif i < 2:
            feed = [low(expand_left_root[i]), low(expand_momenta[i])]
        else:
            feed = [jnp.zeros((row_span, hidden_width + model_width), jnp.bfloat16)]
        return jnp.concatenate(
            [feed[0][:, :model_width], low(attention_momenta[i]), low(attention_right_root[i])]
            + [feed[-1][:, -hidden_width:]],
            axis=1,
        )

    early = jnp.stack([early_block(i) for i in range(matrices)])
    early_width = early.shape[2]

    early = at.exchange_owners(after(early, split)).reshape(-1, early_width)
    factor_one = rms_factor(tokens)

    normed_row, held = at.rows_to_units(
        normed.reshape(micro_rows, tok_local, model_width), [split, grad_rows_out]
    )
    if at.groups == 1:
        weights_qkv = at.gathered(held[0], part)
    else:
        weights_qkv = lax.all_gather(split, "dp", axis=0)
    weights_qkv = weights_qkv.reshape(model_width, 3 * slot + model_width)
    weights_qkv, weights_out = weights_qkv[:, : 3 * slot], weights_qkv[:, 3 * slot :]
    weights_out = jnp.pad(
        weights_out.reshape(at.head_groups, head_width, model_width),
        ((0, 0), (0, slot - head_width), (0, 0)),
    ).reshape(-1, model_width)
    qkv_row = low(dot(normed_row, weights_qkv, 1, 0))
    qkv_row, early = lax.optimization_barrier((qkv_row, early))
    early = at.gather_holders(early)
    if at.groups == 1:
        rest, qkv_row = lax.optimization_barrier((rest, qkv_row))
        for bit in bits[1:-1]:
            rest = at.gather_step(rest, bit)
    onehot = (buckets[:, None] == jnp.arange(bias_table.shape[0], dtype=jnp.int32)[None, :]).astype(
        jnp.float32
    )
    head_begin = (at.unit % at.head_groups) * heads
    part_table = lax.dynamic_slice_in_dim(bias_table, head_begin, heads, 1)
    bias_rel = jnp.einsum("xb,bh->hx", onehot, part_table, precision=HIGH_PRECISION)
    bias_rel = jnp.pad(bias_rel, ((0, 0), (0, 1)))
    seg_col = seg_row[:, None]
    seg_line = seg_row[None, :]
    tile = min(256, tok_row)
    attended_row, attended_f32, log_totals = attn_fwd(
        qkv_row, bias_rel, seg_col, seg_line, heads, head_width // heads, tile
    )
    if at.groups == 1:
        rest, attended_row = lax.optimization_barrier((rest, attended_row))
        rest = at.gather_step(rest, bits[-1])
    grad_pieces = after([held[1][key] for key in range(parts)], attended_row)
    grad_rows_all = jnp.concatenate(grad_pieces, axis=0)
    roots_in = after((expand_right_root, shrink_left_root, attention_left_root), normed_row)
    roots = jnp.stack(
        [low(roots_in[0][0]), low(roots_in[0][1]), low(roots_in[1])]
        + [jnp.zeros(shrink_left_root.shape, jnp.bfloat16)]
    )
    lefts = jnp.pad(
        low(roots_in[2]), ((0, 0), (0, 0), (0, hidden_width - model_width))
    )
    roots = at.exchange_owners(after(jnp.concatenate([roots, lefts], axis=1), attended_row))
    attended = at.exchange(attended_row.reshape(seq_size, tok_local, slot))
    attended = attended.reshape(
        micro_rows, at.head_groups, at.repeat, tok_local, slot
    )[:, :, 0]
    attended = jnp.transpose(attended, (0, 2, 1, 3)).reshape(micro_rows * tok_local, -1)
    resid = tokens + dot(attended, weights_out, 1, 0)
    factor_two = rms_factor(resid)
    normed_two = low(resid * factor_two * vectors[6])

    normed_two_all = at.near_parts(normed_two)
    if at.groups == 1:
        rest, normed_two_all = lax.optimization_barrier((rest, normed_two_all))
        weights_shrink = at.gathered(rest[1], at.seq).reshape(hidden_part, model_width)
        weights_expand = jnp.transpose(at.gathered(rest[0], at.seq), (1, 0, 2, 3)).reshape(model_width, -1)
    expanded = dot(normed_two_all, weights_expand, 1, 0)
    gate_pre = expanded[:, :hidden_part]
    upward = expanded[:, hidden_part:]
    activated, gelu_back = jax.vjp(functools.partial(jax.nn.gelu, approximate=True), gate_pre)
    hidden = low(activated * upward)
    grad_hidden = dot(grad_rows_all, weights_shrink, 1, 1)
    grad_gate_pre = low(gelu_back(grad_hidden * upward)[0])
    grad_upward = low(grad_hidden * activated)
    grad_normed_two = at.scatter_near(
        dot(grad_gate_pre, weights_expand[:, :hidden_part], 1, 1)
        + dot(grad_upward, weights_expand[:, hidden_part:], 1, 1)
    )
    grad_shrink_t = dot(grad_rows_all, hidden, 0, 0)
    grad_gate_w = dot(normed_two_all, grad_gate_pre, 0, 0)
    grad_up_w = dot(normed_two_all, grad_upward, 0, 0)

    feed_sum = [low(item) for item in (grad_gate_w, grad_up_w, grad_shrink_t)]
    feed_sum = jnp.stack(feed_sum + [jnp.zeros_like(feed_sum[0])])
    grad_normed_two = after(grad_normed_two, feed_sum)

    grad_resid_norm, grad_gain_two = norm_back(resid, factor_two, vectors[6], grad_normed_two)
    grad_resid = grad_rows_out.astype(jnp.float32) + grad_resid_norm
    grad_branch = low(grad_resid)
    grad_attended = low(dot(grad_branch, weights_out, 1, 1)).reshape(
        micro_rows, tok_local, at.head_groups, 1, slot
    )
    grad_attended = jnp.pad(
        jnp.transpose(grad_attended, (0, 2, 3, 1, 4)),
        ((0, 0), (0, 0), (0, at.repeat - 1), (0, 0), (0, 0)),
    )
    grad_attended, early, roots = lax.optimization_barrier((grad_attended, early, roots))
    grad_branch = after(grad_branch, grad_attended)
    grad_out = at.scatter(
        low(
            dot(attended, grad_branch, 0, 0)
            .reshape(at.head_groups, slot, model_width)[:, :head_width]
            .reshape(parts, -1, model_width)
        ),
        "dp",
        at.part,
    )
    grad_attended_row = at.exchange(
        grad_attended.reshape(seq_size, tok_local, slot)
    ).reshape(tok_row, slot)
    feed_sum = at.scatter_step(feed_sum, "seq", at.seq, 1)
    feed_sum, grad_attended_row = lax.optimization_barrier((feed_sum, grad_attended_row))
    feed_sum = at.scatter_step(feed_sum, "seq", at.seq, 2)

    grad_qkv_row, grad_bias = attn_bwd(
        qkv_row,
        grad_attended_row,
        attended_f32,
        log_totals,
        bias_rel,
        seg_col,
        seg_line,
        heads,
        tile,
    )
    grad_normed_part = low(dot(grad_qkv_row, weights_qkv, 1, 1))
    grad_normed_part = at.fold_units(grad_normed_part)
    feed_sum, grad_normed_part = lax.optimization_barrier((feed_sum, grad_normed_part))
    feed_sum = feed_sum.reshape(model_width, hidden_part)
    bit = matrices
    got = low(feed_sum)
    while bit < seq_size:
        got = at.flip(low(feed_sum), "seq", bit)
        bit *= 2
        if bit < seq_size:
            feed_sum = low(feed_sum.astype(jnp.float32) + got.astype(jnp.float32))
    grad_out = after(grad_out, grad_qkv_row)
    grad_out = jnp.transpose(
        grad_out.reshape(-1, at.head_groups, head_width), (1, 0, 2)
    )
    grad_out = at.scatter_heads(jnp.pad(grad_out, ((0, 0), (0, 0), (0, slot - head_width))))
    grad_normed_part, grad_qkv_row = lax.optimization_barrier((grad_normed_part, grad_qkv_row))
    grad_normed_part = at.fold_halves(grad_normed_part)
    grad_qkv = low(dot(normed_row, grad_qkv_row, 0, 0))
    grad_normed_part, grad_qkv, grad_out = lax.optimization_barrier(
        (grad_normed_part, grad_qkv, grad_out)
    )
    grad_normed = at.fold_rows(grad_normed_part).reshape(-1, model_width)

    side_rows = model_width // (parts * sides)
    sums = at.scatter(grad_qkv.reshape(parts, -1, 3 * slot), "dp", at.part)
    sums = low(jnp.concatenate([sums, grad_out], axis=1))
    sums = jnp.transpose(sums.reshape(sides, side_rows, matrices, slot), (0, 2, 1, 3))
    sums = sums.reshape(seq_size, side_rows, slot)

    roots = after(roots, grad_qkv_row)
    feed_right_rows = roots[:, :hidden_span].reshape(-1, hidden_width)
    attention_left_rows = roots[:, hidden_span:, :model_width].reshape(-1, model_width)
    early = after(early, grad_qkv)
    feed_left_whole = early[:, :model_width]
    attention_old = early[:, model_width : 2 * model_width]
    attention_right_whole = early[:, 2 * model_width : 3 * model_width]
    feed_old = early[:, 3 * model_width :]
    is_shrink = at.matrix == 2
    feed_start = MOMENTUM * jnp.where(
        is_shrink,
        dot(
            feed_to_down(
                feed_old.reshape(at.count, row_span, hidden_width), model_width
            ).reshape(hidden_width, model_width),
            feed_right_rows,
            0,
            1,
        ),
        dot(feed_old, feed_right_rows, 1, 1),
    )
    attention_start = MOMENTUM * dot(attention_left_rows, attention_old, 1, 0)
    part_grad = jnp.einsum("xb,hx->bh", onehot, grad_bias[:, :-1], precision=HIGH_PRECISION)
    grad_normed, feed_start, attention_start, got, part_grad, sums = lax.optimization_barrier(
        (grad_normed, feed_start, attention_start, got, part_grad, sums)
    )

    grad_tokens_norm, grad_gain_one = norm_back(tokens, factor_one, vectors[5], grad_normed)
    grad_tokens = (grad_resid + grad_tokens_norm).reshape(micro_rows, tok_local, model_width)
    if seq_size > matrices:
        feed_sum = low(feed_sum.astype(jnp.float32) + got.astype(jnp.float32))
    edge = halo // 2
    wide_grads = jnp.concatenate(
        [
            lax.ppermute(grad_tokens[:, tok_local - edge :], "seq", forward),
            grad_tokens,
            lax.ppermute(grad_tokens[:, :edge], "seq", backward),
        ],
        axis=1,
    )
    sums = at.exchange(after(sums, grad_tokens))
    input_grads, grad_taps = bytes_back(counts, place, wide_bytes, wide_grads, vectors, row_len, halo)
    feed_sum = {0: low(at.sum_groups(feed_sum.astype(jnp.float32)))}
    bit = parts // 2
    if bit:
        feed_sum[bit], grad_taps, sums = lax.optimization_barrier(
            (at.flip(feed_sum[0], "dp", bit), grad_taps, sums)
        )
        bit //= 2
    while bit:
        for key in list(feed_sum):
            feed_sum[key | bit] = at.flip(feed_sum[key], "dp", bit)
        bit //= 2
    sums = sums.reshape(
        micro_rows, at.head_groups, at.repeat, side_rows, slot
    )[..., :head_width]
    sums = jnp.sum(sums.astype(jnp.float32), axis=(0, 2))
    sums = at.sum_groups(jnp.transpose(sums, (1, 0, 2)).reshape(side_rows, model_width))
    full_attention = at.gather_members(low(sums)).reshape(model_width, model_width)
    grad_vectors = jnp.concatenate(
        [grad_taps[:5], grad_gain_one[None], grad_gain_two[None]], axis=0
    )
    grad_table = lax.dynamic_update_slice_in_dim(
        jnp.zeros_like(bias_table), part_grad, head_begin, 1
    )
    small = jnp.pad(grad_table.reshape(-1), (0, model_width - grad_table.size))
    small = low(jnp.concatenate([grad_vectors, small[None]], axis=0))

    member_rows = matrices * row_span
    member_cols = matrices * hidden_span
    def to_owners(strips):
        strips = strips.reshape(strips.shape[0], matrices, row_span, strips.shape[2])
        return jnp.transpose(strips, (1, 2, 0, 3)).reshape(matrices, row_span, hidden_width)

    def down_to_owners(rows):
        return down_to_feed(rows.reshape(matrices, hidden_span, model_width), hidden_width)

    whole_tiles = member_rows % 16 == 0 and member_cols % 128 == 0
    if whole_tiles:
        feed_right, feed_left, feed_step, feed_step_t, feed_cols, feed_rows = feed_update(
            jnp.stack([at.part, at.member]),
            [feed_sum[key] for key in range(parts)],
            feed_right_rows,
            feed_start,
            early,
            member_rows,
        )
    else:
        full_feed = at.gathered(feed_sum, at.part)
        feed_rows = lax.dynamic_slice_in_dim(full_feed, at.member * member_rows, member_rows, 1)
        begin = at.member * member_cols
        feed_cols = lax.dynamic_slice(
            full_feed, (begin // hidden_part, 0, begin % hidden_part), (1, model_width, member_cols)
        )[0].T
        feed_product = low(
            feed_start
            + sum(
                dot(full_feed[i], columns(feed_right_rows, i * hidden_part, hidden_part), 1, 1)
                for i in range(parts)
            )
        )
        feed_step = low(dot(feed_left_whole, feed_product, 1, 0))
        feed_right = jnp.concatenate(
            [low(dot(feed_cols, full_feed[i], 1, 0)) for i in range(parts)], axis=1
        )
        feed_left = low(sum(dot(feed_rows[i], full_feed[i], 1, 1) for i in range(parts)))
        feed_step_t = feed_step.T
        feed_rows = jnp.transpose(feed_rows, (1, 0, 2)).reshape(member_rows, hidden_width)
    shrink_out = low(dot(after(hidden, feed_step), weights_shrink, 1, 0))
    shrink_out = at.scatter_near(shrink_out)
    layer_output = low(resid + shrink_out).reshape(micro_rows, tok_local, model_width)

    moved = feed_step.reshape(-1, member_rows, member_cols)
    members = moved.shape[0]
    moved = at.exchange_holders(
        jnp.concatenate(
            [
                moved,
                jnp.broadcast_to(
                    small.reshape(1, -1, member_cols),
                    (members, small.size // member_cols, member_cols),
                ),
            ],
            axis=1,
        )
    )
    small = jnp.sum(moved[:, member_rows:].astype(jnp.float32), axis=0).reshape(small.shape)
    moved = moved[:, :member_rows]

    feed_sums = at.exchange_owners(
        jnp.concatenate(
            [
                feed_right.reshape(matrices, hidden_span, hidden_width),
                as_width(feed_left.reshape(matrices, row_span, model_width), hidden_width),
            ],
            axis=1,
        )
    )
    if whole_tiles:
        attention_parts = attention_update(
            at.member.reshape(1),
            after(full_attention, moved),
            attention_left_rows,
            attention_start,
            early,
        )
    else:
        rows = lax.dynamic_slice_in_dim(full_attention, at.member * member_rows, member_rows, 0)
        cols = columns(full_attention, at.member * member_rows, member_rows)
        attention_product = low(attention_start + dot(attention_left_rows, full_attention, 1, 0))
        attention_parts = [
            low(dot(rows, full_attention, 1, 1)),
            low(dot(cols, full_attention, 0, 0)),
            low(dot(attention_product, attention_right_whole, 1, 0)),
            rows,
        ]
    attention_out = jnp.concatenate(
        [item.reshape(matrices, row_span, model_width) for item in attention_parts], axis=1
    )
    left_rows = -(-row_span * model_width // hidden_width)
    is_down = at.matrix == 2
    feed_pair = jnp.concatenate(
        [
            jnp.where(is_down, down_to_owners(feed_step_t), to_owners(moved)),
            jnp.where(
                is_down,
                down_to_owners(feed_cols),
                feed_rows.reshape(matrices, row_span, hidden_width),
            ),
            as_width(jnp.broadcast_to(low(small), (matrices,) + small.shape), hidden_width),
            as_width(attention_out, hidden_width),
        ],
        axis=1,
    )
    feed_pair = at.exchange_owners(after(feed_pair, feed_sums))
    small_rows = -(-small.size // hidden_width)
    attention_out = of_width(
        feed_pair[:, 2 * row_span + small_rows :], 4 * row_span, model_width
    )
    small = of_width(
        feed_pair[:, 2 * row_span : 2 * row_span + small_rows], small.shape[0], small.shape[1]
    )
    small = jnp.sum(small.astype(jnp.float32), axis=0)
    sum_vectors = small[:-1]
    sum_table = small[-1, : grad_table.size].reshape(grad_table.shape)
    total_tokens = micro_rows * at.dp_size * tok_row
    small_rate = SMALL_RATE / math.sqrt(total_tokens)
    vector_momenta_new = MOMENTUM * vector_momenta + sum_vectors
    vectors_new = vectors - small_rate * vector_momenta_new
    table_momenta_new = MOMENTUM * table_momenta + sum_table
    table_new = bias_table - small_rate * table_momenta_new

    sum_left, sum_right, step, grads = [
        attention_out[:, i * row_span : (i + 1) * row_span].astype(jnp.float32) for i in range(4)
    ]

    def statistics(old, increment):
        return STAT_DECAY * old + (1.0 - STAT_DECAY) * increment

    attention_new = attention_weights - MATRIX_RATE * step
    attention_left_new = statistics(attention_left, sum_left)
    attention_right_new = statistics(attention_right, sum_right)
    attention_mom_new = MOMENTUM * attention_momenta + grads

    def wide(block):
        return block.astype(jnp.float32)

    step, grads = feed_pair[:, :row_span], feed_pair[:, row_span : 2 * row_span]
    sum_left = of_width(feed_sums[:, hidden_span : hidden_span + left_rows], row_span, model_width)
    expand_new = expand_weights - MATRIX_RATE * wide(step[:2])
    expand_left_new = statistics(expand_left, wide(sum_left[:2]))
    expand_right_new = statistics(expand_right, wide(feed_sums[:2, :hidden_span]))
    expand_mom_new = MOMENTUM * expand_momenta + wide(grads[:2])
    shrink_new = shrink_weights - MATRIX_RATE * wide(feed_to_down(step[2], model_width))
    shrink_left_new = statistics(down_left_statistics, wide(feed_sums[2, :hidden_span]))
    shrink_right_new = statistics(shrink_right, wide(sum_left[2]))
    shrink_mom_new = MOMENTUM * shrink_momenta + wide(feed_to_down(grads[2], model_width))
    return (
        layer_output,
        input_grads,
        vectors_new,
        vector_momenta_new,
        table_new,
        table_momenta_new,
        attention_new,
        attention_left_new,
        attention_right_new,
        attention_mom_new,
        low(attention_new),
        expand_new,
        expand_left_new,
        expand_right_new,
        expand_mom_new,
        low(expand_new),
        shrink_new,
        shrink_left_new,
        shrink_right_new,
        shrink_mom_new,
        low(shrink_new),
    )


def solution(mesh):
    row = P("dp", "seq", None)
    stack = P(None, BOTH, None)
    flat = P(BOTH, None)
    return jax.shard_map(
        per_device,
        mesh=mesh,
        in_specs=(row, P("dp", "seq"), P("dp"), P(), row)
        + (P(),) * 4
        + (stack,) * 12
        + (flat,) * 6,
        out_specs=(row, row) + (P(),) * 4 + (stack,) * 10 + (flat,) * 5,
        check_vma=False,
    )
```

```python
import functools
import math

import jax
import jax.numpy as jnp
from jax import lax
from jax.experimental import pallas as pl
from jax.experimental.pallas import tpu as pltpu
from jax.sharding import PartitionSpec as P

EPSILON = 1e-06
STAT_DECAY = 0.95
MOMENTUM = 0.9
MATRIX_RATE = 0.1
SMALL_RATE = 0.1
MASKED = -1e30
HIGH_PRECISION = lax.Precision.HIGHEST
BOTH = ("dp", "seq")


def fill_bias(brel_ref, bias_sc, heads, tile):
    span = brel_ref.shape[1]
    rows = lax.broadcasted_iota(jnp.int32, (8, span), 0)
    for h in range(heads):
        wide = jnp.broadcast_to(brel_ref[h:h + 1, :], (8, span))
        first = wide
        for i in range(8):
            first = jnp.where(rows == i, pltpu.roll(wide, span - (tile - 1) + i, 1), first)
        bias_sc[h, 0:8, :] = first
        size = 8
        while size < tile:
            bias_sc[h, size:2 * size, :] = pltpu.roll(bias_sc[h, 0:size, :], size, 1)
            size *= 2

def attn_fwd_kernel(heads, tile, qkv_ref, brel_ref, segc_ref, segr_ref, out_ref, outf_ref, lse_ref, bias_sc):
    step = pl.program_id(0)
    length = qkv_ref.shape[0]
    width = qkv_ref.shape[1] // 3
    dh = outf_ref.shape[1] // heads

    @pl.when(step == 0)
    def _():
        fill_bias(brel_ref, bias_sc, heads, tile)

    begin = pl.multiple_of(step * tile, tile)
    offset = pl.multiple_of(length - tile - begin, 128)
    same = segc_ref[...] == segr_ref[...]
    lanes = lax.broadcasted_iota(jnp.int32, (tile, 128), 1)
    lse_all = jnp.zeros((tile, 128), jnp.float32)
    outs = []
    for h in range(heads):
        q = qkv_ref[pl.ds(begin, tile), h * dh:(h + 1) * dh]
        k = qkv_ref[:, width + h * dh:width + (h + 1) * dh]
        v = qkv_ref[:, 2 * width + h * dh:2 * width + (h + 1) * dh]
        scores = lax.dot_general(q, k, (((1,), (1,)), ((), ())), preferred_element_type=jnp.float32)
        scores = jnp.where(same, scores + bias_sc[h, :, pl.ds(offset, length)], MASKED)
        top = jnp.max(scores, axis=1, keepdims=True)
        probs = jnp.exp(scores - top)
        total = jnp.sum(probs, axis=1, keepdims=True)
        out = lax.dot_general(probs.astype(jnp.bfloat16), v, (((1,), (0,)), ((), ())), preferred_element_type=jnp.float32)
        outs.append(out / total)
        lse_all = jnp.where(lanes == h, top + jnp.log(total), lse_all)
    joined = jnp.concatenate(outs, axis=1)
    outf_ref[...] = joined
    fill = out_ref.shape[1] - joined.shape[1]
    if fill:
        joined = jnp.concatenate([joined, jnp.zeros((tile, fill), jnp.float32)], axis=1)
    out_ref[...] = joined.astype(jnp.bfloat16)
    lse_ref[...] = lse_all

def attn_fwd(qkv, brel, segc, segr, heads, dh, tile=128):
    length = qkv.shape[0]
    width = heads * dh
    full = lambda s: pl.BlockSpec(s, lambda i: (0,) * len(s))
    rowb = lambda w: pl.BlockSpec((tile, w), lambda i: (i, 0))
    return pl.pallas_call(
        functools.partial(attn_fwd_kernel, heads, tile),
        grid=(length // tile,),
        in_specs=[full(qkv.shape), full(brel.shape), rowb(1), full(segr.shape)],
        out_specs=[rowb(qkv.shape[1] // 3), rowb(width), rowb(128)],
        out_shape=[jax.ShapeDtypeStruct((length, qkv.shape[1] // 3), jnp.bfloat16), jax.ShapeDtypeStruct((length, width), jnp.float32), jax.ShapeDtypeStruct((length, 128), jnp.float32)],
        scratch_shapes=[pltpu.VMEM((heads, tile, 2 * length), jnp.float32)],
        compiler_params=pltpu.CompilerParams(vmem_limit_bytes=48 * 2**20),
        cost_estimate=pl.CostEstimate(flops=4 * length * length * width, bytes_accessed=6 * length * width * 2, transcendentals=heads * length * length),
    )(qkv, brel, segc, segr)

def attn_bwd_kernel(heads, tile, trans, qkv_ref, grad_ref, outf_ref, lse_ref, brel_ref, segc_ref, segr_ref, dqkv_ref, gb_ref, bias_sc, gb_sc, dk_sc, dv_sc):
    step = pl.program_id(0)
    length = qkv_ref.shape[0]
    width = qkv_ref.shape[1] // 3
    dh = outf_ref.shape[1] // heads

    @pl.when(step == 0)
    def _():
        fill_bias(brel_ref, bias_sc, heads, tile)
        gb_sc[...] = jnp.zeros_like(gb_sc)
        dk_sc[...] = jnp.zeros_like(dk_sc)
        dv_sc[...] = jnp.zeros_like(dv_sc)

    begin = pl.multiple_of(step * tile, tile)
    offset = pl.multiple_of(length - tile - begin, 128)
    same = segc_ref[...] == segr_ref[...]
    dqs = []
    for h in range(heads):
        q = qkv_ref[pl.ds(begin, tile), h * dh:(h + 1) * dh]
        k = qkv_ref[:, width + h * dh:width + (h + 1) * dh]
        v = qkv_ref[:, 2 * width + h * dh:2 * width + (h + 1) * dh]
        g = grad_ref[:, h * dh:(h + 1) * dh]
        delta = jnp.sum(g.astype(jnp.float32) * outf_ref[:, h * dh:(h + 1) * dh], axis=1, keepdims=True)
        lse = lse_ref[:, h:h + 1]
        scores = lax.dot_general(q, k, (((1,), (1,)), ((), ())), preferred_element_type=jnp.float32)
        scores = jnp.where(same, scores + bias_sc[h, :, pl.ds(offset, length)], MASKED)
        probs = jnp.exp(scores - lse)
        gp = lax.dot_general(g, v, (((1,), (1,)), ((), ())), preferred_element_type=jnp.float32)
        gs = (probs * (gp - delta))
        gsb = gs.astype(jnp.bfloat16)
        pb = probs.astype(jnp.bfloat16)
        gb_sc[h, :, pl.ds(offset, length)] += gsb.astype(jnp.float32)
        dqs.append(lax.dot_general(gsb, k, (((1,), (0,)), ((), ())), preferred_element_type=jnp.float32))
        if trans:
            dk_sc[h] += lax.dot_general(q, gsb, (((0,), (0,)), ((), ())), preferred_element_type=jnp.float32)
            dv_sc[h] += lax.dot_general(g, pb, (((0,), (0,)), ((), ())), preferred_element_type=jnp.float32)
        else:
            dk_sc[h] += lax.dot_general(gsb, q, (((0,), (0,)), ((), ())), preferred_element_type=jnp.float32)
            dv_sc[h] += lax.dot_general(pb, g, (((0,), (0,)), ((), ())), preferred_element_type=jnp.float32)
    fill = width - heads * dh

    def slot(parts):
        rows = parts[0].shape[0]
        filled = parts + ([jnp.zeros((rows, fill), jnp.float32)] if fill else [])
        return jnp.concatenate(filled, axis=1).astype(jnp.bfloat16)

    dqkv_ref[pl.ds(begin, tile), 0:width] = slot(dqs)

    @pl.when(step == pl.num_programs(0) - 1)
    def _():
        turn = (lambda x: x.T) if trans else (lambda x: x)
        dqkv_ref[:, width:2 * width] = slot([turn(dk_sc[h]) for h in range(heads)])
        dqkv_ref[:, 2 * width:3 * width] = slot([turn(dv_sc[h]) for h in range(heads)])
        span = gb_sc.shape[2]
        rows = lax.broadcasted_iota(jnp.int32, (8, span), 0)
        for h in range(heads):
            size = tile // 2
            part = gb_sc[h]
            while size >= 8:
                part = part[:size] + pltpu.roll(part[size:], span - size, 1)
                size //= 2
            line = jnp.zeros((1, span), jnp.float32)
            for i in range(8):
                line = line + jnp.sum(jnp.where(rows == i, pltpu.roll(part, (tile - 1 - i) % span, 1), 0.0), axis=0, keepdims=True)
            gb_ref[h:h + 1, :] = line

def attn_bwd(qkv, grad, outf, lse, brel, segc, segr, heads, tile=128, trans=True):
    length, width = outf.shape
    dh = width // heads
    full = lambda s: pl.BlockSpec(s, lambda i: (0,) * len(s))
    rowb = lambda w: pl.BlockSpec((tile, w), lambda i: (i, 0))
    acc = (heads, dh, length) if trans else (heads, length, dh)
    return pl.pallas_call(
        functools.partial(attn_bwd_kernel, heads, tile, trans),
        grid=(length // tile,),
        in_specs=[full(qkv.shape), rowb(grad.shape[1]), rowb(width), rowb(128), full(brel.shape), rowb(1), full(segr.shape)],
        out_specs=[full(qkv.shape), full(brel.shape)],
        out_shape=[jax.ShapeDtypeStruct(qkv.shape, jnp.bfloat16), jax.ShapeDtypeStruct(brel.shape, jnp.float32)],
        scratch_shapes=[pltpu.VMEM((heads, tile, 2 * length), jnp.float32), pltpu.VMEM((heads, tile, 2 * length), jnp.float32), pltpu.VMEM(acc, jnp.float32), pltpu.VMEM(acc, jnp.float32)],
        compiler_params=pltpu.CompilerParams(vmem_limit_bytes=56 * 2**20),
        cost_estimate=pl.CostEstimate(flops=10 * length * length * width, bytes_accessed=12 * length * width * 2, transcendentals=heads * length * length),
    )(qkv, grad, outf, lse, brel, segc, segr)

def byte_window(bytes_ref, counts_ref, taps, begin, span, place, row_len):
    row = pl.program_id(0)
    positions = place + begin + lax.broadcasted_iota(jnp.int32, (span, 1), 0)
    window = bytes_ref[0, pl.ds(begin, span), :].astype(jnp.float32)
    valid = (positions >= 0) & (positions < counts_ref[row])
    embedded = jnp.where(valid, window, 0.0)
    conv = embedded * taps[3:4]
    for tap in range(3):
        conv = conv + pltpu.roll(embedded, 3 - tap, 0) * taps[tap : tap + 1]
    conv = jnp.where(positions < row_len, conv, 0.0)
    return positions, embedded, conv


def block_sums(values, positions, span):
    ahead = [None] + [pltpu.roll(values, span - i, 0) for i in (1, 2)]
    behind = [None] + [pltpu.roll(values, i, 0) for i in (1, 2)]
    two = values + jnp.where(positions % 2 == 0, ahead[1], behind[1])
    four = two + jnp.where(
        positions % 4 < 2, pltpu.roll(two, span - 2, 0), pltpu.roll(two, 2, 0)
    )
    phase = (positions + 9) % 3
    three = (
        values
        + jnp.where(phase != 2, ahead[1], behind[2])
        + jnp.where(phase == 0, ahead[2], behind[1])
    )
    return two, three, four


def three_sum(values, positions, span):
    phase = (positions + 9) % 3
    return (
        values
        + jnp.where(phase != 2, pltpu.roll(values, span - 1, 0), pltpu.roll(values, 2, 0))
        + jnp.where(phase == 0, pltpu.roll(values, span - 2, 0), pltpu.roll(values, 1, 0))
    )


def three_share(positions, row_len):
    left = row_len - (positions - (positions + 9) % 3)
    return jnp.where(left >= 3, 1.0 / 3.0, jnp.where(left == 2, 0.5, 1.0))


def block_means(conv, positions, span, row_len):
    two, three, four = block_sums(conv, positions, span)
    return [conv, two * 0.5, three * three_share(positions, row_len), four * 0.25]


def size_softmax(pooled, score_row):
    scores = [jnp.sum(item * score_row, axis=1, keepdims=True) for item in pooled]
    top = functools.reduce(jnp.maximum, scores)
    powers = [jnp.exp(item - top) for item in scores]
    total = sum(powers)
    return [item / total for item in powers]


def tokens_kernel(row_len, halo, chunk, counts_ref, place_ref, bytes_ref, vectors_ref, tokens_ref, normed_ref, pair_ref):
    span = chunk + 2 * halo
    taps = vectors_ref[0:4, :]

    def visit(index, carry):
        begin = pl.multiple_of(index * chunk, chunk)
        positions, embedded, conv = byte_window(
            bytes_ref, counts_ref, taps, begin, span, place_ref[0], row_len
        )
        pooled = block_means(conv, positions, span, row_len)
        pooled = [item[halo : halo + chunk] for item in pooled]
        weights = size_softmax(pooled, vectors_ref[4:5, :])
        blended = sum(weight * item for weight, item in zip(weights, pooled))
        half = chunk // 2
        halves = []
        for lane in range(pair_ref.shape[0]):
            pair_ref[lane] = blended[:, lane * 128 : (lane + 1) * 128]
            halves.append(
                pair_ref[lane, pl.Slice(0, half, 2), :] + pair_ref[lane, pl.Slice(1, half, 2), :]
            )
        tokens = 0.5 * jnp.concatenate(halves, axis=1)
        factor = lax.rsqrt(jnp.mean(tokens * tokens, axis=1, keepdims=True) + EPSILON)
        rows = pl.ds(pl.multiple_of(index * half, half), half)
        tokens_ref[rows, :] = tokens
        normed_ref[rows, :] = (tokens * factor * vectors_ref[5:6, :]).astype(jnp.bfloat16)
        return carry

    lax.fori_loop(0, (bytes_ref.shape[1] - 2 * halo) // chunk, visit, 0)


def make_tokens(counts, place, wide_bytes, vectors, row_len, halo=8, chunk=128):
    micro, wide, width = wide_bytes.shape
    count = (wide - 2 * halo) // 2
    return pl.pallas_call(
        functools.partial(tokens_kernel, row_len, halo, chunk),
        grid=(micro,),
        in_specs=[
            pl.BlockSpec(memory_space=pltpu.SMEM),
            pl.BlockSpec(memory_space=pltpu.SMEM),
            pl.BlockSpec((1, wide, width), lambda i: (i, 0, 0)),
            pl.BlockSpec(vectors.shape, lambda i: (0, 0)),
        ],
        out_specs=[pl.BlockSpec((count, width), lambda i: (i, 0))] * 2,
        out_shape=[
            jax.ShapeDtypeStruct((micro * count, width), jnp.float32),
            jax.ShapeDtypeStruct((micro * count, width), jnp.bfloat16),
        ],
        scratch_shapes=[pltpu.VMEM((width // 128, chunk, 128), jnp.float32)],
        compiler_params=pltpu.CompilerParams(vmem_limit_bytes=32 * 2**20),
        cost_estimate=pl.CostEstimate(
            flops=60 * micro * wide * width, bytes_accessed=6 * micro * wide * width, transcendentals=0
        ),
    )(counts, place, wide_bytes, vectors)


def bytes_kernel(row_len, halo, chunk, counts_ref, place_ref, bytes_ref, grads_ref, vectors_ref, out_ref, sums_ref, spread_ref, parts_ref):
    row = pl.program_id(0)
    span = chunk + 2 * halo
    taps = vectors_ref[0:4, :]
    score_row = vectors_ref[4:5, :]
    half = grads_ref.shape[1]
    for lane in range(spread_ref.shape[0]):
        lanes = grads_ref[0, :, lane * 128 : (lane + 1) * 128] * 0.5
        spread_ref[lane, pl.Slice(0, half, 2), :] = lanes
        spread_ref[lane, pl.Slice(1, half, 2), :] = lanes

    @pl.when(row == 0)
    def _():
        parts_ref[...] = jnp.zeros_like(parts_ref)

    def visit(index, carry):
        begin = pl.multiple_of(index * chunk, chunk)
        positions, embedded, conv = byte_window(
            bytes_ref, counts_ref, taps, begin, span, place_ref[0], row_len
        )
        pooled = block_means(conv, positions, span, row_len)
        weights = size_softmax(pooled, score_row)
        grad = jnp.concatenate(
            [spread_ref[lane, pl.ds(begin, span), :] for lane in range(spread_ref.shape[0])], axis=1
        )
        along = [jnp.sum(grad * item, axis=1, keepdims=True) for item in pooled]
        mean = sum(weight * item for weight, item in zip(weights, along))
        sizes = [weight * (item - mean) for weight, item in zip(weights, along)]
        first, second, third, fourth = [
            weight * grad + size * score_row for weight, size in zip(weights, sizes)
        ]
        even = positions % 2 == 0
        pair = 0.5 * second + 0.25 * fourth
        fours = 0.25 * fourth
        pair = pair + jnp.where(even, pltpu.roll(pair, span - 1, 0), pltpu.roll(pair, 1, 0))
        fours = fours + jnp.where(even, pltpu.roll(fours, span - 1, 0), pltpu.roll(fours, 1, 0))
        fours = jnp.where(
            positions % 4 < 2, pltpu.roll(fours, span - 2, 0), pltpu.roll(fours, 2, 0)
        )
        share = three_share(positions, row_len)
        grad_conv = first + pair + fours + three_sum(third, positions, span) * share
        grad_conv = jnp.where((positions < row_len) & (positions >= 0), grad_conv, 0.0)
        back = grad_conv * taps[3:4]
        for tap in range(3):
            back = back + pltpu.roll(grad_conv, span - (3 - tap), 0) * taps[tap : tap + 1]
        own = slice(halo, halo + chunk)
        back = jnp.where(positions < counts_ref[row], back, 0.0)
        out_ref[0, pl.ds(begin, chunk), :] = back[own]

        def fold(values):
            return jnp.sum(values.reshape(chunk // 8, 8, values.shape[1]), axis=0)

        for tap in range(4):
            beside = embedded if tap == 3 else pltpu.roll(embedded, 3 - tap, 0)
            parts_ref[tap] += fold((grad_conv * beside)[own])
        parts_ref[4] += fold(sum(size * item for size, item in zip(sizes, pooled))[own])
        return carry

    lax.fori_loop(0, (bytes_ref.shape[1] - 2 * halo) // chunk, visit, 0)

    @pl.when(row == pl.num_programs(0) - 1)
    def _():
        sums_ref[...] = jnp.zeros_like(sums_ref)
        for item in range(5):
            sums_ref[item : item + 1, :] = jnp.sum(parts_ref[item], axis=0, keepdims=True)


def bytes_back(counts, place, wide_bytes, wide_grads, vectors, row_len, halo=8, chunk=128):
    micro, wide, width = wide_bytes.shape
    count = wide - 2 * halo
    return pl.pallas_call(
        functools.partial(bytes_kernel, row_len, halo, chunk),
        grid=(micro,),
        in_specs=[
            pl.BlockSpec(memory_space=pltpu.SMEM),
            pl.BlockSpec(memory_space=pltpu.SMEM),
            pl.BlockSpec((1, wide, width), lambda i: (i, 0, 0)),
            pl.BlockSpec((1, wide // 2, width), lambda i: (i, 0, 0)),
            pl.BlockSpec(vectors.shape, lambda i: (0, 0)),
        ],
        out_specs=[
            pl.BlockSpec((1, count, width), lambda i: (i, 0, 0)),
            pl.BlockSpec((8, width), lambda i: (0, 0)),
        ],
        out_shape=[
            jax.ShapeDtypeStruct((micro, count, width), jnp.float32),
            jax.ShapeDtypeStruct((8, width), jnp.float32),
        ],
        scratch_shapes=[
            pltpu.VMEM((width // 128, wide, 128), jnp.float32),
            pltpu.VMEM((5, 8, width), jnp.float32),
        ],
        compiler_params=pltpu.CompilerParams(vmem_limit_bytes=32 * 2**20),
        cost_estimate=pl.CostEstimate(
            flops=150 * micro * wide * width, bytes_accessed=8 * micro * wide * width, transcendentals=0
        ),
    )(counts, place, wide_bytes, wide_grads, vectors)

def low(values):
    return values.astype(jnp.bfloat16)


def dot(left_side, right_side, left_dim, right_dim):
    return lax.dot_general(
        left_side,
        right_side,
        (((left_dim,), (right_dim,)), ((), ())),
        preferred_element_type=jnp.float32,
    )


def rms_factor(values):
    return lax.rsqrt(jnp.mean(values * values, axis=-1, keepdims=True) + EPSILON)


def norm_back(values, factor, gain_row, grad_out):
    scaled = grad_out * gain_row
    grad_gain = jnp.sum(grad_out * values * factor, axis=0)
    inner_mean = jnp.mean(scaled * values, axis=-1, keepdims=True)
    return (factor * (scaled - values * inner_mean * factor * factor), grad_gain)


def feed_kernel(parts, place_ref, *refs):
    pieces = refs[:parts]
    right_ref, start_ref, left_ref = refs[parts : parts + 3]
    sum_right_ref, sum_left_ref, step_ref, step_t_ref, cols_ref, rows_ref = refs[parts + 3 : -1]
    whole_ref = refs[-1]
    width = pieces[0].shape[1]
    for key, piece in enumerate(pieces):
        begin = pl.multiple_of((place_ref[0] ^ key) * width, width)
        whole_ref[:, pl.ds(begin, width)] = piece[...]
    member = place_ref[1]
    count = cols_ref.shape[0]
    cols = whole_ref[:, pl.ds(pl.multiple_of(member * count, count), count)].T
    cols_ref[...] = cols
    count = rows_ref.shape[0]
    rows = whole_ref[pl.ds(pl.multiple_of(member * count, count), count), :]
    rows_ref[...] = rows
    product = start_ref[...]
    for begin in range(0, whole_ref.shape[1], width):
        block = whole_ref[:, begin : begin + width]
        sum_right_ref[:, begin : begin + width] = lax.dot_general(
            cols, block, (((1,), (0,)), ((), ())), preferred_element_type=jnp.float32
        ).astype(jnp.bfloat16)
        product = product + lax.dot_general(
            block,
            right_ref[:, begin : begin + width],
            (((1,), (1,)), ((), ())),
            preferred_element_type=jnp.float32,
        )
    sum_left_ref[...] = lax.dot_general(
        rows, whole_ref[...], (((1,), (1,)), ((), ())), preferred_element_type=jnp.float32
    ).astype(jnp.bfloat16)
    step = lax.dot_general(
        left_ref[...],
        product.astype(jnp.bfloat16),
        (((1,), (0,)), ((), ())),
        preferred_element_type=jnp.float32,
    )
    step_ref[...] = step.astype(jnp.bfloat16)
    step_t_ref[...] = step.T.astype(jnp.bfloat16)


def feed_update(place, pieces, right_rows, start, left_whole, member_rows):
    rows, width = pieces[0].shape
    cols = right_rows.shape[0]
    total = width * len(pieces)
    vmem = pl.BlockSpec(memory_space=pltpu.VMEM)
    shapes = [(cols, total), (member_rows, rows), (rows, cols), (cols, rows), (cols, rows)]
    shapes.append((member_rows, total))
    return pl.pallas_call(
        functools.partial(feed_kernel, len(pieces)),
        grid=(1,),
        in_specs=[pl.BlockSpec(memory_space=pltpu.SMEM)]
        + [vmem] * (len(pieces) + 2)
        + [pl.BlockSpec((rows, rows), lambda i: (0, 0))],
        out_specs=[vmem] * len(shapes),
        out_shape=[jax.ShapeDtypeStruct(shape, jnp.bfloat16) for shape in shapes],
        scratch_shapes=[pltpu.VMEM((rows, total), jnp.bfloat16)],
        compiler_params=pltpu.CompilerParams(vmem_limit_bytes=48 * 2**20),
        cost_estimate=pl.CostEstimate(
            flops=4 * rows * total * cols, bytes_accessed=6 * rows * total, transcendentals=0
        ),
    )(place, *pieces, right_rows, start, left_whole)


def attention_kernel(member_ref, whole_ref, left_ref, start_ref, right_ref, out_ref, square_ref):
    count = left_ref.shape[0]
    mine = pl.ds(pl.multiple_of(member_ref[0] * count, count), count)
    whole = whole_ref[...]
    rows = whole_ref[mine, :]
    out_ref[0] = lax.dot_general(
        rows, whole, (((1,), (1,)), ((), ())), preferred_element_type=jnp.float32
    ).astype(jnp.bfloat16)
    square_ref[...] = lax.dot_general(
        whole, whole, (((0,), (0,)), ((), ())), preferred_element_type=jnp.float32
    )
    out_ref[1] = square_ref[mine, :].astype(jnp.bfloat16)
    product = start_ref[...] + lax.dot_general(
        left_ref[...], whole, (((1,), (0,)), ((), ())), preferred_element_type=jnp.float32
    )
    out_ref[2] = lax.dot_general(
        product.astype(jnp.bfloat16),
        right_ref[...],
        (((1,), (0,)), ((), ())),
        preferred_element_type=jnp.float32,
    ).astype(jnp.bfloat16)
    out_ref[3] = rows


def attention_update(member, whole, left_rows, start, right_whole):
    count, width = left_rows.shape
    vmem = pl.BlockSpec(memory_space=pltpu.VMEM)
    return pl.pallas_call(
        attention_kernel,
        grid=(1,),
        in_specs=[pl.BlockSpec(memory_space=pltpu.SMEM)]
        + [vmem] * 3
        + [pl.BlockSpec((width, width), lambda i: (0, 2))],
        out_specs=vmem,
        out_shape=jax.ShapeDtypeStruct((4, count, width), jnp.bfloat16),
        scratch_shapes=[pltpu.VMEM((width, width), jnp.float32)],
        compiler_params=pltpu.CompilerParams(vmem_limit_bytes=32 * 2**20),
        cost_estimate=pl.CostEstimate(
            flops=2 * width**3, bytes_accessed=6 * width * width, transcendentals=0
        ),
    )(member, whole, left_rows, start, right_whole)


class Layout:
    def __init__(self, head_count, micro_rows):
        self.dp_size = lax.axis_size("dp")
        self.seq_size = lax.axis_size("seq")
        self.count = self.dp_size * self.seq_size
        self.dp = lax.axis_index("dp")
        self.seq = lax.axis_index("seq")
        self.micro = micro_rows
        self.parts = math.gcd(self.dp_size, head_count & -head_count)
        self.groups = self.dp_size // self.parts
        self.part = self.dp % self.parts
        self.head_groups = head_count & -head_count
        self.repeat = self.seq_size // (micro_rows * self.head_groups)
        self.unit = self.seq // self.repeat
        self.matrices = 4
        self.sides = self.seq_size // self.matrices
        self.matrix = self.seq % self.matrices
        self.side = self.seq // self.matrices
        self.member = self.dp * self.sides + self.side
        self.members = [
            [
                (group * self.parts + part) * self.seq_size + side * self.matrices + matrix
                for part in range(self.parts)
                for side in range(self.sides)
            ]
            for group in range(self.groups)
            for matrix in range(self.matrices)
        ]
        self.holders = [
            [
                dp * self.seq_size + side * self.matrices + matrix
                for dp in range(self.dp_size)
                for side in range(self.sides)
            ]
            for matrix in range(self.matrices)
        ]
        self.owners = [
            [side * self.matrices + matrix for matrix in range(self.matrices)]
            for side in range(self.sides)
        ]

    def flip(self, block, axis, bits):
        size = lax.axis_size(axis)
        return lax.ppermute(block, axis, [(i, i ^ bits) for i in range(size)])

    def gather_parts(self, block):
        pieces = {0: block}
        bit = self.parts // 2
        while bit:
            for key in list(pieces):
                pieces[key | bit] = self.flip(pieces[key], "dp", bit)
            bit //= 2
        whole = jnp.zeros((self.parts,) + block.shape, block.dtype)
        for key, piece in pieces.items():
            whole = lax.dynamic_update_index_in_dim(whole, piece, self.part ^ key, 0)
        return whole

    def scatter_step(self, blocks, axis, index, bit):
        pairs = blocks.reshape((blocks.shape[0] // 2, 2) + blocks.shape[1:])
        mine = (index // bit) % 2
        kept = lax.dynamic_index_in_dim(pairs, mine, 1, False)
        sent = lax.dynamic_index_in_dim(pairs, 1 - mine, 1, False)
        got = self.flip(low(sent), axis, bit)
        return low(kept.astype(jnp.float32) + got.astype(jnp.float32))

    def scatter(self, blocks, axis, index):
        bit = 1
        while blocks.shape[0] > 1:
            blocks = self.scatter_step(blocks, axis, index, bit)
            bit *= 2
        return blocks[0]

    def near_parts(self, block):
        pieces = {0: block}
        bit = self.parts // 2
        while bit:
            for key in list(pieces):
                pieces[key | bit] = self.flip(pieces[key], "dp", bit)
            bit //= 2
        return jnp.concatenate([pieces[key] for key in range(self.parts)], axis=0)

    def scatter_near(self, rows):
        blocks = rows.reshape((self.parts, -1) + rows.shape[1:])
        bit = 1
        while blocks.shape[0] > 1:
            pairs = blocks.reshape((blocks.shape[0] // 2, 2) + blocks.shape[1:])
            got = self.flip(low(pairs[:, 1]), "dp", bit)
            blocks = pairs[:, 0].astype(jnp.float32) + got.astype(jnp.float32)
            bit *= 2
        return blocks[0]

    def scatter_heads(self, blocks):
        index, bit = self.unit % self.head_groups, 1
        while blocks.shape[0] > 1:
            pairs = blocks.reshape((blocks.shape[0] // 2, 2) + blocks.shape[1:])
            mine = (index // bit) % 2
            kept = lax.dynamic_index_in_dim(pairs, mine, 1, False)
            sent = lax.dynamic_index_in_dim(pairs, 1 - mine, 1, False)
            got = self.flip(low(sent), "seq", bit * self.repeat)
            blocks = kept.astype(jnp.float32) + got.astype(jnp.float32)
            bit *= 2
        return blocks[0]

    def sum_groups(self, block):
        total = block
        for shift in range(1, self.groups):
            turn = [(i, (i + shift * self.parts) % self.dp_size) for i in range(self.dp_size)]
            total = total + lax.ppermute(low(block), "dp", turn).astype(jnp.float32)
        return total

    def to_units(self, blocks):
        shape = blocks.shape
        blocks = blocks[:, :, None]
        if self.repeat > 1:
            blocks = jnp.broadcast_to(blocks, shape[:2] + (self.repeat,) + shape[2:])
        return self.exchange(blocks.reshape((self.seq_size,) + shape[2:]))

    def exchange(self, blocks):
        return lax.all_to_all(blocks, "seq", 0, 0, tiled=True)

    def gather_step(self, pieces, bit, axis="seq"):
        grown = []
        for held in pieces:
            keys = sorted(held)
            moved = self.flip(jnp.stack([held[key] for key in keys]), axis, bit)
            held = dict(held)
            for place, key in enumerate(keys):
                held[key | bit] = moved[place]
            grown.append(held)
        return grown

    def gathered(self, held, index):
        whole = jnp.zeros((len(held),) + held[0].shape, held[0].dtype)
        for key, piece in held.items():
            whole = lax.dynamic_update_index_in_dim(whole, piece, index ^ key, 0)
        return whole

    def by_halves(self):
        return self.repeat == 1 and self.micro == 2 and self.head_groups == 4

    def rows_to_units(self, blocks, beside):
        held = [{0: item} for item in beside]
        bits = [1 << i for i in reversed(range(self.parts.bit_length() - 1))]
        if not self.by_halves():
            shape = blocks.shape
            blocks = jnp.broadcast_to(blocks[:, None], shape[:1] + (self.head_groups,) + shape[1:])
            whole = self.to_units(blocks)
            for bit in bits:
                held = self.gather_step(held, bit, "dp")
            return whole.reshape((-1,) + shape[2:]), held
        mine = self.unit // self.head_groups
        near = lax.dynamic_index_in_dim(blocks, mine, 0, False)
        far = self.flip(lax.dynamic_index_in_dim(blocks, 1 - mine, 0, False), "seq", 4)
        near_one = self.flip(near, "seq", 1)
        far, held = lax.optimization_barrier((far, held))
        far_two = self.flip(far, "seq", 2)
        for bit in bits[:1]:
            held = self.gather_step(held, bit, "dp")
        near_one, far_two = lax.optimization_barrier((near_one, far_two))
        near_two = self.flip(jnp.stack([near, near_one]), "seq", 2)
        far_one = self.flip(jnp.stack([far, far_two]), "seq", 1)
        near_two, far_one, held = lax.optimization_barrier((near_two, far_one, held))
        for bit in bits[1:]:
            held = self.gather_step(held, bit, "dp")
        pieces = [near, near_one, near_two[0], near_two[1], far, far_one[0], far_two, far_one[1]]
        whole = self.gathered(dict(enumerate(pieces)), self.seq)
        return whole.reshape((-1,) + blocks.shape[2:]), held

    def fold_units(self, row):
        blocks = row.reshape((self.seq_size, -1) + row.shape[1:])
        if not self.by_halves():
            return self.exchange(low(blocks))

        def pick(*keys):
            picked = [
                lax.dynamic_index_in_dim(blocks, self.seq ^ key, 0, False).astype(jnp.float32)
                for key in keys
            ]
            return jnp.stack(picked)

        near = pick(0, 1) + self.flip(low(pick(2, 3)), "seq", 2).astype(jnp.float32)
        far = pick(4, 6) + self.flip(low(pick(5, 7)), "seq", 1).astype(jnp.float32)
        return (near, far)

    def fold_halves(self, folded):
        if not self.by_halves():
            return folded
        near, far = folded
        near = near[0] + self.flip(low(near[1]), "seq", 1).astype(jnp.float32)
        far = far[0] + self.flip(low(far[1]), "seq", 2).astype(jnp.float32)
        return (near, far)

    def fold_rows(self, folded):
        if not self.by_halves():
            blocks = folded.astype(jnp.float32)
            return jnp.sum(blocks.reshape((self.micro, -1) + blocks.shape[1:]), axis=1)
        near, far = folded
        far = self.flip(low(far), "seq", 4).astype(jnp.float32)
        first = self.unit // self.head_groups == 0
        return jnp.stack([jnp.where(first, near, far), jnp.where(first, far, near)])

    def gather_members(self, block):
        whole = lax.all_gather(block, BOTH, axis=0, axis_index_groups=self.members)
        return whole.reshape((self.parts, self.sides) + block.shape)

    def spread_members(self, block):
        count = self.parts * self.sides
        blocks = jnp.broadcast_to(block[None], (count,) + block.shape)
        return lax.all_to_all(blocks, BOTH, 0, 0, tiled=True, axis_index_groups=self.members)

    def gather_holders(self, block):
        return lax.all_gather(block, BOTH, axis=0, axis_index_groups=self.holders, tiled=True)

    def exchange_holders(self, blocks):
        return lax.all_to_all(blocks, BOTH, 0, 0, tiled=True, axis_index_groups=self.holders)

    def exchange_owners(self, blocks):
        return lax.all_to_all(blocks, "seq", 0, 0, tiled=True, axis_index_groups=self.owners)


def after(value, token):
    return lax.optimization_barrier((value, token))[0]


def as_width(blocks, width):
    flat = blocks.reshape(blocks.shape[0], -1)
    short = -flat.shape[1] % width
    return jnp.pad(flat, ((0, 0), (0, short))).reshape(blocks.shape[0], -1, width)


def down_to_feed(blocks, width, lanes=256):
    lead, (rows, columns) = blocks.shape[:-2], blocks.shape[-2:]
    groups, parts = width // lanes, columns // lanes
    count = len(lead)
    blocks = blocks.reshape(lead + (groups, rows // groups, parts, lanes))
    order = tuple(range(count)) + (count + 2, count + 1, count, count + 3)
    return jnp.transpose(blocks, order).reshape(lead + (parts * rows // groups, width))


def feed_to_down(blocks, columns, lanes=256):
    lead, (rows, width) = blocks.shape[:-2], blocks.shape[-2:]
    groups, parts = width // lanes, columns // lanes
    count = len(lead)
    blocks = blocks.reshape(lead + (parts, rows // parts, groups, lanes))
    order = tuple(range(count)) + (count + 2, count + 1, count, count + 3)
    return jnp.transpose(blocks, order).reshape(lead + (groups * rows // parts, columns))


def of_width(blocks, rows, columns):
    flat = blocks.reshape(blocks.shape[0], -1)
    return flat[:, : rows * columns].reshape(blocks.shape[0], rows, columns)


def gather_all(block):
    return lax.all_gather(block, BOTH, axis=0, tiled=True)


def per_device(
    byte_rows,
    segments,
    counts,
    buckets,
    cotangent,
    vectors,
    vector_momenta,
    bias_table,
    table_momenta,
    attention_weights,
    attention_left,
    attention_right,
    attention_left_root,
    attention_right_root,
    attention_momenta,
    expand_weights,
    expand_left,
    expand_right,
    expand_left_root,
    expand_right_root,
    expand_momenta,
    shrink_weights,
    down_left_statistics,
    shrink_right,
    shrink_left_root,
    shrink_right_root,
    shrink_momenta,
):
    micro_rows, width_bytes, model_width = byte_rows.shape
    head_count = bias_table.shape[1]
    at = Layout(head_count, micro_rows)
    parts, part, seq_size, sequence_position = at.parts, at.part, at.seq_size, at.seq
    row_len = width_bytes * seq_size
    tok_local = width_bytes // 2
    tok_row = row_len // 2
    hidden_width = shrink_weights.shape[1 - 1] * at.count
    heads = head_count // parts
    head_width = model_width // parts
    hidden_part = hidden_width // parts

    row_span = model_width // at.count
    hidden_span = hidden_width // at.count
    dp_size, sides, matrices = at.dp_size, at.sides, at.matrices

    slot = -(-head_width // 128) * 128
    slot_fill = ((0, 0), (0, 0), (0, 0), (0, slot - head_width))
    split = low(attention_weights[:3]).reshape(3, row_span, at.head_groups, head_width)
    split = jnp.pad(jnp.transpose(split, (2, 1, 0, 3)), slot_fill).reshape(
        at.head_groups, row_span, 3 * slot
    )
    token_segs = segments[:, 0::2]
    digits = jnp.stack([token_segs // 64, token_segs % 64], axis=1).astype(jnp.bfloat16)
    digits = jnp.pad(digits, ((0, 0), (0, row_span - 2), (0, 0)))
    split = jnp.concatenate(
        [
            jnp.broadcast_to(split[None], (micro_rows,) + split.shape),
            jnp.broadcast_to(
                low(attention_weights[3]), (micro_rows, at.head_groups, row_span, model_width)
            ),
            jnp.broadcast_to(
                digits[:, None], (micro_rows, at.head_groups, row_span, tok_local)
            ),
        ],
        axis=3,
    )
    split = at.to_units(split)

    halo = 8
    count = at.seq_size
    forward = [(i, i + 1) for i in range(count - 1)]
    backward = [(i + 1, i) for i in range(count - 1)]
    wide_bytes = jnp.concatenate(
        [
            lax.ppermute(byte_rows[:, width_bytes - halo :], "seq", forward),
            byte_rows,
            lax.ppermute(byte_rows[:, :halo], "seq", backward),
        ],
        axis=1,
    )
    place = (sequence_position * width_bytes - halo).reshape(1)
    tokens, normed = make_tokens(counts, place, wide_bytes, vectors, row_len, halo)
    grad_rows_out = cotangent.reshape(-1, model_width)

    (
        expand_weights_in,
        shrink_weights_in,
        normed,
    ) = lax.optimization_barrier(
        (expand_weights, shrink_weights, normed)
    )
    def columns(whole, begin, width):
        return lax.dynamic_slice_in_dim(whole, begin, width, 1)

    if at.groups == 1:
        rest = low(expand_weights_in).reshape(2, row_span, parts, hidden_part)
        rest = jnp.transpose(rest, (2, 1, 0, 3)).reshape(parts, row_span, 2 * hidden_part)
        rest = lax.all_to_all(after(rest, split), "dp", 0, 0, tiled=True)
        bits = [1 << i for i in reversed(range(seq_size.bit_length() - 1))]
        rest = [{0: item} for item in (rest, low(shrink_weights_in))]
        rest = at.gather_step(rest, bits[0])
    else:
        rest = jnp.concatenate(
            [low(expand_weights_in[0]), low(expand_weights_in[1])]
            + [low(shrink_weights_in).reshape(row_span, hidden_width)],
            axis=1,
        )
        rest = gather_all(rest)
        weights_expand = jnp.concatenate(
            [
                columns(rest, i * hidden_width + part * hidden_part, hidden_part)
                for i in range(2)
            ],
            axis=1,
        )
        weights_shrink = lax.dynamic_slice(
            rest,
            (part * (model_width // parts), 2 * hidden_width),
            (model_width // parts, hidden_width),
        ).reshape(hidden_part, model_width)

    digits = split[:, :2, 3 * slot + model_width :].astype(jnp.int32)
    seg_row = (digits[:, 0] * 64 + digits[:, 1]).reshape(tok_row)
    split = split[:, :, : 3 * slot + model_width].reshape(
        seq_size * row_span, 3 * slot + model_width
    )
    def early_block(i):
        if i == 2:
            feed = [low(shrink_right_root), down_to_feed(low(shrink_momenta), hidden_width)]
        elif i < 2:
            feed = [low(expand_left_root[i]), low(expand_momenta[i])]
        else:
            feed = [jnp.zeros((row_span, hidden_width + model_width), jnp.bfloat16)]
        return jnp.concatenate(
            [feed[0][:, :model_width], low(attention_momenta[i]), low(attention_right_root[i])]
            + [feed[-1][:, -hidden_width:]],
            axis=1,
        )

    early = jnp.stack([early_block(i) for i in range(matrices)])
    early_width = early.shape[2]

    early = at.exchange_owners(after(early, split)).reshape(-1, early_width)
    factor_one = rms_factor(tokens)

    normed_row, held = at.rows_to_units(
        normed.reshape(micro_rows, tok_local, model_width), [split, grad_rows_out]
    )
    if at.groups == 1:
        weights_qkv = at.gathered(held[0], part)
    else:
        weights_qkv = lax.all_gather(split, "dp", axis=0)
    weights_qkv = weights_qkv.reshape(model_width, 3 * slot + model_width)
    weights_qkv, weights_out = weights_qkv[:, : 3 * slot], weights_qkv[:, 3 * slot :]
    weights_out = jnp.pad(
        weights_out.reshape(at.head_groups, head_width, model_width),
        ((0, 0), (0, slot - head_width), (0, 0)),
    ).reshape(-1, model_width)
    qkv_row = low(dot(normed_row, weights_qkv, 1, 0))
    qkv_row, early = lax.optimization_barrier((qkv_row, early))
    early = at.gather_holders(early)
    if at.groups == 1:
        rest, qkv_row = lax.optimization_barrier((rest, qkv_row))
        for bit in bits[1:-1]:
            rest = at.gather_step(rest, bit)
    onehot = (buckets[:, None] == jnp.arange(bias_table.shape[0], dtype=jnp.int32)[None, :]).astype(
        jnp.float32
    )
    head_begin = (at.unit % at.head_groups) * heads
    part_table = lax.dynamic_slice_in_dim(bias_table, head_begin, heads, 1)
    bias_rel = jnp.einsum("xb,bh->hx", onehot, part_table, precision=HIGH_PRECISION)
    bias_rel = jnp.pad(bias_rel, ((0, 0), (0, 1)))
    seg_col = seg_row[:, None]
    seg_line = seg_row[None, :]
    tile = 512
    while tile * heads * tok_row * 16 > 2**25 or tok_row % tile:
        tile //= 2
    attended_row, attended_f32, log_totals = attn_fwd(
        qkv_row, bias_rel, seg_col, seg_line, heads, head_width // heads, tile
    )
    if at.groups == 1:
        rest, attended_row = lax.optimization_barrier((rest, attended_row))
        rest = at.gather_step(rest, bits[-1])
    grad_pieces = after([held[1][key] for key in range(parts)], attended_row)
    grad_rows_all = jnp.concatenate(grad_pieces, axis=0)
    roots_in = after((expand_right_root, shrink_left_root, attention_left_root), normed_row)
    roots = jnp.stack(
        [low(roots_in[0][0]), low(roots_in[0][1]), low(roots_in[1])]
        + [jnp.zeros(shrink_left_root.shape, jnp.bfloat16)]
    )
    lefts = jnp.pad(
        low(roots_in[2]), ((0, 0), (0, 0), (0, hidden_width - model_width))
    )
    roots = at.exchange_owners(after(jnp.concatenate([roots, lefts], axis=1), attended_row))
    attended = at.exchange(attended_row.reshape(seq_size, tok_local, slot))
    attended = attended.reshape(
        micro_rows, at.head_groups, at.repeat, tok_local, slot
    )[:, :, 0]
    attended = jnp.transpose(attended, (0, 2, 1, 3)).reshape(micro_rows * tok_local, -1)
    resid = tokens + dot(attended, weights_out, 1, 0)
    factor_two = rms_factor(resid)
    normed_two = low(resid * factor_two * vectors[6])

    normed_two_all = at.near_parts(normed_two)
    if at.groups == 1:
        rest, normed_two_all = lax.optimization_barrier((rest, normed_two_all))
        weights_shrink = at.gathered(rest[1], at.seq).reshape(hidden_part, model_width)
        weights_expand = jnp.transpose(at.gathered(rest[0], at.seq), (1, 0, 2, 3)).reshape(model_width, -1)
    expanded = dot(normed_two_all, weights_expand, 1, 0)
    gate_pre = expanded[:, :hidden_part]
    upward = expanded[:, hidden_part:]
    activated, gelu_back = jax.vjp(functools.partial(jax.nn.gelu, approximate=True), gate_pre)
    hidden = low(activated * upward)
    grad_hidden = dot(grad_rows_all, weights_shrink, 1, 1)
    grad_gate_pre = low(gelu_back(grad_hidden * upward)[0])
    grad_upward = low(grad_hidden * activated)
    grad_normed_two = at.scatter_near(
        dot(grad_gate_pre, weights_expand[:, :hidden_part], 1, 1)
        + dot(grad_upward, weights_expand[:, hidden_part:], 1, 1)
    )
    grad_shrink_t = dot(grad_rows_all, hidden, 0, 0)
    grad_gate_w = dot(normed_two_all, grad_gate_pre, 0, 0)
    grad_up_w = dot(normed_two_all, grad_upward, 0, 0)

    feed_sum = [low(item) for item in (grad_gate_w, grad_up_w, grad_shrink_t)]
    feed_sum = jnp.stack(feed_sum + [jnp.zeros_like(feed_sum[0])])
    grad_normed_two = after(grad_normed_two, feed_sum)

    grad_resid_norm, grad_gain_two = norm_back(resid, factor_two, vectors[6], grad_normed_two)
    grad_resid = grad_rows_out.astype(jnp.float32) + grad_resid_norm
    grad_branch = low(grad_resid)
    grad_attended = low(dot(grad_branch, weights_out, 1, 1)).reshape(
        micro_rows, tok_local, at.head_groups, 1, slot
    )
    grad_attended = jnp.pad(
        jnp.transpose(grad_attended, (0, 2, 3, 1, 4)),
        ((0, 0), (0, 0), (0, at.repeat - 1), (0, 0), (0, 0)),
    )
    grad_attended, early, roots = lax.optimization_barrier((grad_attended, early, roots))
    grad_branch = after(grad_branch, grad_attended)
    grad_out = at.scatter(
        low(
            dot(attended, grad_branch, 0, 0)
            .reshape(at.head_groups, slot, model_width)[:, :head_width]
            .reshape(parts, -1, model_width)
        ),
        "dp",
        at.part,
    )
    grad_attended_row = at.exchange(
        grad_attended.reshape(seq_size, tok_local, slot)
    ).reshape(tok_row, slot)
    feed_sum = at.scatter_step(feed_sum, "seq", at.seq, 1)
    feed_sum, grad_attended_row = lax.optimization_barrier((feed_sum, grad_attended_row))
    feed_sum = at.scatter_step(feed_sum, "seq", at.seq, 2)

    grad_qkv_row, grad_bias = attn_bwd(
        qkv_row,
        grad_attended_row,
        attended_f32,
        log_totals,
        bias_rel,
        seg_col,
        seg_line,
        heads,
        tile,
    )
    grad_normed_part = low(dot(grad_qkv_row, weights_qkv, 1, 1))
    grad_normed_part = at.fold_units(grad_normed_part)
    feed_sum, grad_normed_part = lax.optimization_barrier((feed_sum, grad_normed_part))
    feed_sum = feed_sum.reshape(model_width, hidden_part)
    bit = matrices
    got = low(feed_sum)
    while bit < seq_size:
        got = at.flip(low(feed_sum), "seq", bit)
        bit *= 2
        if bit < seq_size:
            feed_sum = low(feed_sum.astype(jnp.float32) + got.astype(jnp.float32))
    grad_out = after(grad_out, grad_qkv_row)
    grad_out = jnp.transpose(
        grad_out.reshape(-1, at.head_groups, head_width), (1, 0, 2)
    )
    grad_out = at.scatter_heads(jnp.pad(grad_out, ((0, 0), (0, 0), (0, slot - head_width))))
    grad_normed_part, grad_qkv_row = lax.optimization_barrier((grad_normed_part, grad_qkv_row))
    grad_normed_part = at.fold_halves(grad_normed_part)
    grad_qkv = low(dot(normed_row, grad_qkv_row, 0, 0))
    grad_normed_part, grad_qkv, grad_out = lax.optimization_barrier(
        (grad_normed_part, grad_qkv, grad_out)
    )
    grad_normed = at.fold_rows(grad_normed_part).reshape(-1, model_width)

    side_rows = model_width // (parts * sides)
    sums = at.scatter(grad_qkv.reshape(parts, -1, 3 * slot), "dp", at.part)
    sums = low(jnp.concatenate([sums, grad_out], axis=1))
    sums = jnp.transpose(sums.reshape(sides, side_rows, matrices, slot), (0, 2, 1, 3))
    sums = sums.reshape(seq_size, side_rows, slot)

    roots = after(roots, grad_qkv_row)
    feed_right_rows = roots[:, :hidden_span].reshape(-1, hidden_width)
    attention_left_rows = roots[:, hidden_span:, :model_width].reshape(-1, model_width)
    early = after(early, grad_qkv)
    feed_left_whole = early[:, :model_width]
    attention_old = early[:, model_width : 2 * model_width]
    attention_right_whole = early[:, 2 * model_width : 3 * model_width]
    feed_old = early[:, 3 * model_width :]
    is_shrink = at.matrix == 2
    feed_start = MOMENTUM * jnp.where(
        is_shrink,
        dot(
            feed_to_down(
                feed_old.reshape(at.count, row_span, hidden_width), model_width
            ).reshape(hidden_width, model_width),
            feed_right_rows,
            0,
            1,
        ),
        dot(feed_old, feed_right_rows, 1, 1),
    )
    attention_start = MOMENTUM * dot(attention_left_rows, attention_old, 1, 0)
    part_grad = jnp.einsum("xb,hx->bh", onehot, grad_bias[:, :-1], precision=HIGH_PRECISION)
    grad_normed, feed_start, attention_start, got, part_grad, sums = lax.optimization_barrier(
        (grad_normed, feed_start, attention_start, got, part_grad, sums)
    )

    grad_tokens_norm, grad_gain_one = norm_back(tokens, factor_one, vectors[5], grad_normed)
    grad_tokens = (grad_resid + grad_tokens_norm).reshape(micro_rows, tok_local, model_width)
    if seq_size > matrices:
        feed_sum = low(feed_sum.astype(jnp.float32) + got.astype(jnp.float32))
    edge = halo // 2
    wide_grads = jnp.concatenate(
        [
            lax.ppermute(grad_tokens[:, tok_local - edge :], "seq", forward),
            grad_tokens,
            lax.ppermute(grad_tokens[:, :edge], "seq", backward),
        ],
        axis=1,
    )
    sums = at.exchange(after(sums, grad_tokens))
    input_grads, grad_taps = bytes_back(counts, place, wide_bytes, wide_grads, vectors, row_len, halo)
    feed_sum = {0: low(at.sum_groups(feed_sum.astype(jnp.float32)))}
    bit = parts // 2
    if bit:
        feed_sum[bit], grad_taps, sums = lax.optimization_barrier(
            (at.flip(feed_sum[0], "dp", bit), grad_taps, sums)
        )
        bit //= 2
    while bit:
        for key in list(feed_sum):
            feed_sum[key | bit] = at.flip(feed_sum[key], "dp", bit)
        bit //= 2
    sums = sums.reshape(
        micro_rows, at.head_groups, at.repeat, side_rows, slot
    )[..., :head_width]
    sums = jnp.sum(sums.astype(jnp.float32), axis=(0, 2))
    sums = at.sum_groups(jnp.transpose(sums, (1, 0, 2)).reshape(side_rows, model_width))
    full_attention = at.gather_members(low(sums)).reshape(model_width, model_width)
    grad_vectors = jnp.concatenate(
        [grad_taps[:5], grad_gain_one[None], grad_gain_two[None]], axis=0
    )
    grad_table = lax.dynamic_update_slice_in_dim(
        jnp.zeros_like(bias_table), part_grad, head_begin, 1
    )
    small = jnp.pad(grad_table.reshape(-1), (0, model_width - grad_table.size))
    small = low(jnp.concatenate([grad_vectors, small[None]], axis=0))

    member_rows = matrices * row_span
    member_cols = matrices * hidden_span
    def to_owners(strips):
        strips = strips.reshape(strips.shape[0], matrices, row_span, strips.shape[2])
        return jnp.transpose(strips, (1, 2, 0, 3)).reshape(matrices, row_span, hidden_width)

    def down_to_owners(rows):
        return down_to_feed(rows.reshape(matrices, hidden_span, model_width), hidden_width)

    whole_tiles = member_rows % 16 == 0 and member_cols % 128 == 0
    if whole_tiles:
        feed_right, feed_left, feed_step, feed_step_t, feed_cols, feed_rows = feed_update(
            jnp.stack([at.part, at.member]),
            [feed_sum[key] for key in range(parts)],
            feed_right_rows,
            feed_start,
            early,
            member_rows,
        )
    else:
        full_feed = at.gathered(feed_sum, at.part)
        feed_rows = lax.dynamic_slice_in_dim(full_feed, at.member * member_rows, member_rows, 1)
        begin = at.member * member_cols
        feed_cols = lax.dynamic_slice(
            full_feed, (begin // hidden_part, 0, begin % hidden_part), (1, model_width, member_cols)
        )[0].T
        feed_product = low(
            feed_start
            + sum(
                dot(full_feed[i], columns(feed_right_rows, i * hidden_part, hidden_part), 1, 1)
                for i in range(parts)
            )
        )
        feed_step = low(dot(feed_left_whole, feed_product, 1, 0))
        feed_right = jnp.concatenate(
            [low(dot(feed_cols, full_feed[i], 1, 0)) for i in range(parts)], axis=1
        )
        feed_left = low(sum(dot(feed_rows[i], full_feed[i], 1, 1) for i in range(parts)))
        feed_step_t = feed_step.T
        feed_rows = jnp.transpose(feed_rows, (1, 0, 2)).reshape(member_rows, hidden_width)
    shrink_out = low(dot(after(hidden, feed_step), weights_shrink, 1, 0))
    shrink_out = at.scatter_near(shrink_out)
    layer_output = low(resid + shrink_out).reshape(micro_rows, tok_local, model_width)

    moved = feed_step.reshape(-1, member_rows, member_cols)
    members = moved.shape[0]
    moved = at.exchange_holders(
        jnp.concatenate(
            [
                moved,
                jnp.broadcast_to(
                    small.reshape(1, -1, member_cols),
                    (members, small.size // member_cols, member_cols),
                ),
            ],
            axis=1,
        )
    )
    small = jnp.sum(moved[:, member_rows:].astype(jnp.float32), axis=0).reshape(small.shape)
    moved = moved[:, :member_rows]

    feed_sums = at.exchange_owners(
        jnp.concatenate(
            [
                feed_right.reshape(matrices, hidden_span, hidden_width),
                as_width(feed_left.reshape(matrices, row_span, model_width), hidden_width),
            ],
            axis=1,
        )
    )
    if whole_tiles:
        attention_parts = attention_update(
            at.member.reshape(1),
            after(full_attention, moved),
            attention_left_rows,
            attention_start,
            early,
        )
    else:
        rows = lax.dynamic_slice_in_dim(full_attention, at.member * member_rows, member_rows, 0)
        cols = columns(full_attention, at.member * member_rows, member_rows)
        attention_product = low(attention_start + dot(attention_left_rows, full_attention, 1, 0))
        attention_parts = [
            low(dot(rows, full_attention, 1, 1)),
            low(dot(cols, full_attention, 0, 0)),
            low(dot(attention_product, attention_right_whole, 1, 0)),
            rows,
        ]
    attention_out = jnp.concatenate(
        [item.reshape(matrices, row_span, model_width) for item in attention_parts], axis=1
    )
    left_rows = -(-row_span * model_width // hidden_width)
    is_down = at.matrix == 2
    feed_pair = jnp.concatenate(
        [
            jnp.where(is_down, down_to_owners(feed_step_t), to_owners(moved)),
            jnp.where(
                is_down,
                down_to_owners(feed_cols),
                feed_rows.reshape(matrices, row_span, hidden_width),
            ),
            as_width(jnp.broadcast_to(low(small), (matrices,) + small.shape), hidden_width),
            as_width(attention_out, hidden_width),
        ],
        axis=1,
    )
    feed_pair = at.exchange_owners(after(feed_pair, feed_sums))
    small_rows = -(-small.size // hidden_width)
    attention_out = of_width(
        feed_pair[:, 2 * row_span + small_rows :], 4 * row_span, model_width
    )
    small = of_width(
        feed_pair[:, 2 * row_span : 2 * row_span + small_rows], small.shape[0], small.shape[1]
    )
    small = jnp.sum(small.astype(jnp.float32), axis=0)
    sum_vectors = small[:-1]
    sum_table = small[-1, : grad_table.size].reshape(grad_table.shape)
    total_tokens = micro_rows * at.dp_size * tok_row
    small_rate = SMALL_RATE / math.sqrt(total_tokens)
    vector_momenta_new = MOMENTUM * vector_momenta + sum_vectors
    vectors_new = vectors - small_rate * vector_momenta_new
    table_momenta_new = MOMENTUM * table_momenta + sum_table
    table_new = bias_table - small_rate * table_momenta_new

    sum_left, sum_right, step, grads = [
        attention_out[:, i * row_span : (i + 1) * row_span].astype(jnp.float32) for i in range(4)
    ]

    def statistics(old, increment):
        return STAT_DECAY * old + (1.0 - STAT_DECAY) * increment

    attention_new = attention_weights - MATRIX_RATE * step
    attention_left_new = statistics(attention_left, sum_left)
    attention_right_new = statistics(attention_right, sum_right)
    attention_mom_new = MOMENTUM * attention_momenta + grads

    def wide(block):
        return block.astype(jnp.float32)

    step, grads = feed_pair[:, :row_span], feed_pair[:, row_span : 2 * row_span]
    sum_left = of_width(feed_sums[:, hidden_span : hidden_span + left_rows], row_span, model_width)
    expand_new = expand_weights - MATRIX_RATE * wide(step[:2])
    expand_left_new = statistics(expand_left, wide(sum_left[:2]))
    expand_right_new = statistics(expand_right, wide(feed_sums[:2, :hidden_span]))
    expand_mom_new = MOMENTUM * expand_momenta + wide(grads[:2])
    shrink_new = shrink_weights - MATRIX_RATE * wide(feed_to_down(step[2], model_width))
    shrink_left_new = statistics(down_left_statistics, wide(feed_sums[2, :hidden_span]))
    shrink_right_new = statistics(shrink_right, wide(sum_left[2]))
    shrink_mom_new = MOMENTUM * shrink_momenta + wide(feed_to_down(grads[2], model_width))
    return (
        layer_output,
        input_grads,
        vectors_new,
        vector_momenta_new,
        table_new,
        table_momenta_new,
        attention_new,
        attention_left_new,
        attention_right_new,
        attention_mom_new,
        low(attention_new),
        expand_new,
        expand_left_new,
        expand_right_new,
        expand_mom_new,
        low(expand_new),
        shrink_new,
        shrink_left_new,
        shrink_right_new,
        shrink_mom_new,
        low(shrink_new),
    )


def solution(mesh):
    row = P("dp", "seq", None)
    stack = P(None, BOTH, None)
    flat = P(BOTH, None)
    return jax.shard_map(
        per_device,
        mesh=mesh,
        in_specs=(row, P("dp", "seq"), P("dp"), P(), row)
        + (P(),) * 4
        + (stack,) * 12
        + (flat,) * 6,
        out_specs=(row, row) + (P(),) * 4 + (stack,) * 10 + (flat,) * 5,
        check_vma=False,
    )
```
